512 devices in a mesh: axial: 32 (over x, z), girth: 16 (over y, core).
Axes of the slice: x: 4, y: 8, z: 8, core: 2. Of those that a mesh axis runs over, the one named last changes fastest.
Arguments:
- field: float32 [4, 16, 512, 2048], P(None, None, 'axial', 'girth'), may hold values from -6 to 6
- geometry: float32 [3, 16, 512, 2048], P(None, None, 'axial', 'girth'), may hold values from 5e-05 to 0.0003
- mass: float32 [16, 512, 2048], P(None, 'axial', 'girth'), may hold values from 0.4 to 2
- cycle_id: int32 [2048], P('axial'), may hold values from -1 to 511, as said below
- cycle_radial: int32 [2048], P('axial'), may hold values from 0 to 1
- cycle_axial: int32 [2048], P('axial'), may hold values from 0 to 1
- cycle_weights: float32 [2, 8, 2048], P(None, None, 'axial'), as said below
- az_elem: int32 [2048], P('girth'), may hold values from 0 to 15
- az_weights: float32 [8, 2048], P(None, 'girth'), as said below
Outputs:
- field_out: float32 [4, 16, 512, 2048], P(None, None, 'axial', 'girth')
- spectrum: float32 [2, 512, 4, 2048], P(None, 'axial', None, 'girth')
The draws below stay inside these ranges and needn't reach their ends.
Inputs may be any that keep to these rules, and one draw needn't show every extreme that they name: `cycle_id`: every cycle 0 to 511 is named by exactly one slot; empty slots hold -1. The 64 slots of one index of axial hold at most 64 cycles, and one index of axial holds exactly 64. `cycle_weights`: the values of the 8 Lagrange polynomials of the Gauss-Lobatto-Legendre nodes at a point of [-1, 1], for the radial and for the axial direction of each slot. `az_weights`: the values of the 8 Lagrange polynomials of the Gauss-Lobatto-Legendre nodes at a point of [-1, 1] for each azimuth probe.
All inputs are finite; a program needn't handle non-finite values.
Results may differ from the reference program's by a relative error of at most 0.0003.
Values sent between devices are 32-bit elements; how exact they have to be, the bound alone decides.
No kernel may reach another device: no remote copies, remote signals or barrier semaphores. Data moves between devices by JAX's collectives and lax.ppermute only.
A program may use at most 64 MiB of HBM per device.

```python
import math
import jax
import jax.numpy as jnp
from jax import lax

C = 4
P_SIZE = 8
ITERS = 4
ER = 2
EA_DEV = 2
EG_DEV = 16
PA = 2048
NR = 16
NA = 512
NG = 2048
ROWS = 512
CYCLE_CAP = 64
CYCLE_SLOTS = 2048
N_AXIAL = 32
N_GIRTH = 16


LOBATTO = (-1.0, -0.8717401485096066, -0.5917001814331423, -0.2092992179024789, 0.2092992179024789, 0.5917001814331423, 0.8717401485096066, 1.0)


def lagrange_values(points):
    weight_rows = []
    for first_index in range(P_SIZE):
        product = jnp.ones_like(points)
        for other_index in range(P_SIZE):
            if other_index != first_index:
                product = product * (points - LOBATTO[other_index]) / (LOBATTO[first_index] - LOBATTO[other_index])
        weight_rows.append(product)
    return jnp.stack(weight_rows)


def draw_cycle_weights(key, part):
    key = jax.random.fold_in(key, 5)
    key_size, key_sign = jax.random.split(key)
    points = jax.random.uniform(key_size, (2, CYCLE_SLOTS), jnp.float32, -1.0, 1.0)
    return jnp.transpose(lagrange_values(points), (1, 0, 2)).astype(jnp.float32)


def draw_az_weights(key, part):
    key = jax.random.fold_in(key, 9)
    key_size, key_sign = jax.random.split(key)
    points = jax.random.uniform(key_size, (PA,), jnp.float32, -1.0, 1.0)
    return lagrange_values(points).astype(jnp.float32)


def draw_cycle_id(key, part):
    key_busy, key_shuffle = jax.random.split(jax.random.fold_in(key, 17))
    busiest = jax.random.randint(key_busy, (), 0, N_AXIAL).astype(jnp.int32)
    shuffled = jax.random.permutation(key_shuffle, ROWS).astype(jnp.int32)
    rank_list = jnp.arange(ROWS, dtype=jnp.int32)
    spread = (rank_list - CYCLE_CAP) % (N_AXIAL - 1)
    others = spread + (spread >= busiest).astype(jnp.int32)
    owner_by_rank = jnp.where(rank_list < CYCLE_CAP, busiest, others)
    owner_axis = jnp.zeros((ROWS,), jnp.int32).at[shuffled].set(owner_by_rank)
    sort_keys = owner_axis * ROWS + rank_list
    sorted_cycles = jnp.argsort(sort_keys).astype(jnp.int32)
    sorted_owner = owner_axis[sorted_cycles]
    counts = jnp.sum((owner_axis[:, None] == jnp.arange(N_AXIAL, dtype=jnp.int32)[None, :]).astype(jnp.int32), axis=0)
    starts = jnp.cumsum(counts) - counts
    within = rank_list - starts[sorted_owner]
    empty_slots = jnp.full((CYCLE_SLOTS,), -1, jnp.int32)
    return empty_slots.at[sorted_owner * CYCLE_CAP + within].set(sorted_cycles)


def with_ends(drawn, own_key, least, top_value):
    dims = drawn.shape
    place = [jax.random.randint(jax.random.fold_in(own_key, axis), (), 0, dims[axis]) for axis in range(len(dims))]
    drawn = drawn.at[tuple(place)].set(least)
    longest = dims.index(max(dims))
    place[longest] = (place[longest] + 1) % dims[longest]
    return drawn.at[tuple(place)].set(top_value)


def block_scale(rng, dims, cuts, low, top_value):
    level = 1.0
    for dim, shards_of in cuts:
        draws = jax.random.uniform(jax.random.fold_in(jax.random.fold_in(rng, 6), dim), (shards_of,), jnp.float32, low / len(cuts), top_value / len(cuts))
        level = level * jnp.repeat(jnp.exp(draws), dims[dim] // shards_of).reshape((-1,) + (1,) * (len(dims) - 1 - dim))
    return level


def centred(own_key, shape, deviation, reach, cuts=(), kind=jnp.bfloat16):
    level = block_scale(own_key, shape, cuts, -0.22, 0.18) if cuts else 1.0
    drawn = jax.random.normal(own_key, shape, jnp.float32) * deviation * level
    return jnp.minimum(jnp.maximum(drawn, -reach), reach).astype(kind)


def setup_inputs(seed: int = 0) -> dict:
    key_of = jax.random.split(jax.random.key(seed), 10)
    field = centred(key_of[0], (C, NR, NA, NG), 1.0, 6.0, ((2, 32), (3, 16)), jnp.float32)
    geometry = jnp.clip(jnp.exp(math.log(0.0003) - 1.7917595 * jax.random.uniform(key_of[1], (3, NR, NA, NG), jnp.float32) ** block_scale(key_of[1], (3, NR, NA, NG), ((2, 32), (3, 16)), -0.2, 0.2)), 4.999999873689376e-05, 0.0003)
    mass = jnp.clip(jnp.exp(math.log(2.0) - 1.609438 * jax.random.uniform(key_of[2], (NR, NA, NG), jnp.float32) ** block_scale(key_of[2], (NR, NA, NG), ((1, 32), (2, 16)), -0.2, 0.2)), 0.4, 2.0)
    cycle_id = draw_cycle_id(jax.random.fold_in(key_of[9], 71), 0)
    cycle_radial = with_ends(jax.random.randint(key_of[4], (CYCLE_SLOTS,), 0, ER), jax.random.fold_in(key_of[4], 1), 0, ER - 1).astype(jnp.int32)
    cycle_axial = with_ends(jax.random.randint(key_of[5], (CYCLE_SLOTS,), 0, EA_DEV), jax.random.fold_in(key_of[5], 1), 0, EA_DEV - 1).astype(jnp.int32)
    cycle_weights = draw_cycle_weights(jax.random.fold_in(key_of[9], 71), 0)
    az_elem = with_ends(jax.random.randint(key_of[7], (PA,), 0, EG_DEV), jax.random.fold_in(key_of[7], 1), 0, EG_DEV - 1).astype(jnp.int32)
    az_weights = draw_az_weights(jax.random.fold_in(key_of[9], 71), 0)
    return {"field": field, "geometry": geometry, "mass": mass, "cycle_id": cycle_id, "cycle_radial": cycle_radial, "cycle_axial": cycle_axial, "cycle_weights": cycle_weights, "az_elem": az_elem, "az_weights": az_weights}


LOBATTO = (-1.0, -0.8717401485096066, -0.5917001814331423, -0.2092992179024789,
           0.2092992179024789, 0.5917001814331423, 0.8717401485096066, 1.0)
HIGHEST = lax.Precision.HIGHEST


def derivative_table():
    node_count = len(LOBATTO)
    barycentric = []
    for row_index in range(node_count):
        product = 1.0
        for col_index in range(node_count):
            if col_index != row_index:
                product = product * (LOBATTO[row_index] - LOBATTO[col_index])
        barycentric.append(1.0 / product)
    table_rows = []
    for row_index in range(node_count):
        entries = []
        for col_index in range(node_count):
            if col_index != row_index:
                entries.append(barycentric[col_index] / barycentric[row_index] / (LOBATTO[row_index] - LOBATTO[col_index]))
            else:
                entries.append(0.0)
        entries[row_index] = -sum(entries)
        table_rows.append(entries)
    return table_rows


def apply_matrix(values, matrix, dimension):
    extent = values.shape
    split_shape = extent[:dimension] + (extent[dimension] // P_SIZE, P_SIZE) + extent[dimension + 1:]
    blocks = values.reshape(split_shape)
    rotated = jnp.tensordot(blocks, matrix, axes=[[dimension + 1], [1]], precision=HIGHEST)
    return jnp.moveaxis(rotated, -1, dimension + 1).reshape(extent)


def add_shared(core, padded, dimension):
    length = core.shape[dimension]
    lower = lax.slice_in_dim(padded, 0, length, axis=dimension)
    upper = lax.slice_in_dim(padded, 2, length + 2, axis=dimension)
    broadcast_shape = [1] * core.ndim
    broadcast_shape[dimension] = length
    position = (jnp.arange(length, dtype=jnp.int32) % P_SIZE).reshape(broadcast_shape)
    nothing = jnp.zeros((), core.dtype)
    partner = jnp.where(position == 0, lower, jnp.where(position == P_SIZE - 1, upper, nothing))
    return core + partner


def pad_one(values, dimension, closed):
    widths = [(0, 0)] * values.ndim
    widths[dimension] = (1, 1)
    return jnp.pad(values, widths, mode="wrap" if closed else "constant")


def shared_sum(values):
    for dimension, closed in ((1, False), (2, False), (3, True)):
        values = add_shared(values, pad_one(values, dimension, closed), dimension)
    return values


def reference(field, geometry, mass, cycle_id, cycle_radial, cycle_axial, cycle_weights, az_elem, az_weights):
    matrix = jnp.asarray(derivative_table(), jnp.float32)

    def stiffness(component):
        total = jnp.zeros_like(component)
        for dimension in range(3):
            slope = apply_matrix(component, matrix, dimension)
            total = total + apply_matrix(geometry[dimension] * slope, matrix.T, dimension)
        return total

    def shared_one(component):
        return shared_sum(component[None])[0]

    assembled = shared_one(mass)
    current = field
    for step_index in range(ITERS):
        action = lax.map(stiffness, current)
        summed = lax.map(shared_one, action)
        current = current - summed / assembled

    pa_dev = PA // N_GIRTH
    slot_device = jnp.arange(CYCLE_SLOTS, dtype=jnp.int32) // CYCLE_CAP
    axial_elem = (slot_device * EA_DEV + cycle_axial).astype(jnp.int32)
    girth_elem = (jnp.arange(PA, dtype=jnp.int32) // pa_dev) * EG_DEV + az_elem
    girth_nodes = girth_elem[None, :] * P_SIZE + jnp.arange(P_SIZE, dtype=jnp.int32)[:, None]
    anchor = jnp.zeros((), jnp.int32)

    def one_slot(inputs):
        radial_index, axial_index, weights = inputs
        starts = (anchor, (radial_index * P_SIZE).astype(jnp.int32), (axial_index * P_SIZE).astype(jnp.int32), anchor)
        slab = lax.dynamic_slice(current, starts, (C, P_SIZE, P_SIZE, current.shape[3]))
        cycle_line = jnp.einsum("crag,r,a->cg", slab, weights[0], weights[1], precision=HIGHEST)
        picked = cycle_line[:, girth_nodes]
        return jnp.sum(picked * az_weights[None], axis=1)

    values = lax.map(one_slot, (cycle_radial, axial_elem, jnp.moveaxis(cycle_weights, 2, 0)))
    target = jnp.where(cycle_id >= 0, cycle_id, ROWS).astype(jnp.int32)
    probe_rows = jnp.zeros((ROWS + 1, C, PA), jnp.float32).at[target].add(values)[:ROWS]
    transform = jnp.fft.fft(probe_rows, axis=2, norm="ortho")
    spectrum = jnp.stack([jnp.real(transform), jnp.imag(transform)]).astype(jnp.float32)
    return current, spectrum
```

```python
import math

import jax
import jax.numpy as jnp
import ml_dtypes
import numpy as np
from jax import lax
from jax.experimental import pallas as pl
from jax.experimental.pallas import tpu as pltpu
from jax.sharding import PartitionSpec as P

C = 4
P_SIZE = 8
LANES = 128
HALO = 32
NODES = 256
WIDE = 6 * LANES
ROWS_DEV = 16
F32 = jnp.float32
BF16 = jnp.bfloat16

LOBATTO = (
    -1.0,
    -0.8717401485096066,
    -0.5917001814331423,
    -0.2092992179024789,
    0.2092992179024789,
    0.5917001814331423,
    0.8717401485096066,
    1.0,
)


def derivative_table():
    node_count = len(LOBATTO)
    barycentric = []
    for row_index in range(node_count):
        product = 1.0
        for col_index in range(node_count):
            if col_index != row_index:
                product = product * (LOBATTO[row_index] - LOBATTO[col_index])
        barycentric.append(1.0 / product)
    table_rows = []
    for row_index in range(node_count):
        entries = []
        for col_index in range(node_count):
            if col_index != row_index:
                entries.append(
                    barycentric[col_index]
                    / barycentric[row_index]
                    / (LOBATTO[row_index] - LOBATTO[col_index])
                )
            else:
                entries.append(0.0)
        entries[row_index] = -sum(entries)
        table_rows.append(entries)
    return np.asarray(table_rows, np.float32)


def np_split(table):
    table = np.asarray(table, np.float32)
    high = table.astype(ml_dtypes.bfloat16)
    low = (table - high.astype(np.float32)).astype(ml_dtypes.bfloat16)
    return high, low


def left_operand(table):
    high, low = np_split(table)
    return np.concatenate([high, high, low], axis=1)


def right_operand(table):
    high, low = np_split(table)
    return np.concatenate([high, high, low], axis=0)


def stiffness_tables():
    d = derivative_table()
    eye = lambda n: np.eye(n, dtype=np.float32)
    radial = np.kron(np.kron(eye(2), d), eye(16))
    axial = np.kron(eye(32), d)
    slope = np.concatenate([radial, axial], axis=0)
    return (
        left_operand(slope),
        left_operand(slope.T),
        right_operand(axial.T),
        right_operand(axial),
    )


def dft_tables():
    a = np.arange(2048)[:, None]
    m = np.arange(LANES)[None, :]
    angle = 2.0 * np.pi * ((a * m) % 2048) / 2048.0
    table = np.concatenate([np.cos(angle), np.sin(angle)], axis=1)
    high, low = np_split(table)
    k = np.arange(16)[:, None]
    lane = np.arange(LANES)[None, :]
    turn = 2.0 * np.pi * ((k * lane) % 16) / 16.0
    phase = np.stack([np.cos(turn), -np.sin(turn)], axis=1) / math.sqrt(2048.0)
    return high, low, phase.astype(np.float32)


def split(x):
    high = x.astype(BF16)
    return high, (x - high.astype(F32)).astype(BF16)


def dot(a, b):
    return jnp.dot(a, b, preferred_element_type=F32)


def left_mul(table, x):
    high, low = split(x)
    return dot(table, jnp.concatenate([high, low, high], axis=0))


def right_mul(x, table):
    high, low = split(x)
    return dot(jnp.concatenate([high, low, high], axis=1), table)


def stiff(u, gr, ga, gg, tables):
    slope_l, slope_t, girth, girth_t = tables
    ra = left_mul(slope_l[...], u)
    g = right_mul(u, girth[...])
    y = jnp.concatenate([ra[:NODES] * gr, ra[NODES:] * ga], axis=0)
    return left_mul(slope_t[...], y) + right_mul(g * gg, girth_t[...])


def twice(x):
    return jnp.concatenate([x, x], axis=1)


def sum_nodes(t):
    width = t.shape[1]
    v = t.reshape(16, 16, width)
    mid = v[7:8] + v[8:9]
    v = jnp.concatenate([v[:7], mid, mid, v[9:]], axis=0)
    pair = v[:, 7:8, :] + v[:, 8:9, :]
    node = lax.broadcasted_iota(jnp.int32, v.shape, 1)
    return jnp.where((node == 7) | (node == 8), pair, v)


def sum_girth(own, left, right, owners):
    lane = lax.broadcasted_iota(jnp.int32, left.shape, 1)
    first = lane % P_SIZE == 0
    last = lane % P_SIZE == P_SIZE - 1

    def inner(x):
        return jnp.where(
            first, pltpu.roll(x, 1, 1), jnp.where(last, pltpu.roll(x, LANES - 1, 1), 0.0)
        )

    sums = []
    for c, x in enumerate(own):
        p = inner(x)
        p = jnp.where(lane == 0, pltpu.roll(left, (LANES - HALO * c - HALO + 1) % LANES, 1), p)
        p = jnp.where(lane == LANES - 1, pltpu.roll(right, (LANES - 1 - HALO * c) % LANES, 1), p)
        sums.append(x + p)
    p = inner(left)
    q = inner(right)
    for c, x in enumerate(owners):
        p = jnp.where(lane == HALO * c + HALO - 1, pltpu.roll(x, HALO * c + HALO - 1, 1), p)
        q = jnp.where(lane == HALO * c, pltpu.roll(x, (HALO * c + 1) % LANES, 1), q)
    return sums + [left + p, right + q]


def shared_local(parts):
    return jnp.concatenate(sum_girth(parts[:4], parts[4], parts[5], parts[:4]), axis=1)


def lanes_of(x, k):
    return x[:, k * LANES : (k + 1) * LANES]


def pack_kernel(field, geom, mass, to_right, to_left):
    lane = lax.broadcasted_iota(jnp.int32, (NODES, LANES), 1)

    def pack(arrays, start):
        out = None
        for k, x in enumerate(arrays):
            moved = pltpu.roll(x, (HALO * k - start) % LANES, 1) if (HALO * k - start) else x
            out = moved if out is None else jnp.where(lane // HALO == k, moved, out)
        return out

    fields = [field[c] for c in range(C)]
    others = [geom[k] for k in range(3)] + [mass[...]]
    to_right[0] = pack(fields, LANES - HALO)
    to_right[1] = pack(others, LANES - HALO)
    to_left[0] = pack(fields, 0)
    to_left[1] = pack(others, 0)


def own_kernel(field, geom, *refs):
    tables, out = refs[:4], refs[4]
    gr, ga, gg = [twice(geom[k]) for k in range(3)]
    for pair in range(2):
        u = jnp.concatenate([field[2 * pair], field[2 * pair + 1]], axis=1)
        out[:, 2 * pair * LANES : (2 * pair + 2) * LANES] = stiff(u, gr, ga, gg, tables)


def faces(total, low, high, offset):
    width = total.shape[2]
    low[:, offset : offset + width] = total[:, 0, :]
    high[:, offset : offset + width] = total[:, 15, :]


def halo_kernel(left, right, own_total, mass, *refs):
    tables = refs[:4]
    halo_geom, total_out, mass_out, low, high = refs[4:]
    lane = lax.broadcasted_iota(jnp.int32, (NODES, LANES), 1)

    def spread(x, k):
        y = jnp.where(lane // HALO == k, x, 0.0)
        y = y + pltpu.roll(y, HALO, 1)
        return y + pltpu.roll(y, 2 * HALO, 1)

    left_others, right_others = left[1], right[1]
    geoms = []
    for k in range(3):
        g = jnp.concatenate([spread(left_others, k), spread(right_others, k)], axis=1)
        halo_geom[k] = g
        geoms.append(g)
    u = jnp.concatenate([left[0], right[0]], axis=1)
    t = stiff(u, *geoms, tables)
    parts = [own_total[:, c * LANES : (c + 1) * LANES] for c in range(C)]
    total = sum_nodes(shared_local(parts + [lanes_of(t, 0), lanes_of(t, 1)]))
    total_out[...] = total.reshape(NODES, WIDE)
    faces(total, low, high, 0)
    m = mass[...]
    masses = sum_girth([m], spread(left_others, 3), spread(right_others, 3), [m] * C)
    lumped = sum_nodes(jnp.concatenate(masses, axis=1))
    mass_out[...] = lumped.reshape(NODES, 3 * LANES)
    faces(lumped, low, high, WIDE)


def received(low, high):
    shape = (16, 16, low.shape[1])
    node = lax.broadcasted_iota(jnp.int32, shape, 1)
    both = jnp.where(
        node == 0, low[:, None, :], jnp.where(node == 15, high[:, None, :], 0.0)
    )
    return both.reshape(NODES, low.shape[1])


def wide(x):
    own = lanes_of(x, 0)
    return jnp.concatenate([own] * C + [x[:, LANES:]], axis=1)


def advance(u, inverse, geom, halo_geom, tables, out, low, high):
    gr, ga, gg = [twice(geom[k]) for k in range(3)]
    parts = []
    for tile in range(3):
        if tile == 2:
            gr, ga, gg = [halo_geom[k] for k in range(3)]
        t = stiff(u[:, 2 * tile * LANES : (2 * tile + 2) * LANES], gr, ga, gg, tables)
        parts += [lanes_of(t, 0), lanes_of(t, 1)]
    total = sum_nodes(shared_local(parts))
    faces(total, low, high, 0)
    out[...] = u - total.reshape(NODES, WIDE) * wide(inverse)


def first_kernel(field, left, right, total, lumped, got_low, got_high, geom, halo_geom, *refs):
    tables = refs[:4]
    out, inverse_out, low, high = refs[4:]
    arrived = received(got_low[...], got_high[...])
    inverse = 1.0 / (lumped[...] + arrived[:, WIDE:])
    inverse_out[...] = inverse
    u = jnp.concatenate([field[c] for c in range(C)] + [left[0], right[0]], axis=1)
    u = u - (total[...] + arrived[:, :WIDE]) * wide(inverse)
    advance(u, inverse, geom, halo_geom, tables, out, low, high)


def step_kernel(state, inverse_ref, got_low, got_high, geom, halo_geom, *refs):
    tables = refs[:4]
    out, low, high = refs[4:]
    inverse = inverse_ref[...]
    u = state[...] - received(got_low[...], got_high[...]) * wide(inverse)
    advance(u, inverse, geom, halo_geom, tables, out, low, high)


def last_kernel(state, inverse_ref, got_low, got_high, slab, girth_weight, select, out, dense):
    own = C * LANES
    inverse = jnp.concatenate([inverse_ref[:, :LANES]] * C, axis=1)
    u = state[:, :own] - received(got_low[:, :own], got_high[:, :own]) * inverse
    for c in range(C):
        out[c] = lanes_of(u, c)
    slab_high, slab_low = split(slab[...])
    values = left_mul(jnp.concatenate([slab_high, slab_high, slab_low], axis=1), u)
    stacked = jnp.concatenate([lanes_of(values, c) for c in range(C)], axis=0)
    weight_high, weight_low = split(girth_weight[...])
    weights = jnp.concatenate([weight_high, weight_high, weight_low], axis=0)
    probes = right_mul(stacked, weights)
    slots = slab.shape[0]
    spread = jnp.concatenate([probes[c * slots : (c + 1) * slots] for c in range(C)], axis=1)
    high, low = split(spread)
    chosen = select[...].astype(BF16)
    rows = dot(jnp.concatenate([chosen, chosen], axis=1), jnp.concatenate([high, low], axis=0))
    for c in range(C):
        dense[:, c * ROWS_DEV : (c + 1) * ROWS_DEV, :] = lanes_of(rows, c).reshape(
            -1, ROWS_DEV, LANES
        )


def dft_kernel(rows, phase, table_high, table_low, out):
    turn_re = phase[0:1, :]
    turn_im = phase[1:2, :]
    total = None
    for pair in range(8):
        x = jnp.concatenate([rows[2 * pair], rows[2 * pair + 1]], axis=1)
        z = jnp.concatenate([x * twice(turn_re), x * twice(turn_im)], axis=0)
        high, low = split(z)
        block = pl.ds(pair * 256, 256)
        th, tl = table_high[block, :], table_low[block, :]
        part = dot(high, th) + dot(low, th) + dot(high, tl)
        total = part if total is None else total + part
    n = C * ROWS_DEV
    re = total[:n, :LANES] + total[n:, LANES:]
    im = total[n:, :LANES] - total[:n, LANES:]
    for c in range(C):
        out[0, :, c, :] = re[c * ROWS_DEV : (c + 1) * ROWS_DEV]
        out[1, :, c, :] = im[c * ROWS_DEV : (c + 1) * ROWS_DEV]


def call(kernel, shapes, flops, *args):
    vmem = pl.BlockSpec(memory_space=pltpu.VMEM)
    out_shape = [jax.ShapeDtypeStruct(s, F32) for s in shapes]
    return pl.pallas_call(
        kernel,
        out_shape=out_shape,
        in_specs=[vmem] * len(args),
        out_specs=[vmem] * len(shapes),
        compiler_params=pltpu.CompilerParams(vmem_limit_bytes=40 * 1024 * 1024),
        cost_estimate=pl.CostEstimate(flops=flops, bytes_accessed=2000000, transcendentals=0),
    )(*args)


def body(
    field, geometry, mass, cycle_id, cycle_radial, cycle_axial, cycle_weights, az_elem, az_weights
):
    axial_count, girth_count = lax.axis_size("axial"), lax.axis_size("girth")
    up = [(i, i + 1) for i in range(axial_count - 1)]
    down = [(j, i) for i, j in up]
    around = [(i, (i + 1) % girth_count) for i in range(girth_count)]
    back = [(j, i) for i, j in around]
    tables = [jnp.asarray(t) for t in stiffness_tables()]
    field = field.reshape(C, NODES, LANES)
    geom = geometry.reshape(3, NODES, LANES)
    mass = mass.reshape(NODES, LANES)
    tile_flops = 18 * 2 * 256**3

    to_right, to_left = call(pack_kernel, [(2, NODES, LANES)] * 2, 1000000, field, geom, mass)
    left = lax.ppermute(to_right, "girth", around)
    right = lax.ppermute(to_left, "girth", back)
    (own_total,) = call(own_kernel, [(NODES, C * LANES)], 2 * tile_flops, field, geom, *tables)

    def exchange(low, high):
        return lax.ppermute(high, "axial", up), lax.ppermute(low, "axial", down)

    face_wide = (16, WIDE + 3 * LANES)
    halo_geom, total, lumped, low, high = call(
        halo_kernel,
        [(3, NODES, 2 * LANES), (NODES, WIDE), (NODES, 3 * LANES), face_wide, face_wide],
        tile_flops,
        left,
        right,
        own_total,
        mass,
        *tables,
    )
    got_low, got_high = exchange(low, high)
    face = (16, WIDE)
    state, inverse, low, high = call(
        first_kernel,
        [(NODES, WIDE), (NODES, 3 * LANES), face, face],
        3 * tile_flops,
        field,
        left,
        right,
        total,
        lumped,
        got_low,
        got_high,
        geom,
        halo_geom,
        *tables,
    )
    for _ in range(2):
        got_low, got_high = exchange(low, high)
        state, low, high = call(
            step_kernel,
            [(NODES, WIDE), face, face],
            3 * tile_flops,
            state,
            inverse,
            got_low,
            got_high,
            geom,
            halo_geom,
            *tables,
        )
    got_low, got_high = exchange(low, high)

    slot_count = cycle_id.shape[0]
    node = jnp.arange(NODES, dtype=jnp.int32)
    radial_node, axial_node = node // 16, node % 16
    radial_weight = jnp.where(
        radial_node[None, :] // P_SIZE == cycle_radial[:, None],
        jnp.tile(jnp.repeat(cycle_weights[0].T, 16, axis=1), (1, 2)),
        0.0,
    )
    axial_weight = jnp.where(
        axial_node[None, :] // P_SIZE == cycle_axial[:, None],
        jnp.tile(cycle_weights[1].T, (1, NODES // P_SIZE)),
        0.0,
    )
    slab = radial_weight * axial_weight
    girth_node = jnp.arange(LANES, dtype=jnp.int32)
    girth_weight = jnp.where(
        girth_node[:, None] // P_SIZE == az_elem[None, :],
        jnp.tile(az_weights, (LANES // P_SIZE, 1)),
        0.0,
    )
    wanted = jnp.arange(ROWS_DEV * axial_count, dtype=jnp.int32)
    select = (wanted[:, None] == cycle_id[None, :]).astype(F32)

    final, dense = call(
        last_kernel,
        [(C, NODES, LANES), (axial_count, C * ROWS_DEV, LANES)],
        tile_flops,
        state,
        inverse,
        got_low,
        got_high,
        slab,
        girth_weight,
        select,
    )
    pieces = lax.all_to_all(dense, "axial", 0, 0)
    rows = lax.all_gather(jnp.sum(pieces, axis=0), "girth")
    table_high, table_low, phases = dft_tables()
    phase = lax.dynamic_index_in_dim(
        jnp.asarray(phases), lax.axis_index("girth"), 0, keepdims=False
    )
    (spectrum,) = call(
        dft_kernel,
        [(2, ROWS_DEV, C, LANES)],
        tile_flops,
        rows,
        phase,
        jnp.asarray(table_high),
        jnp.asarray(table_low),
    )
    return final.reshape(C, 16, 16, LANES), spectrum


def solution(mesh):
    return jax.shard_map(
        body,
        mesh=mesh,
        in_specs=(
            P(None, None, "axial", "girth"),
            P(None, None, "axial", "girth"),
            P(None, "axial", "girth"),
            P("axial"),
            P("axial"),
            P("axial"),
            P(None, None, "axial"),
            P("girth"),
            P(None, "girth"),
        ),
        out_specs=(P(None, None, "axial", "girth"), P(None, "axial", None, "girth")),
        check_vma=False,
    )
```

```python
import math

import jax
import jax.numpy as jnp
import ml_dtypes
import numpy as np
from jax import lax
from jax.experimental import pallas as pl
from jax.experimental.pallas import tpu as pltpu
from jax.sharding import PartitionSpec as P

C = 4
P_SIZE = 8
LANES = 128
HALO = 32
NODES = 256
WIDE = 6 * LANES
ROWS_DEV = 16
SLOTS = 8
F32 = jnp.float32
BF16 = jnp.bfloat16

LOBATTO = (
    -1.0,
    -0.8717401485096066,
    -0.5917001814331423,
    -0.2092992179024789,
    0.2092992179024789,
    0.5917001814331423,
    0.8717401485096066,
    1.0,
)


def derivative_table():
    node_count = len(LOBATTO)
    barycentric = []
    for row_index in range(node_count):
        product = 1.0
        for col_index in range(node_count):
            if col_index != row_index:
                product = product * (LOBATTO[row_index] - LOBATTO[col_index])
        barycentric.append(1.0 / product)
    table_rows = []
    for row_index in range(node_count):
        entries = []
        for col_index in range(node_count):
            if col_index != row_index:
                entries.append(
                    barycentric[col_index]
                    / barycentric[row_index]
                    / (LOBATTO[row_index] - LOBATTO[col_index])
                )
            else:
                entries.append(0.0)
        entries[row_index] = -sum(entries)
        table_rows.append(entries)
    return np.asarray(table_rows, np.float32)


def np_split(table):
    table = np.asarray(table, np.float32)
    high = table.astype(ml_dtypes.bfloat16)
    low = (table - high.astype(np.float32)).astype(ml_dtypes.bfloat16)
    return high, low


def left_operand(table):
    high, low = np_split(table)
    return np.concatenate([high, high, low], axis=1)


def right_operand(table):
    high, low = np_split(table)
    return np.concatenate([high, high, low], axis=0)


def stiffness_tables():
    d = derivative_table()
    eye = lambda n: np.eye(n, dtype=np.float32)
    radial = np.kron(np.kron(eye(2), d), eye(16))
    axial = np.kron(eye(32), d)
    slope = np.concatenate([radial, axial], axis=0)
    ends = np.tile(np.concatenate([d[:, 0], d[:, 7]]), 16)[:, None]
    return (
        left_operand(slope),
        left_operand(slope.T),
        right_operand(axial.T),
        right_operand(axial),
        left_operand(axial.T),
        left_operand(np.kron(eye(4), d)),
        left_operand(np.kron(eye(8), d.T)),
        np.ascontiguousarray(np.broadcast_to(ends, (NODES, LANES))),
    )


def dft_tables():
    a = np.arange(2048)[:, None]
    m = np.arange(LANES)[None, :]
    angle = 2.0 * np.pi * ((a * m) % 2048) / 2048.0
    table = np.concatenate([np.cos(angle), np.sin(angle)], axis=1)
    high, low = np_split(table)
    k = np.arange(16)[:, None]
    lane = np.arange(LANES)[None, :]
    turn = 2.0 * np.pi * ((k * lane) % 16) / 16.0
    phase = np.stack([np.cos(turn), -np.sin(turn)], axis=1) / math.sqrt(2048.0)
    return high, low, phase.astype(np.float32)


def split(x):
    high = x.astype(BF16)
    return high, (x - high.astype(F32)).astype(BF16)


def dot(a, b):
    return jnp.dot(a, b, preferred_element_type=F32)


def left_mul(table, x):
    high, low = split(x)
    return dot(table, jnp.concatenate([high, low, high], axis=0))


def right_mul(x, table):
    high, low = split(x)
    return dot(jnp.concatenate([high, low, high], axis=1), table)


def stiff(u, gr, ga, gg, tables):
    slope_l, slope_t, girth, girth_t = tables[:4]
    ra = left_mul(slope_l[...], u)
    g = right_mul(u, girth[...])
    y = jnp.concatenate([ra[:NODES] * gr, ra[NODES:] * ga], axis=0)
    return left_mul(slope_t[...], y) + right_mul(g * gg, girth_t[...])


def twice(x):
    return jnp.concatenate([x, x], axis=1)


def sum_nodes(t):
    width = t.shape[1]
    v = t.reshape(16, 16, width)
    mid = v[7:8] + v[8:9]
    v = jnp.concatenate([v[:7], mid, mid, v[9:]], axis=0)
    pair = v[:, 7:8, :] + v[:, 8:9, :]
    node = lax.broadcasted_iota(jnp.int32, v.shape, 1)
    return jnp.where((node == 7) | (node == 8), pair, v)


def sum_girth(own, left, right, owners):
    lane = lax.broadcasted_iota(jnp.int32, left.shape, 1)
    first = lane % P_SIZE == 0
    last = lane % P_SIZE == P_SIZE - 1

    def inner(x):
        return jnp.where(
            first, pltpu.roll(x, 1, 1), jnp.where(last, pltpu.roll(x, LANES - 1, 1), 0.0)
        )

    sums = []
    for c, x in enumerate(own):
        p = inner(x)
        p = jnp.where(lane == 0, pltpu.roll(left, (LANES - HALO * c - HALO + 1) % LANES, 1), p)
        p = jnp.where(lane == LANES - 1, pltpu.roll(right, (LANES - 1 - HALO * c) % LANES, 1), p)
        sums.append(x + p)
    p = inner(left)
    q = inner(right)
    for c, x in enumerate(owners):
        p = jnp.where(lane == HALO * c + HALO - 1, pltpu.roll(x, HALO * c + HALO - 1, 1), p)
        q = jnp.where(lane == HALO * c, pltpu.roll(x, (HALO * c + 1) % LANES, 1), q)
    return sums + [left + p, right + q]


def shared_local(parts):
    return jnp.concatenate(sum_girth(parts[:4], parts[4], parts[5], parts[:4]), axis=1)


def lanes_of(x, k):
    return x[:, k * LANES : (k + 1) * LANES]


def load_kernel(count, *refs):
    sources, targets = refs[:count], refs[count : 2 * count]
    to_right, to_left, sems = refs[2 * count :]
    copies = []
    for k in range(count):
        copy = pltpu.make_async_copy(sources[k], targets[k], sems.at[k])
        copy.start()
        copies.append(copy)
    for copy in copies[:3]:
        copy.wait()
    field, geom, mass = targets[:3]
    lane = lax.broadcasted_iota(jnp.int32, (NODES, LANES), 1)

    def pack(arrays, start):
        out = None
        for k, x in enumerate(arrays):
            moved = pltpu.roll(x, (HALO * k - start) % LANES, 1) if (HALO * k - start) else x
            out = moved if out is None else jnp.where(lane // HALO == k, moved, out)
        return out

    fields = [field[c] for c in range(C)]
    others = [geom[k] for k in range(3)] + [mass[...]]
    to_right[0] = pack(fields, LANES - HALO)
    to_right[1] = pack(others, LANES - HALO)
    to_left[0] = pack(fields, 0)
    to_left[1] = pack(others, 0)
    for copy in copies[3:]:
        copy.wait()


def own_kernel(field, geom, *refs):
    tables, out = refs[:-1], refs[-1]
    gr, ga, gg = [twice(geom[k]) for k in range(3)]
    for pair in range(2):
        u = jnp.concatenate([field[2 * pair], field[2 * pair + 1]], axis=1)
        out[:, 2 * pair * LANES : (2 * pair + 2) * LANES] = stiff(u, gr, ga, gg, tables)


def at_faces(low, high, width):
    shape = (16, 16, width)
    node = lax.broadcasted_iota(jnp.int32, shape, 1)
    both = jnp.where(
        node == 0, low[:, None, :], jnp.where(node == 15, high[:, None, :], 0.0)
    )
    return both.reshape(NODES, width)


def wide(x):
    own = lanes_of(x, 0)
    return jnp.concatenate([own] * C + [x[:, LANES:]], axis=1)


def put_faces(x, low, high, offset):
    width = x.shape[1]
    v = x.reshape(16, 16, width)
    low[:, offset : offset + width] = v[:, 0, :]
    high[:, offset : offset + width] = v[:, 15, :]


def action(u, geom, halo_geom, tables):
    gr, ga, gg = [twice(geom[k]) for k in range(3)]
    parts = []
    for tile in range(3):
        if tile == 2:
            gr, ga, gg = [halo_geom[k] for k in range(3)]
        t = stiff(u[:, 2 * tile * LANES : (2 * tile + 2) * LANES], gr, ga, gg, tables)
        parts += [lanes_of(t, 0), lanes_of(t, 1)]
    return sum_nodes(shared_local(parts)).reshape(NODES, WIDE)


def inner_update(u, total, inverse):
    row = lax.broadcasted_iota(jnp.int32, u.shape, 0) % 16
    return jnp.where((row == 0) | (row == 15), u, u - total * wide(inverse))


def two_steps(u, geom, halo_geom, inverse, first, tables, state, second, low, high):
    v = inner_update(u, first, inverse)
    state[...] = v
    total = action(v, geom, halo_geom, tables)
    second[...] = total
    put_faces(first, low, high, 0)
    put_faces(total, low, high, WIDE)


STATIC = 2 * WIDE
NARROW = 3 * LANES


def halo_kernel(left, right, own_total, field, mass, geom, *refs):
    tables = refs[:8]
    halo_geom, state, second, mass_out, ends_out, low, high = refs[8:]
    lane = lax.broadcasted_iota(jnp.int32, (NODES, LANES), 1)

    def spread(x, k):
        y = jnp.where(lane // HALO == k, x, 0.0)
        y = y + pltpu.roll(y, HALO, 1)
        return y + pltpu.roll(y, 2 * HALO, 1)

    left_others, right_others = left[1], right[1]
    geoms = []
    for k in range(3):
        g = jnp.concatenate([spread(left_others, k), spread(right_others, k)], axis=1)
        halo_geom[k] = g
        geoms.append(g)
    u = jnp.concatenate([left[0], right[0]], axis=1)
    t = stiff(u, *geoms, tables)
    parts = [own_total[:, c * LANES : (c + 1) * LANES] for c in range(C)]
    first = sum_nodes(shared_local(parts + [lanes_of(t, 0), lanes_of(t, 1)]))
    first = first.reshape(NODES, WIDE)
    m = mass[...]
    masses = sum_girth([m], spread(left_others, 3), spread(right_others, 3), [m] * C)
    lumped = sum_nodes(jnp.concatenate(masses, axis=1)).reshape(NODES, NARROW)
    mass_out[...] = lumped
    whole = [jnp.concatenate([geom[k], geoms[k]], axis=1) for k in range(3)]
    end = tables[7][...]
    ends = left_mul(tables[4][...], whole[1] * jnp.concatenate([end] * 3, axis=1))
    ends_out[...] = ends
    for k, x in enumerate([lumped, whole[0], whole[2], ends]):
        put_faces(x, low, high, STATIC + k * NARROW)
    start = jnp.concatenate([field[c] for c in range(C)] + [u], axis=1)
    two_steps(start, geom, halo_geom, 1.0 / lumped, first, tables, state, second, low, high)


def static_part(ref, k):
    return ref[:, STATIC + k * NARROW : STATIC + (k + 1) * NARROW]


def finish_pair(state, second, inverse, ends, statics, own, got, tables):
    low, high, got_low, got_high = statics
    own_low, own_high = own
    new_low, new_high = got
    w_low = -(own_low[:, :WIDE] + new_low[:, :WIDE]) * wide(
        1.0 / (static_part(low, 0) + static_part(got_low, 0))
    )
    w_high = -(own_high[:, :WIDE] + new_high[:, :WIDE]) * wide(
        1.0 / (static_part(high, 0) + static_part(got_high, 0))
    )
    w = jnp.concatenate([w_low, w_high], axis=0)
    radial, girthwise = [
        wide(jnp.concatenate([static_part(ref, k) for ref in statics], axis=0)) for k in (1, 2)
    ]
    slope = left_mul(tables[5][...], w)
    face = left_mul(tables[6][...], jnp.concatenate([slope, slope], axis=0) * radial)
    pieces = []
    for tile in range(3):
        span = slice(2 * tile * LANES, (2 * tile + 2) * LANES)
        g = right_mul(w[:, span], tables[2][...])
        y = jnp.concatenate([g, g], axis=0) * girthwise[:, span]
        pieces.append(right_mul(y, tables[3][...]))
    face = face + jnp.concatenate(pieces, axis=1)
    other = jnp.concatenate([static_part(got_low, 3), static_part(got_high, 3)], axis=0)
    beyond = face[32:] + wide(other) * w
    beyond = shared_local([lanes_of(beyond, k) for k in range(6)]).reshape(2, 16, WIDE)
    pair = beyond[:, 7:8, :] + beyond[:, 8:9, :]
    node = lax.broadcasted_iota(jnp.int32, beyond.shape, 1)
    beyond = jnp.where((node == 7) | (node == 8), pair, beyond)
    beyond_low = beyond[0] + new_low[:, WIDE : 2 * WIDE]
    beyond_high = beyond[1] + new_high[:, WIDE : 2 * WIDE]
    node = lax.broadcasted_iota(jnp.int32, (16, 16, WIDE), 1)
    along = jnp.where(node < P_SIZE, w_low[:, None, :], w_high[:, None, :])
    change = wide(ends) * along.reshape(NODES, WIDE) + at_faces(face[:16], face[16:32], WIDE)
    change = sum_nodes(shared_local([lanes_of(change, k) for k in range(6)]))
    total = second + change.reshape(NODES, WIDE) + at_faces(beyond_low, beyond_high, WIDE)
    return state + at_faces(w_low, w_high, WIDE) - total * wide(inverse)


def middle_kernel(state, second, lumped, ends, low, high, got_low, got_high, geom, halo_geom, *refs):
    tables = refs[:8]
    state_out, second_out, inverse_out, next_low, next_high = refs[8:]
    inverse = 1.0 / (
        lumped[...] + at_faces(static_part(got_low, 0), static_part(got_high, 0), NARROW)
    )
    inverse_out[...] = inverse
    statics = (low, high, got_low, got_high)
    u = finish_pair(
        state[...], second[...], inverse, ends[...], statics, (low, high), (got_low, got_high), tables
    )
    first = action(u, geom, halo_geom, tables)
    two_steps(u, geom, halo_geom, inverse, first, tables, state_out, second_out, next_low, next_high)


def last_kernel(
    state,
    second,
    inverse,
    ends,
    low,
    high,
    got_low,
    got_high,
    own_low,
    own_high,
    new_low,
    new_high,
    slab,
    girth_weight,
    select,
    header,
    *refs,
):
    tables = refs[:8]
    out, packed, probes_out = refs[8:]
    u = finish_pair(
        state[...],
        second[...],
        inverse[...],
        ends[...],
        (low, high, got_low, got_high),
        (own_low, own_high),
        (new_low, new_high),
        tables,
    )
    u = u[:, : C * LANES]
    for c in range(C):
        out[c] = lanes_of(u, c)
    slab_high, slab_low = split(slab[...])
    values = left_mul(jnp.concatenate([slab_high, slab_high, slab_low], axis=1), u)
    stacked = jnp.concatenate([lanes_of(values, c) for c in range(C)], axis=0)
    weight_high, weight_low = split(girth_weight[...])
    weights = jnp.concatenate([weight_high, weight_high, weight_low], axis=0)
    probes = right_mul(stacked, weights)
    slots = slab.shape[0]
    spread = jnp.concatenate([probes[c * slots : (c + 1) * slots] for c in range(C)], axis=1)
    probes_out[...] = spread
    high_part, low_part = split(spread)
    chosen = select[...].astype(BF16)
    rows = dot(
        jnp.concatenate([chosen, chosen], axis=1),
        jnp.concatenate([high_part, low_part], axis=0),
    )
    for c in range(C):
        block = lanes_of(rows, c).reshape(-1, SLOTS, LANES)
        if c == 0:
            place = lax.broadcasted_iota(jnp.int32, block.shape, 1)
            block = jnp.where(place == SLOTS - 1, header[...][:, None, :], block)
        packed[:, c * SLOTS : (c + 1) * SLOTS, :] = block


def unpack_kernel(pieces, out):
    sources = pieces.shape[0]
    heads = pieces[:, 0:SLOTS, :]
    head = jnp.broadcast_to(heads[:, SLOTS - 1 : SLOTS, :], heads.shape)
    place = lax.broadcasted_iota(jnp.int32, heads.shape, 1)
    lane = lax.broadcasted_iota(jnp.int32, heads.shape, 2)
    mine = jnp.where((lane == place) & (place < SLOTS - 1), head, 0.0)
    row = jnp.sum(mine.reshape(sources * SLOTS, LANES), axis=1, keepdims=True)
    column = lax.broadcasted_iota(jnp.int32, (sources * SLOTS, LANES), 1).astype(F32)
    chosen = jnp.transpose(jnp.where(row == column + 1.0, 1.0, 0.0))[:ROWS_DEV].astype(BF16)
    both = jnp.concatenate([chosen, chosen], axis=1)
    for c in range(C):
        x = pieces[:, c * SLOTS : (c + 1) * SLOTS, :].reshape(sources * SLOTS, LANES)
        high, low = split(x)
        out[c * ROWS_DEV : (c + 1) * ROWS_DEV, :] = dot(
            both, jnp.concatenate([high, low], axis=0)
        )


def dft_kernel(rows, phase, table_high, table_low, out):
    turn_re = phase[0:1, :]
    turn_im = phase[1:2, :]
    total = None
    for pair in range(8):
        x = jnp.concatenate([rows[2 * pair], rows[2 * pair + 1]], axis=1)
        z = jnp.concatenate([x * twice(turn_re), x * twice(turn_im)], axis=0)
        high, low = split(z)
        block = pl.ds(pair * 256, 256)
        th, tl = table_high[block, :], table_low[block, :]
        part = dot(high, th) + dot(low, th) + dot(high, tl)
        total = part if total is None else total + part
    n = C * ROWS_DEV
    re = total[:n, :LANES] + total[n:, LANES:]
    im = total[n:, :LANES] - total[:n, LANES:]
    for c in range(C):
        out[0, :, c, :] = re[c * ROWS_DEV : (c + 1) * ROWS_DEV]
        out[1, :, c, :] = im[c * ROWS_DEV : (c + 1) * ROWS_DEV]


def call(kernel, shapes, flops, *args):
    vmem = pl.BlockSpec(memory_space=pltpu.VMEM)
    out_shape = [jax.ShapeDtypeStruct(s, F32) for s in shapes]
    return pl.pallas_call(
        kernel,
        out_shape=out_shape,
        in_specs=[vmem] * len(args),
        out_specs=[vmem] * len(shapes),
        compiler_params=pltpu.CompilerParams(vmem_limit_bytes=40 * 1024 * 1024),
        cost_estimate=pl.CostEstimate(flops=flops, bytes_accessed=2000000, transcendentals=0),
    )(*args)


def load(*args):
    halo = jax.ShapeDtypeStruct((2, NODES, LANES), F32)
    outs = [jax.ShapeDtypeStruct(x.shape, x.dtype) for x in args] + [halo] * 2
    got = pl.pallas_call(
        lambda *refs: load_kernel(len(args), *refs),
        out_shape=outs,
        in_specs=[pl.BlockSpec(memory_space=pltpu.HBM)] * len(args),
        out_specs=[pl.BlockSpec(memory_space=pltpu.VMEM)] * len(outs),
        scratch_shapes=[pltpu.SemaphoreType.DMA((len(args),))],
        compiler_params=pltpu.CompilerParams(vmem_limit_bytes=40 * 1024 * 1024),
    )(*args)
    return got[: len(args)], got[len(args)], got[len(args) + 1]


def body(
    field, geometry, mass, cycle_id, cycle_radial, cycle_axial, cycle_weights, az_elem, az_weights
):
    axial_count, girth_count = lax.axis_size("axial"), lax.axis_size("girth")
    up = [(i, i + 1) for i in range(axial_count - 1)]
    down = [(j, i) for i, j in up]
    around = [(i, (i + 1) % girth_count) for i in range(girth_count)]
    back = [(j, i) for i, j in around]
    loaded, to_right, to_left = load(
        field.reshape(C, NODES, LANES),
        geometry.reshape(3, NODES, LANES),
        mass.reshape(NODES, LANES),
        *[jnp.asarray(t) for t in stiffness_tables()],
    )
    field, geom, mass = loaded[:3]
    tables = loaded[3:]
    tile_flops = 18 * 2 * 256**3

    left = lax.ppermute(to_right, "girth", around)
    right = lax.ppermute(to_left, "girth", back)
    (own_total,) = call(own_kernel, [(NODES, C * LANES)], 2 * tile_flops, field, geom, *tables[:4])

    def exchange(low, high):
        return lax.ppermute(high, "axial", up), lax.ppermute(low, "axial", down)

    whole, narrow = (NODES, WIDE), (NODES, NARROW)
    face_static = (16, STATIC + 4 * NARROW)
    halo_geom, state, second, lumped, ends, low, high = call(
        halo_kernel,
        [(3, NODES, 2 * LANES), whole, whole, narrow, narrow, face_static, face_static],
        4 * tile_flops,
        left,
        right,
        own_total,
        field,
        mass,
        geom,
        *tables,
    )
    got_low, got_high = exchange(low, high)
    state, second, inverse, own_low, own_high = call(
        middle_kernel,
        [whole, whole, narrow, (16, STATIC), (16, STATIC)],
        6 * tile_flops,
        state,
        second,
        lumped,
        ends,
        low,
        high,
        got_low,
        got_high,
        geom,
        halo_geom,
        *tables,
    )
    new_low, new_high = exchange(own_low, own_high)

    slot_count = cycle_id.shape[0]
    node = jnp.arange(NODES, dtype=jnp.int32)
    radial_node, axial_node = node // 16, node % 16
    radial_weight = jnp.where(
        radial_node[None, :] // P_SIZE == cycle_radial[:, None],
        jnp.tile(jnp.repeat(cycle_weights[0].T, 16, axis=1), (1, 2)),
        0.0,
    )
    axial_weight = jnp.where(
        axial_node[None, :] // P_SIZE == cycle_axial[:, None],
        jnp.tile(cycle_weights[1].T, (1, NODES // P_SIZE)),
        0.0,
    )
    slab = radial_weight * axial_weight
    girth_node = jnp.arange(LANES, dtype=jnp.int32)
    girth_weight = jnp.where(
        girth_node[:, None] // P_SIZE == az_elem[None, :],
        jnp.tile(az_weights, (LANES // P_SIZE, 1)),
        0.0,
    )
    target = jnp.where(cycle_id >= 0, cycle_id // ROWS_DEV, -1)
    order = jnp.arange(slot_count, dtype=jnp.int32)
    earlier = (target[:, None] == target[None, :]) & (order[None, :] < order[:, None])
    rank = jnp.sum(earlier.astype(jnp.int32), axis=1)
    fits = (cycle_id >= 0) & (rank < SLOTS - 1)
    position = jnp.where(fits, target * SLOTS + rank, -1)
    wanted = jnp.arange(SLOTS * axial_count, dtype=jnp.int32)
    select = (wanted[:, None] == position[None, :]).astype(F32)
    number = jnp.sum(select * (cycle_id % ROWS_DEV + 1).astype(F32)[None, :], axis=1)
    overflow = jnp.any((cycle_id >= 0) & (rank >= SLOTS - 1)).astype(F32)
    header = jnp.concatenate(
        [
            number.reshape(axial_count, SLOTS),
            jnp.broadcast_to(overflow, (axial_count, LANES - SLOTS)),
        ],
        axis=1,
    )

    final, packed, probes = call(
        last_kernel,
        [(C, NODES, LANES), (axial_count, C * SLOTS, LANES), (slot_count, C * LANES)],
        tile_flops,
        state,
        second,
        inverse,
        ends,
        low,
        high,
        got_low,
        got_high,
        own_low,
        own_high,
        new_low,
        new_high,
        slab,
        girth_weight,
        select,
        header,
        *tables,
    )
    pieces = lax.all_to_all(packed, "axial", 0, 0)

    def compact(pieces, probes, cycle_id):
        return call(unpack_kernel, [(C * ROWS_DEV, LANES)], tile_flops, pieces)[0]

    def dense(pieces, probes, cycle_id):
        wanted = jnp.arange(ROWS_DEV * axial_count, dtype=jnp.int32)
        chosen = (wanted[:, None] == cycle_id[None, :]).astype(F32)
        rows = jnp.dot(chosen, probes, precision=lax.Precision.HIGHEST)
        rows = rows.reshape(axial_count, ROWS_DEV, C * LANES)
        rows = jnp.sum(lax.all_to_all(rows, "axial", 0, 0), axis=0)
        return rows.reshape(ROWS_DEV, C, LANES).swapaxes(0, 1).reshape(C * ROWS_DEV, LANES)

    crowded = jnp.max(pieces[:, SLOTS - 1, SLOTS]) > 0.5
    rows = lax.cond(crowded, dense, compact, pieces, probes, cycle_id)
    rows = lax.all_gather(rows, "girth")
    table_high, table_low, phases = dft_tables()
    phase = lax.dynamic_index_in_dim(
        jnp.asarray(phases), lax.axis_index("girth"), 0, keepdims=False
    )
    (spectrum,) = call(
        dft_kernel,
        [(2, ROWS_DEV, C, LANES)],
        tile_flops,
        rows,
        phase,
        jnp.asarray(table_high),
        jnp.asarray(table_low),
    )
    return final.reshape(C, 16, 16, LANES), spectrum


def solution(mesh):
    return jax.shard_map(
        body,
        mesh=mesh,
        in_specs=(
            P(None, None, "axial", "girth"),
            P(None, None, "axial", "girth"),
            P(None, "axial", "girth"),
            P("axial"),
            P("axial"),
            P("axial"),
            P(None, None, "axial"),
            P("girth"),
            P(None, "girth"),
        ),
        out_specs=(P(None, None, "axial", "girth"), P(None, "axial", None, "girth")),
        check_vma=False,
    )
```

```python
import math

import jax
import jax.numpy as jnp
import ml_dtypes
import numpy as np
from jax import lax
from jax.experimental import pallas as pl
from jax.experimental.pallas import tpu as pltpu
from jax.sharding import PartitionSpec as P

C = 4
P_SIZE = 8
LANES = 128
HALO = 32
NODES = 256
WIDE = 6 * LANES
ROWS_DEV = 16
SLOTS = 8
VMEM_LIMIT = 32 * 1024 * 1024
LOAD_LIMIT = 60000000
F32 = jnp.float32
BF16 = jnp.bfloat16

LOBATTO = (
    -1.0,
    -0.8717401485096066,
    -0.5917001814331423,
    -0.2092992179024789,
    0.2092992179024789,
    0.5917001814331423,
    0.8717401485096066,
    1.0,
)


def derivative_table():
    node_count = len(LOBATTO)
    barycentric = []
    for row_index in range(node_count):
        product = 1.0
        for col_index in range(node_count):
            if col_index != row_index:
                product = product * (LOBATTO[row_index] - LOBATTO[col_index])
        barycentric.append(1.0 / product)
    table_rows = []
    for row_index in range(node_count):
        entries = []
        for col_index in range(node_count):
            if col_index != row_index:
                entries.append(
                    barycentric[col_index]
                    / barycentric[row_index]
                    / (LOBATTO[row_index] - LOBATTO[col_index])
                )
            else:
                entries.append(0.0)
        entries[row_index] = -sum(entries)
        table_rows.append(entries)
    return np.asarray(table_rows, np.float32)


def np_split(table):
    table = np.asarray(table, np.float32)
    high = table.astype(ml_dtypes.bfloat16)
    low = (table - high.astype(np.float32)).astype(ml_dtypes.bfloat16)
    return high, low


def stiffness_table():
    d = derivative_table()
    eye = lambda n: np.eye(n, dtype=np.float32)
    axial = np.kron(eye(32), d)
    blocks = list(np_split(axial)) + list(np_split(axial.T))
    for small in (np.kron(eye(4), d), np.kron(eye(8), d.T)):
        high, low = np_split(small)
        row = np.concatenate([high, high, low], axis=1)
        blocks.append(np.pad(row, ((0, 0), (0, NODES - row.shape[1]))))
    return np.concatenate(blocks, axis=0)


def dft_tables():
    a = np.arange(2048)[:, None]
    m = np.arange(LANES)[None, :]
    angle = 2.0 * np.pi * ((a * m) % 2048) / 2048.0
    table = np.concatenate([np.cos(angle), np.sin(angle)], axis=1)
    high, low = np_split(table)
    k = np.arange(16)[:, None]
    lane = np.arange(LANES)[None, :]
    turn = 2.0 * np.pi * ((k * lane) % 16) / 16.0
    phase = np.stack([np.cos(turn), -np.sin(turn)], axis=1) / math.sqrt(2048.0)
    return high, low, phase.astype(np.float32)


def split(x):
    high = x.astype(BF16)
    return high, (x - high.astype(F32)).astype(BF16)


def dot(a, b):
    return jnp.dot(a, b, preferred_element_type=F32)


def left_mul(table, x):
    high, low = split(x)
    return dot(table, jnp.concatenate([high, low, high], axis=0))


def right_mul(x, table):
    high, low = split(x)
    return dot(jnp.concatenate([high, low, high], axis=1), table)


def square(table, k):
    return table[k * NODES : (k + 1) * NODES, :]


def axial_left(table):
    return jnp.concatenate([square(table, 0), square(table, 0), square(table, 1)], axis=1)


def axial_left_t(table):
    return jnp.concatenate([square(table, 2), square(table, 2), square(table, 3)], axis=1)


def girth_right(table):
    return jnp.concatenate([square(table, 2), square(table, 2), square(table, 3)], axis=0)


def girth_right_t(table):
    return jnp.concatenate([square(table, 0), square(table, 0), square(table, 1)], axis=0)


def radial_small(table):
    return table[4 * NODES : 4 * NODES + 32, :96]


def radial_small_t(table):
    return table[4 * NODES + 32 : 4 * NODES + 96, :192]


def radial_apply(x, matrix):
    half = P_SIZE // 2
    odd_rows = 0.5 * (matrix[:half, :half] - matrix[:half, : half - 1 : -1])
    even_rows = 0.5 * (matrix[:half, :half] + matrix[:half, : half - 1 : -1])
    outs = {}
    for element in range(2):
        for part in range(2):
            for tile in range(x.shape[1] // LANES):
                nodes = []
                for i in range(P_SIZE):
                    row = (element * P_SIZE + i) * 16 + part * 8
                    nodes.append(x[row : row + 8, tile * LANES : (tile + 1) * LANES])
                even = [nodes[j] + nodes[P_SIZE - 1 - j] for j in range(half)]
                odd = [nodes[j] - nodes[P_SIZE - 1 - j] for j in range(half)]
                for i in range(half):
                    p = float(odd_rows[i, 0]) * odd[0]
                    q = float(even_rows[i, 0]) * even[0]
                    for j in range(1, half):
                        p = p + float(odd_rows[i, j]) * odd[j]
                        q = q + float(even_rows[i, j]) * even[j]
                    outs[element * P_SIZE + i, part, tile] = p + q
                    outs[element * P_SIZE + P_SIZE - 1 - i, part, tile] = p - q
    columns = []
    for tile in range(x.shape[1] // LANES):
        columns.append(
            jnp.concatenate([outs[i, part, tile] for i in range(16) for part in range(2)], axis=0)
        )
    return jnp.concatenate(columns, axis=1)


def end_columns(rows):
    d = derivative_table()
    values = [float(x) for x in np.concatenate([d[:, 0], d[:, 7]])]
    node = lax.broadcasted_iota(jnp.int32, (16, LANES), 0)
    column = jnp.full((16, LANES), values[0], F32)
    for k in range(1, 16):
        column = jnp.where(node == k, values[k], column)
    return jnp.broadcast_to(column[None], (16, 16, LANES)).reshape(rows, LANES)


def stiff(u, gr, ga, gg, table):
    d = derivative_table()
    high, low = split(u)
    axial = dot(axial_left(table), jnp.concatenate([high, low, high], axis=0)) * ga
    girth = dot(jnp.concatenate([high, low, high], axis=1), girth_right(table)) * gg
    radial = radial_apply(radial_apply(u, d) * gr, d.T)
    return (
        left_mul(axial_left_t(table), axial) + right_mul(girth, girth_right_t(table)) + radial
    )


def twice(x):
    return jnp.concatenate([x, x], axis=1)


def sum_nodes(t):
    width = t.shape[1]
    v = t.reshape(16, 16, width)
    mid = v[7:8] + v[8:9]
    v = jnp.concatenate([v[:7], mid, mid, v[9:]], axis=0)
    pair = v[:, 7:8, :] + v[:, 8:9, :]
    node = lax.broadcasted_iota(jnp.int32, v.shape, 1)
    return jnp.where((node == 7) | (node == 8), pair, v)


def sum_girth(own, left, right, owners):
    lane = lax.broadcasted_iota(jnp.int32, left.shape, 1)
    first = lane % P_SIZE == 0
    last = lane % P_SIZE == P_SIZE - 1

    def inner(x):
        return jnp.where(
            first, pltpu.roll(x, 1, 1), jnp.where(last, pltpu.roll(x, LANES - 1, 1), 0.0)
        )

    sums = []
    for c, x in enumerate(own):
        p = inner(x)
        p = jnp.where(lane == 0, pltpu.roll(left, (LANES - HALO * c - HALO + 1) % LANES, 1), p)
        p = jnp.where(lane == LANES - 1, pltpu.roll(right, (LANES - 1 - HALO * c) % LANES, 1), p)
        sums.append(x + p)
    p = inner(left)
    q = inner(right)
    for c, x in enumerate(owners):
        p = jnp.where(lane == HALO * c + HALO - 1, pltpu.roll(x, HALO * c + HALO - 1, 1), p)
        q = jnp.where(lane == HALO * c, pltpu.roll(x, (HALO * c + 1) % LANES, 1), q)
    return sums + [left + p, right + q]


def shared_local(parts):
    return jnp.concatenate(sum_girth(parts[:4], parts[4], parts[5], parts[:4]), axis=1)


def lanes_of(x, k):
    return x[:, k * LANES : (k + 1) * LANES]


def pack_kernel(field_in, geom_in, mass_in, to_right, to_left, field, geom, mass, sems):
    copies = [
        pltpu.make_async_copy(field_in, field, sems.at[0]),
        pltpu.make_async_copy(geom_in, geom, sems.at[1]),
        pltpu.make_async_copy(mass_in, mass, sems.at[2]),
    ]
    for copy in copies:
        copy.start()
    lane = lax.broadcasted_iota(jnp.int32, (NODES, LANES), 1)

    def pack(arrays, start):
        out = None
        for k, x in enumerate(arrays):
            moved = pltpu.roll(x, (HALO * k - start) % LANES, 1) if (HALO * k - start) else x
            out = moved if out is None else jnp.where(lane // HALO == k, moved, out)
        return out

    copies[0].wait()
    fields = [field[c] for c in range(C)]
    to_right[0] = pack(fields, LANES - HALO)
    to_left[0] = pack(fields, 0)
    copies[1].wait()
    copies[2].wait()
    others = [geom[k] for k in range(3)] + [mass[...]]
    to_right[1] = pack(others, LANES - HALO)
    to_left[1] = pack(others, 0)


def own_kernel(field, geom, table, out):
    gr, ga, gg = [twice(geom[k]) for k in range(3)]
    for pair in range(2):
        u = jnp.concatenate([field[2 * pair], field[2 * pair + 1]], axis=1)
        out[:, 2 * pair * LANES : (2 * pair + 2) * LANES] = stiff(u, gr, ga, gg, table)


def at_faces(low, high, width):
    shape = (16, 16, width)
    node = lax.broadcasted_iota(jnp.int32, shape, 1)
    both = jnp.where(
        node == 0, low[:, None, :], jnp.where(node == 15, high[:, None, :], 0.0)
    )
    return both.reshape(NODES, width)


def wide(x):
    own = lanes_of(x, 0)
    return jnp.concatenate([own] * C + [x[:, LANES:]], axis=1)


def put_faces(x, low, high, offset):
    width = x.shape[1]
    v = x.reshape(16, 16, width)
    low[:, offset : offset + width] = v[:, 0, :]
    high[:, offset : offset + width] = v[:, 15, :]


def action(u, geom, halo_geom, tables):
    gr, ga, gg = [twice(geom[k]) for k in range(3)]
    parts = []
    for tile in range(3):
        if tile == 2:
            gr, ga, gg = [halo_geom[k] for k in range(3)]
        t = stiff(u[:, 2 * tile * LANES : (2 * tile + 2) * LANES], gr, ga, gg, tables)
        parts += [lanes_of(t, 0), lanes_of(t, 1)]
    return sum_nodes(shared_local(parts)).reshape(NODES, WIDE)


def inner_update(u, total, inverse):
    row = lax.broadcasted_iota(jnp.int32, u.shape, 0) % 16
    return jnp.where((row == 0) | (row == 15), u, u - total * wide(inverse))


def two_steps(u, geom, halo_geom, inverse, first, tables, state, second, low, high):
    v = inner_update(u, first, inverse)
    state[...] = v
    total = action(v, geom, halo_geom, tables)
    second[...] = total
    put_faces(first, low, high, 0)
    put_faces(total, low, high, WIDE)


STATIC = 2 * WIDE
NARROW = 3 * LANES


def halo_kernel(
    left, right, own_total, field, mass, geom, tables, halo_geom, state, second, mass_out, ends_out, low, high
):
    lane = lax.broadcasted_iota(jnp.int32, (NODES, LANES), 1)

    def spread(x, k):
        y = jnp.where(lane // HALO == k, x, 0.0)
        y = y + pltpu.roll(y, HALO, 1)
        return y + pltpu.roll(y, 2 * HALO, 1)

    left_others, right_others = left[1], right[1]
    geoms = []
    for k in range(3):
        g = jnp.concatenate([spread(left_others, k), spread(right_others, k)], axis=1)
        halo_geom[k] = g
        geoms.append(g)
    u = jnp.concatenate([left[0], right[0]], axis=1)
    t = stiff(u, *geoms, tables)
    parts = [own_total[:, c * LANES : (c + 1) * LANES] for c in range(C)]
    first = sum_nodes(shared_local(parts + [lanes_of(t, 0), lanes_of(t, 1)]))
    first = first.reshape(NODES, WIDE)
    m = mass[...]
    masses = sum_girth([m], spread(left_others, 3), spread(right_others, 3), [m] * C)
    lumped = sum_nodes(jnp.concatenate(masses, axis=1)).reshape(NODES, NARROW)
    mass_out[...] = lumped
    whole = [jnp.concatenate([geom[k], geoms[k]], axis=1) for k in range(3)]
    end = end_columns(NODES)
    ends = left_mul(axial_left_t(tables), whole[1] * jnp.concatenate([end] * 3, axis=1))
    ends_out[...] = ends
    for k, x in enumerate([lumped, whole[0], whole[2], ends]):
        put_faces(x, low, high, STATIC + k * NARROW)
    start = jnp.concatenate([field[c] for c in range(C)] + [u], axis=1)
    two_steps(start, geom, halo_geom, 1.0 / lumped, first, tables, state, second, low, high)


def static_part(ref, k):
    return ref[:, STATIC + k * NARROW : STATIC + (k + 1) * NARROW]


def finish_pair(state, second, inverse, ends, statics, own, got, tables):
    low, high, got_low, got_high = statics
    own_low, own_high = own
    new_low, new_high = got
    w_low = -(own_low[:, :WIDE] + new_low[:, :WIDE]) * wide(
        1.0 / (static_part(low, 0) + static_part(got_low, 0))
    )
    w_high = -(own_high[:, :WIDE] + new_high[:, :WIDE]) * wide(
        1.0 / (static_part(high, 0) + static_part(got_high, 0))
    )
    w = jnp.concatenate([w_low, w_high], axis=0)
    radial, girthwise = [
        wide(jnp.concatenate([static_part(ref, k) for ref in statics], axis=0)) for k in (1, 2)
    ]
    slope = left_mul(radial_small(tables), w)
    face = left_mul(radial_small_t(tables), jnp.concatenate([slope, slope], axis=0) * radial)
    pieces = []
    for tile in range(3):
        span = slice(2 * tile * LANES, (2 * tile + 2) * LANES)
        g = right_mul(w[:, span], girth_right(tables))
        y = jnp.concatenate([g, g], axis=0) * girthwise[:, span]
        pieces.append(right_mul(y, girth_right_t(tables)))
    face = face + jnp.concatenate(pieces, axis=1)
    other = jnp.concatenate([static_part(got_low, 3), static_part(got_high, 3)], axis=0)
    beyond = face[32:] + wide(other) * w
    beyond = shared_local([lanes_of(beyond, k) for k in range(6)]).reshape(2, 16, WIDE)
    pair = beyond[:, 7:8, :] + beyond[:, 8:9, :]
    node = lax.broadcasted_iota(jnp.int32, beyond.shape, 1)
    beyond = jnp.where((node == 7) | (node == 8), pair, beyond)
    beyond_low = beyond[0] + new_low[:, WIDE : 2 * WIDE]
    beyond_high = beyond[1] + new_high[:, WIDE : 2 * WIDE]
    node = lax.broadcasted_iota(jnp.int32, (16, 16, WIDE), 1)
    along = jnp.where(node < P_SIZE, w_low[:, None, :], w_high[:, None, :])
    change = wide(ends) * along.reshape(NODES, WIDE) + at_faces(face[:16], face[16:32], WIDE)
    change = sum_nodes(shared_local([lanes_of(change, k) for k in range(6)]))
    total = second + change.reshape(NODES, WIDE) + at_faces(beyond_low, beyond_high, WIDE)
    return state + at_faces(w_low, w_high, WIDE) - total * wide(inverse)


def middle_kernel(state, second, lumped, ends, low, high, got_low, got_high, geom, halo_geom, *refs):
    tables, state_out, second_out, inverse_out, next_low, next_high = refs
    inverse = 1.0 / (
        lumped[...] + at_faces(static_part(got_low, 0), static_part(got_high, 0), NARROW)
    )
    inverse_out[...] = inverse
    statics = (low, high, got_low, got_high)
    u = finish_pair(
        state[...], second[...], inverse, ends[...], statics, (low, high), (got_low, got_high), tables
    )
    first = action(u, geom, halo_geom, tables)
    two_steps(u, geom, halo_geom, inverse, first, tables, state_out, second_out, next_low, next_high)


def last_kernel(
    state,
    second,
    inverse,
    ends,
    low,
    high,
    got_low,
    got_high,
    own_low,
    own_high,
    new_low,
    new_high,
    slab,
    girth_weight,
    select,
    header,
    tables,
    out,
    packed,
    probes_out,
):
    u = finish_pair(
        state[...],
        second[...],
        inverse[...],
        ends[...],
        (low, high, got_low, got_high),
        (own_low, own_high),
        (new_low, new_high),
        tables,
    )
    u = u[:, : C * LANES]
    for c in range(C):
        out[c] = lanes_of(u, c)
    slab_high, slab_low = split(slab[...])
    values = left_mul(jnp.concatenate([slab_high, slab_high, slab_low], axis=1), u)
    stacked = jnp.concatenate([lanes_of(values, c) for c in range(C)], axis=0)
    weight_high, weight_low = split(girth_weight[...])
    weights = jnp.concatenate([weight_high, weight_high, weight_low], axis=0)
    probes = right_mul(stacked, weights)
    slots = slab.shape[0]
    spread = jnp.concatenate([probes[c * slots : (c + 1) * slots] for c in range(C)], axis=1)
    probes_out[...] = spread
    high_part, low_part = split(spread)
    chosen = select[...].astype(BF16)
    rows = dot(
        jnp.concatenate([chosen, chosen], axis=1),
        jnp.concatenate([high_part, low_part], axis=0),
    )
    for c in range(C):
        block = lanes_of(rows, c).reshape(-1, SLOTS, LANES)
        if c == 0:
            place = lax.broadcasted_iota(jnp.int32, block.shape, 1)
            block = jnp.where(place == SLOTS - 1, header[...][:, None, :], block)
        packed[:, c * SLOTS : (c + 1) * SLOTS, :] = block


def weights_kernel(
    cycle_id, cycle_radial, cycle_axial, cycle_weights, az_elem, az_weights, slab, girth, select, header
):
    slots = cycle_id.shape[0]
    ids = cycle_id[...].reshape(1, slots)
    in_radial, in_axial = [x[...].reshape(1, slots) for x in (cycle_radial, cycle_axial)]
    radial, axial = [
        jnp.concatenate(
            [jnp.where(owner == e, cycle_weights[k], 0.0) for e in range(2)], axis=0
        )
        for k, owner in enumerate((in_radial, in_axial))
    ]
    slab[...] = jnp.transpose((radial[:, None, :] * axial[None, :, :]).reshape(NODES, slots))
    places = az_elem[...].reshape(1, 1, LANES)
    element = lax.broadcasted_iota(jnp.int32, (LANES // P_SIZE, P_SIZE, LANES), 0)
    girth[...] = jnp.where(element == places, az_weights[...][None], 0.0).reshape(LANES, LANES)
    used = ids >= 0
    target = jnp.where(used, lax.shift_right_logical(ids, 4), -1).astype(F32)
    across = jnp.broadcast_to(target, (slots, slots))
    down = jnp.transpose(across)
    before = lax.broadcasted_iota(jnp.int32, across.shape, 0) < lax.broadcasted_iota(
        jnp.int32, across.shape, 1
    )
    rank = jnp.sum(jnp.where((across == down) & before, 1.0, 0.0), axis=0, keepdims=True)
    position = jnp.where(used & (rank < SLOTS - 1.5), target * SLOTS + rank, -1.0)
    wanted = lax.broadcasted_iota(jnp.int32, select.shape, 0).astype(F32)
    select[...] = jnp.where(wanted == position, 1.0, 0.0)
    number = (ids & (ROWS_DEV - 1)).astype(F32) + 1.0
    owners = lax.broadcasted_iota(jnp.int32, (header.shape[0], slots), 0).astype(F32)
    named = jnp.where(owners == target, number, 0.0).astype(BF16)
    ranks = lax.broadcasted_iota(jnp.int32, (LANES, slots), 0).astype(F32)
    placed = jnp.where(ranks == rank, 1.0, 0.0).astype(BF16)
    numbers = lax.dot_general(
        named, placed, (((1,), (1,)), ((), ())), preferred_element_type=F32
    )
    overflow = jnp.max(jnp.where(used & (rank > SLOTS - 1.5), 1.0, 0.0), axis=1, keepdims=True)
    lane = lax.broadcasted_iota(jnp.int32, header.shape, 1)
    header[...] = jnp.where(
        lane >= SLOTS, overflow, jnp.where(lane < SLOTS - 1, numbers, 0.0)
    )


def unpack_kernel(pieces, out, crowded):
    sources = pieces.shape[0]
    heads = pieces[:, 0:SLOTS, :]
    head = jnp.broadcast_to(heads[:, SLOTS - 1 : SLOTS, :], heads.shape)
    place = lax.broadcasted_iota(jnp.int32, heads.shape, 1)
    lane = lax.broadcasted_iota(jnp.int32, heads.shape, 2)
    mine = jnp.where((lane == place) & (place < SLOTS - 1), head, 0.0)
    crowded[0, 0] = jnp.max(jnp.where(lane >= SLOTS, head, 0.0)).astype(jnp.int32)
    row = jnp.sum(mine.reshape(sources * SLOTS, LANES), axis=1, keepdims=True)
    column = lax.broadcasted_iota(jnp.int32, (sources * SLOTS, LANES), 1).astype(F32)
    chosen = jnp.transpose(jnp.where(row == column + 1.0, 1.0, 0.0))[:ROWS_DEV].astype(BF16)
    both = jnp.concatenate([chosen, chosen], axis=1)
    for c in range(C):
        x = pieces[:, c * SLOTS : (c + 1) * SLOTS, :].reshape(sources * SLOTS, LANES)
        high, low = split(x)
        out[c * ROWS_DEV : (c + 1) * ROWS_DEV, :] = dot(
            both, jnp.concatenate([high, low], axis=0)
        )


def dft_kernel(rows, phase, table_high, table_low, out):
    turn_re = phase[0:1, :]
    turn_im = phase[1:2, :]
    total = None
    for pair in range(8):
        x = jnp.concatenate([rows[2 * pair], rows[2 * pair + 1]], axis=1)
        z = jnp.concatenate([x * twice(turn_re), x * twice(turn_im)], axis=0)
        high, low = split(z)
        block = pl.ds(pair * 256, 256)
        th, tl = table_high[block, :], table_low[block, :]
        part = dot(high, th) + dot(low, th) + dot(high, tl)
        total = part if total is None else total + part
    n = C * ROWS_DEV
    re = total[:n, :LANES] + total[n:, LANES:]
    im = total[n:, :LANES] - total[:n, LANES:]
    for c in range(C):
        out[0, :, c, :] = re[c * ROWS_DEV : (c + 1) * ROWS_DEV]
        out[1, :, c, :] = im[c * ROWS_DEV : (c + 1) * ROWS_DEV]


def call(kernel, shapes, flops, *args):
    vmem = pl.BlockSpec(memory_space=pltpu.VMEM)
    out_shape = [jax.ShapeDtypeStruct(s, F32) for s in shapes]
    return pl.pallas_call(
        kernel,
        out_shape=out_shape,
        in_specs=[vmem] * len(args),
        out_specs=[vmem] * len(shapes),
        compiler_params=pltpu.CompilerParams(vmem_limit_bytes=VMEM_LIMIT),
        cost_estimate=pl.CostEstimate(flops=flops, bytes_accessed=2000000, transcendentals=0),
    )(*args)


def pack_halos(*args):
    hbm, vmem = [pl.BlockSpec(memory_space=m) for m in (pltpu.HBM, pltpu.VMEM)]
    return pl.pallas_call(
        pack_kernel,
        out_shape=[jax.ShapeDtypeStruct((2, NODES, LANES), F32)] * 2,
        in_specs=[hbm] * len(args),
        out_specs=[vmem] * 2,
        scratch_shapes=[pltpu.VMEM(x.shape, F32) for x in args]
        + [pltpu.SemaphoreType.DMA((len(args),))],
        compiler_params=pltpu.CompilerParams(vmem_limit_bytes=LOAD_LIMIT),
    )(*args)


def body(
    field, geometry, mass, cycle_id, cycle_radial, cycle_axial, cycle_weights, az_elem, az_weights
):
    axial_count, girth_count = lax.axis_size("axial"), lax.axis_size("girth")
    up = [(i, i + 1) for i in range(axial_count - 1)]
    down = [(j, i) for i, j in up]
    around = [(i, (i + 1) % girth_count) for i in range(girth_count)]
    back = [(j, i) for i, j in around]
    field = field.reshape(C, NODES, LANES)
    geom = geometry.reshape(3, NODES, LANES)
    mass = mass.reshape(NODES, LANES)
    table = jnp.asarray(stiffness_table())
    to_right, to_left = pack_halos(field, geom, mass)
    tile_flops = 18 * 2 * 256**3

    left = lax.ppermute(to_right, "girth", around)
    right = lax.ppermute(to_left, "girth", back)
    (own_total,) = call(own_kernel, [(NODES, C * LANES)], 2 * tile_flops, field, geom, table)

    def exchange(low, high):
        return lax.ppermute(high, "axial", up), lax.ppermute(low, "axial", down)

    whole, narrow = (NODES, WIDE), (NODES, NARROW)
    face_static = (16, STATIC + 4 * NARROW)
    halo_geom, state, second, lumped, ends, low, high = call(
        halo_kernel,
        [(3, NODES, 2 * LANES), whole, whole, narrow, narrow, face_static, face_static],
        4 * tile_flops,
        left,
        right,
        own_total,
        field,
        mass,
        geom,
        table,
    )
    got_low, got_high = exchange(low, high)
    state, second, inverse, own_low, own_high = call(
        middle_kernel,
        [whole, whole, narrow, (16, STATIC), (16, STATIC)],
        6 * tile_flops,
        state,
        second,
        lumped,
        ends,
        low,
        high,
        got_low,
        got_high,
        geom,
        halo_geom,
        table,
    )
    new_low, new_high = exchange(own_low, own_high)

    slot_count = cycle_id.shape[0]
    slab, girth_weight, select, header = call(
        weights_kernel,
        [
            (slot_count, NODES),
            (LANES, LANES),
            (SLOTS * axial_count, slot_count),
            (axial_count, LANES),
        ],
        1000000,
        cycle_id,
        cycle_radial,
        cycle_axial,
        cycle_weights,
        az_elem,
        az_weights,
    )

    final, packed, probes = call(
        last_kernel,
        [(C, NODES, LANES), (axial_count, C * SLOTS, LANES), (slot_count, C * LANES)],
        tile_flops,
        state,
        second,
        inverse,
        ends,
        low,
        high,
        got_low,
        got_high,
        own_low,
        own_high,
        new_low,
        new_high,
        slab,
        girth_weight,
        select,
        header,
        table,
    )
    pieces = lax.all_to_all(packed, "axial", 0, 0)

    vmem = pl.BlockSpec(memory_space=pltpu.VMEM)
    rows, crowded = pl.pallas_call(
        unpack_kernel,
        out_shape=[
            jax.ShapeDtypeStruct((C * ROWS_DEV, LANES), F32),
            jax.ShapeDtypeStruct((1, 1), jnp.int32),
        ],
        in_specs=[vmem],
        out_specs=[vmem, pl.BlockSpec(memory_space=pltpu.SMEM)],
        compiler_params=pltpu.CompilerParams(vmem_limit_bytes=VMEM_LIMIT),
    )(pieces)

    def dense(rows, probes, cycle_id):
        wanted = jnp.arange(ROWS_DEV * axial_count, dtype=jnp.int32)
        chosen = (wanted[:, None] == cycle_id[None, :]).astype(F32)
        rows = jnp.dot(chosen, probes, precision=lax.Precision.HIGHEST)
        rows = rows.reshape(axial_count, ROWS_DEV, C * LANES)
        rows = jnp.sum(lax.all_to_all(rows, "axial", 0, 0), axis=0)
        return rows.reshape(ROWS_DEV, C, LANES).swapaxes(0, 1).reshape(C * ROWS_DEV, LANES)

    rows = lax.cond(
        crowded[0, 0] > 0, dense, lambda rows, *_: rows, rows, probes, cycle_id
    )
    rows = lax.all_gather(rows, "girth")
    table_high, table_low, phases = dft_tables()
    phase = lax.dynamic_index_in_dim(
        jnp.asarray(phases), lax.axis_index("girth"), 0, keepdims=False
    )
    (spectrum,) = call(
        dft_kernel,
        [(2, ROWS_DEV, C, LANES)],
        tile_flops,
        rows,
        phase,
        jnp.asarray(table_high),
        jnp.asarray(table_low),
    )
    return final.reshape(C, 16, 16, LANES), spectrum


def solution(mesh):
    return jax.shard_map(
        body,
        mesh=mesh,
        in_specs=(
            P(None, None, "axial", "girth"),
            P(None, None, "axial", "girth"),
            P(None, "axial", "girth"),
            P("axial"),
            P("axial"),
            P("axial"),
            P(None, None, "axial"),
            P("girth"),
            P(None, "girth"),
        ),
        out_specs=(P(None, None, "axial", "girth"), P(None, "axial", None, "girth")),
        check_vma=False,
    )
```

```python
import math

import jax
import jax.numpy as jnp
import ml_dtypes
import numpy as np
from jax import lax
from jax.experimental import pallas as pl
from jax.experimental.pallas import tpu as pltpu
from jax.sharding import PartitionSpec as P

C = 4
P_SIZE = 8
LANES = 128
HALO = 32
NODES = 256
WIDE = 6 * LANES
ROWS_DEV = 16
SLOTS = 8
VMEM_LIMIT = 32 * 1024 * 1024
LOAD_LIMIT = 60000000
F32 = jnp.float32
BF16 = jnp.bfloat16

LOBATTO = (
    -1.0,
    -0.8717401485096066,
    -0.5917001814331423,
    -0.2092992179024789,
    0.2092992179024789,
    0.5917001814331423,
    0.8717401485096066,
    1.0,
)


def derivative_table():
    node_count = len(LOBATTO)
    barycentric = []
    for row_index in range(node_count):
        product = 1.0
        for col_index in range(node_count):
            if col_index != row_index:
                product = product * (LOBATTO[row_index] - LOBATTO[col_index])
        barycentric.append(1.0 / product)
    table_rows = []
    for row_index in range(node_count):
        entries = []
        for col_index in range(node_count):
            if col_index != row_index:
                entries.append(
                    barycentric[col_index]
                    / barycentric[row_index]
                    / (LOBATTO[row_index] - LOBATTO[col_index])
                )
            else:
                entries.append(0.0)
        entries[row_index] = -sum(entries)
        table_rows.append(entries)
    return np.asarray(table_rows, np.float32)


def np_split(table):
    table = np.asarray(table, np.float32)
    high = table.astype(ml_dtypes.bfloat16)
    low = (table - high.astype(np.float32)).astype(ml_dtypes.bfloat16)
    return high, low


def stiffness_table():
    d = derivative_table()
    eye = lambda n: np.eye(n, dtype=np.float32)
    axial = np.kron(eye(32), d)
    blocks = list(np_split(axial)) + list(np_split(axial.T))
    ends = axial.T.reshape(16, 16, NODES)[:, [0, 15]].swapaxes(0, 1).reshape(32, NODES)
    blocks += list(np_split(ends))
    for small in (np.kron(eye(4), d), np.kron(eye(8), d.T), np.kron(eye(4), d.T)):
        high, low = np_split(small)
        row = np.concatenate([high, high, low], axis=1)
        blocks.append(np.pad(row, ((0, 0), (0, NODES - row.shape[1]))))
    return np.concatenate(blocks, axis=0)


def dft_tables():
    a = np.arange(2048)[:, None]
    m = np.arange(LANES)[None, :]
    angle = 2.0 * np.pi * ((a * m) % 2048) / 2048.0
    table = np.concatenate([np.cos(angle), np.sin(angle)], axis=1)
    high, low = np_split(table)
    k = np.arange(16)[:, None]
    lane = np.arange(LANES)[None, :]
    turn = 2.0 * np.pi * ((k * lane) % 16) / 16.0
    phase = np.stack([np.cos(turn), -np.sin(turn)], axis=1) / math.sqrt(2048.0)
    return high, low, phase.astype(np.float32)


def split(x):
    high = x.astype(BF16)
    return high, (x - high.astype(F32)).astype(BF16)


def dot(a, b):
    return jnp.dot(a, b, preferred_element_type=F32)


def left_mul(table, x):
    high, low = split(x)
    return dot(table, jnp.concatenate([high, low, high], axis=0))


def right_mul(x, table):
    high, low = split(x)
    return dot(jnp.concatenate([high, low, high], axis=1), table)


def square(table, k):
    return table[k * NODES : (k + 1) * NODES, :]


def axial_left(table):
    return jnp.concatenate([square(table, 0), square(table, 0), square(table, 1)], axis=1)


def axial_left_t(table):
    return jnp.concatenate([square(table, 2), square(table, 2), square(table, 3)], axis=1)


def girth_right(table):
    return jnp.concatenate([square(table, 2), square(table, 2), square(table, 3)], axis=0)


def girth_right_t(table):
    return jnp.concatenate([square(table, 0), square(table, 0), square(table, 1)], axis=0)


SMALL = 4 * NODES


def ends_left(table):
    high, low = table[SMALL : SMALL + 32, :], table[SMALL + 32 : SMALL + 64, :]
    return jnp.concatenate([high, high, low], axis=1)


def radial_small(table):
    return table[SMALL + 64 : SMALL + 96, :96]


def radial_small_t(table):
    return table[SMALL + 96 : SMALL + 160, :192]


def radial_faces_t(table):
    return table[SMALL + 160 : SMALL + 192, :96]


def radial_apply(x, matrix):
    half = P_SIZE // 2
    odd_rows = 0.5 * (matrix[:half, :half] - matrix[:half, : half - 1 : -1])
    even_rows = 0.5 * (matrix[:half, :half] + matrix[:half, : half - 1 : -1])
    outs = {}
    for element in range(2):
        for part in range(2):
            for tile in range(x.shape[1] // LANES):
                nodes = []
                for i in range(P_SIZE):
                    row = (element * P_SIZE + i) * 16 + part * 8
                    nodes.append(x[row : row + 8, tile * LANES : (tile + 1) * LANES])
                even = [nodes[j] + nodes[P_SIZE - 1 - j] for j in range(half)]
                odd = [nodes[j] - nodes[P_SIZE - 1 - j] for j in range(half)]
                for i in range(half):
                    p = float(odd_rows[i, 0]) * odd[0]
                    q = float(even_rows[i, 0]) * even[0]
                    for j in range(1, half):
                        p = p + float(odd_rows[i, j]) * odd[j]
                        q = q + float(even_rows[i, j]) * even[j]
                    outs[element * P_SIZE + i, part, tile] = p + q
                    outs[element * P_SIZE + P_SIZE - 1 - i, part, tile] = p - q
    columns = []
    for tile in range(x.shape[1] // LANES):
        columns.append(
            jnp.concatenate([outs[i, part, tile] for i in range(16) for part in range(2)], axis=0)
        )
    return jnp.concatenate(columns, axis=1)


def end_columns(rows):
    d = derivative_table()
    values = [float(x) for x in np.concatenate([d[:, 0], d[:, 7]])]
    node = lax.broadcasted_iota(jnp.int32, (16, LANES), 0)
    column = jnp.full((16, LANES), values[0], F32)
    for k in range(1, 16):
        column = jnp.where(node == k, values[k], column)
    return jnp.broadcast_to(column[None], (16, 16, LANES)).reshape(rows, LANES)


def stiff(u, gr, ga, gg, table):
    d = derivative_table()
    high, low = split(u)
    axial = dot(axial_left(table), jnp.concatenate([high, low, high], axis=0)) * ga
    girth = dot(jnp.concatenate([high, low, high], axis=1), girth_right(table)) * gg
    radial = radial_apply(radial_apply(u, d) * gr, d.T)
    return (
        left_mul(axial_left_t(table), axial) + right_mul(girth, girth_right_t(table)) + radial
    )


def twice(x):
    return jnp.concatenate([x, x], axis=1)


def sum_nodes(t):
    width = t.shape[1]
    v = t.reshape(16, 16, width)
    mid = v[7:8] + v[8:9]
    v = jnp.concatenate([v[:7], mid, mid, v[9:]], axis=0)
    pair = v[:, 7:8, :] + v[:, 8:9, :]
    node = lax.broadcasted_iota(jnp.int32, v.shape, 1)
    return jnp.where((node == 7) | (node == 8), pair, v)


def sum_girth(own, left, right, owners):
    lane = lax.broadcasted_iota(jnp.int32, left.shape, 1)
    first = lane % P_SIZE == 0
    last = lane % P_SIZE == P_SIZE - 1

    def inner(x):
        return jnp.where(
            first, pltpu.roll(x, 1, 1), jnp.where(last, pltpu.roll(x, LANES - 1, 1), 0.0)
        )

    sums = []
    for c, x in enumerate(own):
        p = inner(x)
        p = jnp.where(lane == 0, pltpu.roll(left, (LANES - HALO * c - HALO + 1) % LANES, 1), p)
        p = jnp.where(lane == LANES - 1, pltpu.roll(right, (LANES - 1 - HALO * c) % LANES, 1), p)
        sums.append(x + p)
    p = inner(left)
    q = inner(right)
    for c, x in enumerate(owners):
        p = jnp.where(lane == HALO * c + HALO - 1, pltpu.roll(x, HALO * c + HALO - 1, 1), p)
        q = jnp.where(lane == HALO * c, pltpu.roll(x, (HALO * c + 1) % LANES, 1), q)
    return sums + [left + p, right + q]


def shared_local(parts):
    return jnp.concatenate(sum_girth(parts[:4], parts[4], parts[5], parts[:4]), axis=1)


def lanes_of(x, k):
    return x[:, k * LANES : (k + 1) * LANES]


def pack_kernel(field_in, geom_in, mass_in, to_right, to_left, field, geom, mass, sems):
    copies = [
        pltpu.make_async_copy(field_in, field, sems.at[0]),
        pltpu.make_async_copy(geom_in, geom, sems.at[1]),
        pltpu.make_async_copy(mass_in, mass, sems.at[2]),
    ]
    for copy in copies:
        copy.start()
    lane = lax.broadcasted_iota(jnp.int32, (NODES, LANES), 1)

    def pack(arrays, start):
        out = None
        for k, x in enumerate(arrays):
            moved = pltpu.roll(x, (HALO * k - start) % LANES, 1) if (HALO * k - start) else x
            out = moved if out is None else jnp.where(lane // HALO == k, moved, out)
        return out

    copies[0].wait()
    fields = [field[c] for c in range(C)]
    to_right[0] = pack(fields, LANES - HALO)
    to_left[0] = pack(fields, 0)
    copies[1].wait()
    copies[2].wait()
    others = [geom[k] for k in range(3)] + [mass[...]]
    to_right[1] = pack(others, LANES - HALO)
    to_left[1] = pack(others, 0)


def own_kernel(field, geom, table, out):
    gr, ga, gg = [twice(geom[k]) for k in range(3)]
    for pair in range(2):
        u = jnp.concatenate([field[2 * pair], field[2 * pair + 1]], axis=1)
        out[:, 2 * pair * LANES : (2 * pair + 2) * LANES] = stiff(u, gr, ga, gg, table)


def at_faces(low, high, width):
    shape = (16, 16, width)
    node = lax.broadcasted_iota(jnp.int32, shape, 1)
    both = jnp.where(
        node == 0, low[:, None, :], jnp.where(node == 15, high[:, None, :], 0.0)
    )
    return both.reshape(NODES, width)


def wide(x):
    own = lanes_of(x, 0)
    return jnp.concatenate([own] * C + [x[:, LANES:]], axis=1)


def put_faces(x, low, high, offset):
    width = x.shape[1]
    v = x.reshape(16, 16, width)
    low[:, offset : offset + width] = v[:, 0, :]
    high[:, offset : offset + width] = v[:, 15, :]


def action(u, geom, halo_geom, tables):
    gr, ga, gg = [twice(geom[k]) for k in range(3)]
    parts = []
    for tile in range(3):
        if tile == 2:
            gr, ga, gg = [halo_geom[k] for k in range(3)]
        t = stiff(u[:, 2 * tile * LANES : (2 * tile + 2) * LANES], gr, ga, gg, tables)
        parts += [lanes_of(t, 0), lanes_of(t, 1)]
    return sum_nodes(shared_local(parts)).reshape(NODES, WIDE)


def inner_update(u, total, inverse):
    row = lax.broadcasted_iota(jnp.int32, u.shape, 0) % 16
    return jnp.where((row == 0) | (row == 15), u, u - total * wide(inverse))


def sum_faces(x):
    summed = shared_local([lanes_of(x, k) for k in range(6)]).reshape(2, 16, WIDE)
    pair = summed[:, 7:8, :] + summed[:, 8:9, :]
    node = lax.broadcasted_iota(jnp.int32, summed.shape, 1)
    return jnp.where((node == 7) | (node == 8), pair, summed)


def face_action(v, geom, halo_geom, statics, table):
    low, high = statics
    radial, girthwise = [
        wide(jnp.concatenate([static_part(low, k), static_part(high, k)], axis=0)) for k in (1, 2)
    ]
    nodes = v.reshape(16, 16, WIDE)
    ends = jnp.concatenate([nodes[:, 0, :], nodes[:, 15, :]], axis=0)
    face = left_mul(radial_faces_t(table), left_mul(radial_small(table), ends) * radial)
    pieces = []
    for tile in range(3):
        span = slice(2 * tile * LANES, (2 * tile + 2) * LANES)
        ga = halo_geom[1] if tile == 2 else twice(geom[1])
        slope = left_mul(axial_left(table), v[:, span]) * ga
        g = right_mul(ends[:, span], girth_right(table)) * girthwise[:, span]
        pieces.append(left_mul(ends_left(table), slope) + right_mul(g, girth_right_t(table)))
    return sum_faces(face + jnp.concatenate(pieces, axis=1))


def two_steps(u, geom, halo_geom, inverse, first, statics, table, state, low, high):
    v = inner_update(u, first, inverse)
    state[...] = v
    put_faces(first, low, high, 0)
    faces = face_action(v, geom, halo_geom, statics, table)
    low[:, WIDE : 2 * WIDE] = faces[0]
    high[:, WIDE : 2 * WIDE] = faces[1]


def second_kernel(state, geom, halo_geom, table, out):
    out[...] = action(state[...], geom, halo_geom, table)


STATIC = 2 * WIDE
NARROW = 3 * LANES


def halo_kernel(
    left, right, own_total, field, mass, geom, tables, halo_geom, state, mass_out, ends_out, low, high
):
    lane = lax.broadcasted_iota(jnp.int32, (NODES, LANES), 1)

    def spread(x, k):
        y = jnp.where(lane // HALO == k, x, 0.0)
        y = y + pltpu.roll(y, HALO, 1)
        return y + pltpu.roll(y, 2 * HALO, 1)

    left_others, right_others = left[1], right[1]
    geoms = []
    for k in range(3):
        g = jnp.concatenate([spread(left_others, k), spread(right_others, k)], axis=1)
        halo_geom[k] = g
        geoms.append(g)
    u = jnp.concatenate([left[0], right[0]], axis=1)
    t = stiff(u, *geoms, tables)
    parts = [own_total[:, c * LANES : (c + 1) * LANES] for c in range(C)]
    first = sum_nodes(shared_local(parts + [lanes_of(t, 0), lanes_of(t, 1)]))
    first = first.reshape(NODES, WIDE)
    m = mass[...]
    masses = sum_girth([m], spread(left_others, 3), spread(right_others, 3), [m] * C)
    lumped = sum_nodes(jnp.concatenate(masses, axis=1)).reshape(NODES, NARROW)
    mass_out[...] = lumped
    whole = [jnp.concatenate([geom[k], geoms[k]], axis=1) for k in range(3)]
    end = end_columns(NODES)
    ends = left_mul(axial_left_t(tables), whole[1] * jnp.concatenate([end] * 3, axis=1))
    ends_out[...] = ends
    for k, x in enumerate([lumped, whole[0], whole[2], ends]):
        put_faces(x, low, high, STATIC + k * NARROW)
    start = jnp.concatenate([field[c] for c in range(C)] + [u], axis=1)
    two_steps(start, geom, halo_geom, 1.0 / lumped, first, (low, high), tables, state, low, high)


def static_part(ref, k):
    return ref[:, STATIC + k * NARROW : STATIC + (k + 1) * NARROW]


def finish_pair(state, second, inverse, ends, statics, own, got, tables):
    low, high, got_low, got_high = statics
    own_low, own_high = own
    new_low, new_high = got
    w_low = -(own_low[:, :WIDE] + new_low[:, :WIDE]) * wide(
        1.0 / (static_part(low, 0) + static_part(got_low, 0))
    )
    w_high = -(own_high[:, :WIDE] + new_high[:, :WIDE]) * wide(
        1.0 / (static_part(high, 0) + static_part(got_high, 0))
    )
    w = jnp.concatenate([w_low, w_high], axis=0)
    radial, girthwise = [
        wide(jnp.concatenate([static_part(ref, k) for ref in statics], axis=0)) for k in (1, 2)
    ]
    slope = left_mul(radial_small(tables), w)
    face = left_mul(radial_small_t(tables), jnp.concatenate([slope, slope], axis=0) * radial)
    pieces = []
    for tile in range(3):
        span = slice(2 * tile * LANES, (2 * tile + 2) * LANES)
        g = right_mul(w[:, span], girth_right(tables))
        y = jnp.concatenate([g, g], axis=0) * girthwise[:, span]
        pieces.append(right_mul(y, girth_right_t(tables)))
    face = face + jnp.concatenate(pieces, axis=1)
    other = jnp.concatenate([static_part(got_low, 3), static_part(got_high, 3)], axis=0)
    beyond = face[32:] + wide(other) * w
    beyond = sum_faces(beyond)
    beyond_low = beyond[0] + new_low[:, WIDE : 2 * WIDE]
    beyond_high = beyond[1] + new_high[:, WIDE : 2 * WIDE]
    node = lax.broadcasted_iota(jnp.int32, (16, 16, WIDE), 1)
    along = jnp.where(node < P_SIZE, w_low[:, None, :], w_high[:, None, :])
    change = wide(ends) * along.reshape(NODES, WIDE) + at_faces(face[:16], face[16:32], WIDE)
    change = sum_nodes(shared_local([lanes_of(change, k) for k in range(6)]))
    total = second + change.reshape(NODES, WIDE) + at_faces(beyond_low, beyond_high, WIDE)
    return state + at_faces(w_low, w_high, WIDE) - total * wide(inverse)


def middle_kernel(state, second, lumped, ends, low, high, got_low, got_high, geom, halo_geom, *refs):
    tables, state_out, inverse_out, next_low, next_high = refs
    inverse = 1.0 / (
        lumped[...] + at_faces(static_part(got_low, 0), static_part(got_high, 0), NARROW)
    )
    inverse_out[...] = inverse
    statics = (low, high, got_low, got_high)
    u = finish_pair(
        state[...], second[...], inverse, ends[...], statics, (low, high), (got_low, got_high), tables
    )
    first = action(u, geom, halo_geom, tables)
    two_steps(u, geom, halo_geom, inverse, first, (low, high), tables, state_out, next_low, next_high)


def last_kernel(
    state,
    second,
    inverse,
    ends,
    low,
    high,
    got_low,
    got_high,
    own_low,
    own_high,
    new_low,
    new_high,
    slab,
    girth_weight,
    select,
    header,
    tables,
    out,
    packed,
    probes_out,
):
    u = finish_pair(
        state[...],
        second[...],
        inverse[...],
        ends[...],
        (low, high, got_low, got_high),
        (own_low, own_high),
        (new_low, new_high),
        tables,
    )
    u = u[:, : C * LANES]
    for c in range(C):
        out[c] = lanes_of(u, c)
    slab_high, slab_low = split(slab[...])
    values = left_mul(jnp.concatenate([slab_high, slab_high, slab_low], axis=1), u)
    stacked = jnp.concatenate([lanes_of(values, c) for c in range(C)], axis=0)
    weight_high, weight_low = split(girth_weight[...])
    weights = jnp.concatenate([weight_high, weight_high, weight_low], axis=0)
    probes = right_mul(stacked, weights)
    slots = slab.shape[0]
    spread = jnp.concatenate([probes[c * slots : (c + 1) * slots] for c in range(C)], axis=1)
    probes_out[...] = spread
    high_part, low_part = split(spread)
    chosen = select[...].astype(BF16)
    rows = dot(
        jnp.concatenate([chosen, chosen], axis=1),
        jnp.concatenate([high_part, low_part], axis=0),
    )
    for c in range(C):
        block = lanes_of(rows, c).reshape(-1, SLOTS, LANES)
        if c == 0:
            place = lax.broadcasted_iota(jnp.int32, block.shape, 1)
            block = jnp.where(place == SLOTS - 1, header[...][:, None, :], block)
        packed[:, c * SLOTS : (c + 1) * SLOTS, :] = block


def weights_kernel(
    cycle_id, cycle_radial, cycle_axial, cycle_weights, az_elem, az_weights, slab, girth, select, header
):
    slots = cycle_id.shape[0]
    ids = cycle_id[...].reshape(1, slots)
    in_radial, in_axial = [x[...].reshape(1, slots) for x in (cycle_radial, cycle_axial)]
    radial, axial = [
        jnp.concatenate(
            [jnp.where(owner == e, cycle_weights[k], 0.0) for e in range(2)], axis=0
        )
        for k, owner in enumerate((in_radial, in_axial))
    ]
    slab[...] = jnp.transpose((radial[:, None, :] * axial[None, :, :]).reshape(NODES, slots))
    places = az_elem[...].reshape(1, 1, LANES)
    element = lax.broadcasted_iota(jnp.int32, (LANES // P_SIZE, P_SIZE, LANES), 0)
    girth[...] = jnp.where(element == places, az_weights[...][None], 0.0).reshape(LANES, LANES)
    used = ids >= 0
    target = jnp.where(used, lax.shift_right_logical(ids, 4), -1).astype(F32)
    across = jnp.broadcast_to(target, (slots, slots))
    down = jnp.transpose(across)
    before = lax.broadcasted_iota(jnp.int32, across.shape, 0) < lax.broadcasted_iota(
        jnp.int32, across.shape, 1
    )
    rank = jnp.sum(jnp.where((across == down) & before, 1.0, 0.0), axis=0, keepdims=True)
    position = jnp.where(used & (rank < SLOTS - 1.5), target * SLOTS + rank, -1.0)
    wanted = lax.broadcasted_iota(jnp.int32, select.shape, 0).astype(F32)
    select[...] = jnp.where(wanted == position, 1.0, 0.0)
    number = (ids & (ROWS_DEV - 1)).astype(F32) + 1.0
    owners = lax.broadcasted_iota(jnp.int32, (header.shape[0], slots), 0).astype(F32)
    named = jnp.where(owners == target, number, 0.0).astype(BF16)
    ranks = lax.broadcasted_iota(jnp.int32, (LANES, slots), 0).astype(F32)
    placed = jnp.where(ranks == rank, 1.0, 0.0).astype(BF16)
    numbers = lax.dot_general(
        named, placed, (((1,), (1,)), ((), ())), preferred_element_type=F32
    )
    overflow = jnp.max(jnp.where(used & (rank > SLOTS - 1.5), 1.0, 0.0), axis=1, keepdims=True)
    lane = lax.broadcasted_iota(jnp.int32, header.shape, 1)
    header[...] = jnp.where(
        lane >= SLOTS, overflow, jnp.where(lane < SLOTS - 1, numbers, 0.0)
    )


def unpack_kernel(pieces, out, crowded):
    sources = pieces.shape[0]
    heads = pieces[:, 0:SLOTS, :]
    head = jnp.broadcast_to(heads[:, SLOTS - 1 : SLOTS, :], heads.shape)
    place = lax.broadcasted_iota(jnp.int32, heads.shape, 1)
    lane = lax.broadcasted_iota(jnp.int32, heads.shape, 2)
    mine = jnp.where((lane == place) & (place < SLOTS - 1), head, 0.0)
    crowded[0, 0] = jnp.max(jnp.where(lane >= SLOTS, head, 0.0)).astype(jnp.int32)
    row = jnp.sum(mine.reshape(sources * SLOTS, LANES), axis=1, keepdims=True)
    column = lax.broadcasted_iota(jnp.int32, (sources * SLOTS, LANES), 1).astype(F32)
    chosen = jnp.transpose(jnp.where(row == column + 1.0, 1.0, 0.0))[:ROWS_DEV].astype(BF16)
    both = jnp.concatenate([chosen, chosen], axis=1)
    for c in range(C):
        x = pieces[:, c * SLOTS : (c + 1) * SLOTS, :].reshape(sources * SLOTS, LANES)
        high, low = split(x)
        out[c * ROWS_DEV : (c + 1) * ROWS_DEV, :] = dot(
            both, jnp.concatenate([high, low], axis=0)
        )


def dft_kernel(rows, phase, table_high, table_low, out):
    turn_re = phase[0:1, :]
    turn_im = phase[1:2, :]
    total = None
    for pair in range(8):
        x = jnp.concatenate([rows[2 * pair], rows[2 * pair + 1]], axis=1)
        z = jnp.concatenate([x * twice(turn_re), x * twice(turn_im)], axis=0)
        high, low = split(z)
        block = pl.ds(pair * 256, 256)
        th, tl = table_high[block, :], table_low[block, :]
        part = dot(high, th) + dot(low, th) + dot(high, tl)
        total = part if total is None else total + part
    n = C * ROWS_DEV
    re = total[:n, :LANES] + total[n:, LANES:]
    im = total[n:, :LANES] - total[:n, LANES:]
    for c in range(C):
        out[0, :, c, :] = re[c * ROWS_DEV : (c + 1) * ROWS_DEV]
        out[1, :, c, :] = im[c * ROWS_DEV : (c + 1) * ROWS_DEV]


def call(kernel, shapes, flops, *args):
    vmem = pl.BlockSpec(memory_space=pltpu.VMEM)
    out_shape = [jax.ShapeDtypeStruct(s, F32) for s in shapes]
    return pl.pallas_call(
        kernel,
        out_shape=out_shape,
        in_specs=[vmem] * len(args),
        out_specs=[vmem] * len(shapes),
        compiler_params=pltpu.CompilerParams(vmem_limit_bytes=VMEM_LIMIT),
        cost_estimate=pl.CostEstimate(flops=flops, bytes_accessed=2000000, transcendentals=0),
    )(*args)


def pack_halos(*args):
    hbm, vmem = [pl.BlockSpec(memory_space=m) for m in (pltpu.HBM, pltpu.VMEM)]
    return pl.pallas_call(
        pack_kernel,
        out_shape=[jax.ShapeDtypeStruct((2, NODES, LANES), F32)] * 2,
        in_specs=[hbm] * len(args),
        out_specs=[vmem] * 2,
        scratch_shapes=[pltpu.VMEM(x.shape, F32) for x in args]
        + [pltpu.SemaphoreType.DMA((len(args),))],
        compiler_params=pltpu.CompilerParams(vmem_limit_bytes=LOAD_LIMIT),
    )(*args)


def body(
    field, geometry, mass, cycle_id, cycle_radial, cycle_axial, cycle_weights, az_elem, az_weights
):
    axial_count, girth_count = lax.axis_size("axial"), lax.axis_size("girth")
    up = [(i, i + 1) for i in range(axial_count - 1)]
    down = [(j, i) for i, j in up]
    around = [(i, (i + 1) % girth_count) for i in range(girth_count)]
    back = [(j, i) for i, j in around]
    field = field.reshape(C, NODES, LANES)
    geom = geometry.reshape(3, NODES, LANES)
    mass = mass.reshape(NODES, LANES)
    table = jnp.asarray(stiffness_table())
    to_right, to_left = pack_halos(field, geom, mass)
    tile_flops = 18 * 2 * 256**3

    left = lax.ppermute(to_right, "girth", around)
    right = lax.ppermute(to_left, "girth", back)
    (own_total,) = call(own_kernel, [(NODES, C * LANES)], 2 * tile_flops, field, geom, table)

    def exchange(low, high):
        return lax.ppermute(high, "axial", up), lax.ppermute(low, "axial", down)

    whole, narrow = (NODES, WIDE), (NODES, NARROW)
    face_static = (16, STATIC + 4 * NARROW)
    halo_geom, state, lumped, ends, low, high = call(
        halo_kernel,
        [(3, NODES, 2 * LANES), whole, narrow, narrow, face_static, face_static],
        2 * tile_flops,
        left,
        right,
        own_total,
        field,
        mass,
        geom,
        table,
    )
    got_low, got_high = exchange(low, high)
    (second,) = call(second_kernel, [whole], 3 * tile_flops, state, geom, halo_geom, table)
    state, inverse, own_low, own_high = call(
        middle_kernel,
        [whole, narrow, (16, STATIC), (16, STATIC)],
        4 * tile_flops,
        state,
        second,
        lumped,
        ends,
        low,
        high,
        got_low,
        got_high,
        geom,
        halo_geom,
        table,
    )
    new_low, new_high = exchange(own_low, own_high)
    (second,) = call(second_kernel, [whole], 3 * tile_flops, state, geom, halo_geom, table)

    slot_count = cycle_id.shape[0]
    slab, girth_weight, select, header = call(
        weights_kernel,
        [
            (slot_count, NODES),
            (LANES, LANES),
            (SLOTS * axial_count, slot_count),
            (axial_count, LANES),
        ],
        1000000,
        cycle_id,
        cycle_radial,
        cycle_axial,
        cycle_weights,
        az_elem,
        az_weights,
    )

    final, packed, probes = call(
        last_kernel,
        [(C, NODES, LANES), (axial_count, C * SLOTS, LANES), (slot_count, C * LANES)],
        tile_flops,
        state,
        second,
        inverse,
        ends,
        low,
        high,
        got_low,
        got_high,
        own_low,
        own_high,
        new_low,
        new_high,
        slab,
        girth_weight,
        select,
        header,
        table,
    )
    pieces = lax.all_to_all(packed, "axial", 0, 0)

    vmem = pl.BlockSpec(memory_space=pltpu.VMEM)
    rows, crowded = pl.pallas_call(
        unpack_kernel,
        out_shape=[
            jax.ShapeDtypeStruct((C * ROWS_DEV, LANES), F32),
            jax.ShapeDtypeStruct((1, 1), jnp.int32),
        ],
        in_specs=[vmem],
        out_specs=[vmem, pl.BlockSpec(memory_space=pltpu.SMEM)],
        compiler_params=pltpu.CompilerParams(vmem_limit_bytes=VMEM_LIMIT),
    )(pieces)

    def dense(rows, probes, cycle_id):
        wanted = jnp.arange(ROWS_DEV * axial_count, dtype=jnp.int32)
        chosen = (wanted[:, None] == cycle_id[None, :]).astype(F32)
        rows = jnp.dot(chosen, probes, precision=lax.Precision.HIGHEST)
        rows = rows.reshape(axial_count, ROWS_DEV, C * LANES)
        rows = jnp.sum(lax.all_to_all(rows, "axial", 0, 0), axis=0)
        return rows.reshape(ROWS_DEV, C, LANES).swapaxes(0, 1).reshape(C * ROWS_DEV, LANES)

    rows = lax.cond(
        crowded[0, 0] > 0, dense, lambda rows, *_: rows, rows, probes, cycle_id
    )
    rows = lax.all_gather(rows, "girth")
    table_high, table_low, phases = dft_tables()
    phase = lax.dynamic_index_in_dim(
        jnp.asarray(phases), lax.axis_index("girth"), 0, keepdims=False
    )
    (spectrum,) = call(
        dft_kernel,
        [(2, ROWS_DEV, C, LANES)],
        tile_flops,
        rows,
        phase,
        jnp.asarray(table_high),
        jnp.asarray(table_low),
    )
    return final.reshape(C, 16, 16, LANES), spectrum


def solution(mesh):
    return jax.shard_map(
        body,
        mesh=mesh,
        in_specs=(
            P(None, None, "axial", "girth"),
            P(None, None, "axial", "girth"),
            P(None, "axial", "girth"),
            P("axial"),
            P("axial"),
            P("axial"),
            P(None, None, "axial"),
            P("girth"),
            P(None, "girth"),
        ),
        out_specs=(P(None, None, "axial", "girth"), P(None, "axial", None, "girth")),
        check_vma=False,
    )
```

```python
import math

import jax
import jax.numpy as jnp
import ml_dtypes
import numpy as np
from jax import lax
from jax.experimental import pallas as pl
from jax.experimental.pallas import tpu as pltpu
from jax.sharding import PartitionSpec as P

C = 4
P_SIZE = 8
LANES = 128
HALO = 32
NODES = 256
WIDE = 6 * LANES
ROWS_DEV = 16
SLOTS = 8
VMEM_LIMIT = 32 * 1024 * 1024
LOAD_LIMIT = 60000000
F32 = jnp.float32
BF16 = jnp.bfloat16

LOBATTO = (
    -1.0,
    -0.8717401485096066,
    -0.5917001814331423,
    -0.2092992179024789,
    0.2092992179024789,
    0.5917001814331423,
    0.8717401485096066,
    1.0,
)


def derivative_table():
    node_count = len(LOBATTO)
    barycentric = []
    for row_index in range(node_count):
        product = 1.0
        for col_index in range(node_count):
            if col_index != row_index:
                product = product * (LOBATTO[row_index] - LOBATTO[col_index])
        barycentric.append(1.0 / product)
    table_rows = []
    for row_index in range(node_count):
        entries = []
        for col_index in range(node_count):
            if col_index != row_index:
                entries.append(
                    barycentric[col_index]
                    / barycentric[row_index]
                    / (LOBATTO[row_index] - LOBATTO[col_index])
                )
            else:
                entries.append(0.0)
        entries[row_index] = -sum(entries)
        table_rows.append(entries)
    return np.asarray(table_rows, np.float32)


def np_split(table):
    table = np.asarray(table, np.float32)
    high = table.astype(ml_dtypes.bfloat16)
    low = (table - high.astype(np.float32)).astype(ml_dtypes.bfloat16)
    return high, low


def stiffness_table():
    d = derivative_table()
    eye = lambda n: np.eye(n, dtype=np.float32)
    axial = np.kron(eye(32), d)
    blocks = list(np_split(axial)) + list(np_split(axial.T))
    ends = axial.T.reshape(16, 16, NODES)[:, [0, 15]].swapaxes(0, 1).reshape(32, NODES)
    blocks += list(np_split(ends))
    for small in (np.kron(eye(4), d), np.kron(eye(8), d.T), np.kron(eye(4), d.T)):
        high, low = np_split(small)
        row = np.concatenate([high, high, low], axis=1)
        blocks.append(np.pad(row, ((0, 0), (0, NODES - row.shape[1]))))
    return np.concatenate(blocks, axis=0)


def dft_tables():
    a = np.arange(2048)[:, None]
    m = np.arange(LANES)[None, :]
    angle = 2.0 * np.pi * ((a * m) % 2048) / 2048.0
    table = np.concatenate([np.cos(angle), np.sin(angle)], axis=1)
    high, low = np_split(table)
    k = np.arange(16)[:, None]
    lane = np.arange(LANES)[None, :]
    turn = 2.0 * np.pi * ((k * lane) % 16) / 16.0
    phase = np.stack([np.cos(turn), -np.sin(turn)], axis=1) / math.sqrt(2048.0)
    return high, low, phase.astype(np.float32)


def split(x):
    high = x.astype(BF16)
    return high, (x - high.astype(F32)).astype(BF16)


def dot(a, b):
    return jnp.dot(a, b, preferred_element_type=F32)


def left_mul(table, x):
    high, low = split(x)
    return dot(table, jnp.concatenate([high, low, high], axis=0))


def right_mul(x, table):
    high, low = split(x)
    return dot(jnp.concatenate([high, low, high], axis=1), table)


def square(table, k):
    return table[k * NODES : (k + 1) * NODES, :]


def axial_left(table):
    return jnp.concatenate([square(table, 0), square(table, 0), square(table, 1)], axis=1)


def axial_left_t(table):
    return jnp.concatenate([square(table, 2), square(table, 2), square(table, 3)], axis=1)


def girth_right(table):
    return jnp.concatenate([square(table, 2), square(table, 2), square(table, 3)], axis=0)


def girth_right_t(table):
    return jnp.concatenate([square(table, 0), square(table, 0), square(table, 1)], axis=0)


SMALL = 4 * NODES


def ends_pair(table):
    return table[SMALL : SMALL + 64, :]


def radial_small(table):
    return table[SMALL + 64 : SMALL + 96, :96]


def radial_small_t(table):
    return table[SMALL + 96 : SMALL + 160, :192]


def radial_faces_t(table):
    return table[SMALL + 160 : SMALL + 192, :96]


def radial_apply(x, matrix):
    half = P_SIZE // 2
    odd_rows = 0.5 * (matrix[:half, :half] - matrix[:half, : half - 1 : -1])
    even_rows = 0.5 * (matrix[:half, :half] + matrix[:half, : half - 1 : -1])
    outs = {}
    for element in range(2):
        for part in range(2):
            for tile in range(x.shape[1] // LANES):
                nodes = []
                for i in range(P_SIZE):
                    row = (element * P_SIZE + i) * 16 + part * 8
                    nodes.append(x[row : row + 8, tile * LANES : (tile + 1) * LANES])
                even = [nodes[j] + nodes[P_SIZE - 1 - j] for j in range(half)]
                odd = [nodes[j] - nodes[P_SIZE - 1 - j] for j in range(half)]
                for i in range(half):
                    p = float(odd_rows[i, 0]) * odd[0]
                    q = float(even_rows[i, 0]) * even[0]
                    for j in range(1, half):
                        p = p + float(odd_rows[i, j]) * odd[j]
                        q = q + float(even_rows[i, j]) * even[j]
                    outs[element * P_SIZE + i, part, tile] = p + q
                    outs[element * P_SIZE + P_SIZE - 1 - i, part, tile] = p - q
    columns = []
    for tile in range(x.shape[1] // LANES):
        columns.append(
            jnp.concatenate([outs[i, part, tile] for i in range(16) for part in range(2)], axis=0)
        )
    return jnp.concatenate(columns, axis=1)


def end_columns(rows):
    d = derivative_table()
    values = [float(x) for x in np.concatenate([d[:, 0], d[:, 7]])]
    node = lax.broadcasted_iota(jnp.int32, (16, LANES), 0)
    column = jnp.full((16, LANES), values[0], F32)
    for k in range(1, 16):
        column = jnp.where(node == k, values[k], column)
    return jnp.broadcast_to(column[None], (16, 16, LANES)).reshape(rows, LANES)


def stiff_many(us, geoms, table):
    d = derivative_table()
    halves = [split(u) for u in us]
    rows = [jnp.concatenate([high, low, high], axis=1) for high, low in halves]
    girth = dot(jnp.concatenate(rows, axis=0), girth_right(table))
    girth = girth * jnp.concatenate([g[2] for g in geoms], axis=0)
    girth = right_mul(girth, girth_right_t(table))
    outs = []
    for k, (u, (high, low), (gr, ga, _)) in enumerate(zip(us, halves, geoms)):
        axial = dot(axial_left(table), jnp.concatenate([high, low, high], axis=0)) * ga
        radial = radial_apply(radial_apply(u, d) * gr, d.T)
        part = girth[k * NODES : (k + 1) * NODES]
        outs.append(left_mul(axial_left_t(table), axial) + part + radial)
    return outs


def left_pair(both, x):
    high, low = split(x)
    rows = both.shape[0] // 2
    first = dot(both, high)
    return first[:rows] + first[rows:] + dot(both[:rows], low)


def girth_faces(x, factor, repeat, table):
    rows = x.shape[0]
    stacked = jnp.concatenate([x[:, k * NODES : (k + 1) * NODES] for k in range(3)], axis=0)
    slope = right_mul(stacked, girth_right(table))
    scaled = []
    for k in range(3):
        part = slope[k * rows : (k + 1) * rows]
        part = jnp.concatenate([part] * repeat, axis=0)
        scaled.append(part * factor[:, k * NODES : (k + 1) * NODES])
    moved = right_mul(jnp.concatenate(scaled, axis=0), girth_right_t(table))
    rows = rows * repeat
    return jnp.concatenate([moved[k * rows : (k + 1) * rows] for k in range(3)], axis=1)


def twice(x):
    return jnp.concatenate([x, x], axis=1)


def sum_nodes(t):
    width = t.shape[1]
    v = t.reshape(16, 16, width)
    mid = v[7:8] + v[8:9]
    v = jnp.concatenate([v[:7], mid, mid, v[9:]], axis=0)
    pair = v[:, 7:8, :] + v[:, 8:9, :]
    node = lax.broadcasted_iota(jnp.int32, v.shape, 1)
    return jnp.where((node == 7) | (node == 8), pair, v)


def sum_girth(own, left, right, owners):
    lane = lax.broadcasted_iota(jnp.int32, left.shape, 1)
    first = lane % P_SIZE == 0
    last = lane % P_SIZE == P_SIZE - 1

    def inner(x):
        return jnp.where(
            first, pltpu.roll(x, 1, 1), jnp.where(last, pltpu.roll(x, LANES - 1, 1), 0.0)
        )

    sums = []
    for c, x in enumerate(own):
        p = inner(x)
        p = jnp.where(lane == 0, pltpu.roll(left, (LANES - HALO * c - HALO + 1) % LANES, 1), p)
        p = jnp.where(lane == LANES - 1, pltpu.roll(right, (LANES - 1 - HALO * c) % LANES, 1), p)
        sums.append(x + p)
    p = inner(left)
    q = inner(right)
    for c, x in enumerate(owners):
        p = jnp.where(lane == HALO * c + HALO - 1, pltpu.roll(x, HALO * c + HALO - 1, 1), p)
        q = jnp.where(lane == HALO * c, pltpu.roll(x, (HALO * c + 1) % LANES, 1), q)
    return sums + [left + p, right + q]


def shared_local(parts):
    return jnp.concatenate(sum_girth(parts[:4], parts[4], parts[5], parts[:4]), axis=1)


def lanes_of(x, k):
    return x[:, k * LANES : (k + 1) * LANES]


def pack_kernel(field_in, geom_in, mass_in, to_right, to_left, field, geom, mass, sems):
    copies = [
        pltpu.make_async_copy(field_in, field, sems.at[0]),
        pltpu.make_async_copy(geom_in, geom, sems.at[1]),
        pltpu.make_async_copy(mass_in, mass, sems.at[2]),
    ]
    for copy in copies:
        copy.start()
    lane = lax.broadcasted_iota(jnp.int32, (NODES, LANES), 1)

    def pack(arrays, start):
        out = None
        for k, x in enumerate(arrays):
            moved = pltpu.roll(x, (HALO * k - start) % LANES, 1) if (HALO * k - start) else x
            out = moved if out is None else jnp.where(lane // HALO == k, moved, out)
        return out

    copies[0].wait()
    fields = [field[c] for c in range(C)]
    to_right[0] = pack(fields, LANES - HALO)
    to_left[0] = pack(fields, 0)
    copies[1].wait()
    copies[2].wait()
    others = [geom[k] for k in range(3)] + [mass[...]]
    to_right[1] = pack(others, LANES - HALO)
    to_left[1] = pack(others, 0)


def own_kernel(field, geom, table, out):
    geoms = tuple(twice(geom[k]) for k in range(3))
    us = [jnp.concatenate([field[2 * k], field[2 * k + 1]], axis=1) for k in range(2)]
    out[...] = jnp.concatenate(stiff_many(us, [geoms] * 2, table), axis=1)


def at_faces(low, high, width):
    shape = (16, 16, width)
    node = lax.broadcasted_iota(jnp.int32, shape, 1)
    both = jnp.where(
        node == 0, low[:, None, :], jnp.where(node == 15, high[:, None, :], 0.0)
    )
    return both.reshape(NODES, width)


def wide(x):
    own = lanes_of(x, 0)
    return jnp.concatenate([own] * C + [x[:, LANES:]], axis=1)


def put_faces(x, low, high, offset):
    width = x.shape[1]
    v = x.reshape(16, 16, width)
    low[:, offset : offset + width] = v[:, 0, :]
    high[:, offset : offset + width] = v[:, 15, :]


def action(u, geom, halo_geom, tables):
    own = tuple(twice(geom[k]) for k in range(3))
    geoms = [own, own, tuple(halo_geom[k] for k in range(3))]
    us = [u[:, k * NODES : (k + 1) * NODES] for k in range(3)]
    parts = []
    for t in stiff_many(us, geoms, tables):
        parts += [lanes_of(t, 0), lanes_of(t, 1)]
    return sum_nodes(shared_local(parts)).reshape(NODES, WIDE)


def inner_update(u, total, inverse):
    row = lax.broadcasted_iota(jnp.int32, u.shape, 0) % 16
    return jnp.where((row == 0) | (row == 15), u, u - total * wide(inverse))


def sum_faces(x):
    summed = shared_local([lanes_of(x, k) for k in range(6)]).reshape(2, 16, WIDE)
    pair = summed[:, 7:8, :] + summed[:, 8:9, :]
    node = lax.broadcasted_iota(jnp.int32, summed.shape, 1)
    return jnp.where((node == 7) | (node == 8), pair, summed)


def face_action(v, geom, halo_geom, statics, table):
    low, high = statics
    radial, girthwise = [
        wide(jnp.concatenate([static_part(low, k), static_part(high, k)], axis=0)) for k in (1, 2)
    ]
    nodes = v.reshape(16, 16, WIDE)
    ends = jnp.concatenate([nodes[:, 0, :], nodes[:, 15, :]], axis=0)
    face = left_mul(radial_faces_t(table), left_mul(radial_small(table), ends) * radial)
    face = face + girth_faces(ends, girthwise, 1, table)
    pieces = []
    for tile in range(3):
        ga = halo_geom[1] if tile == 2 else twice(geom[1])
        slope = left_pair(table[: 2 * NODES, :], v[:, tile * NODES : (tile + 1) * NODES]) * ga
        pieces.append(left_pair(ends_pair(table), slope))
    return sum_faces(face + jnp.concatenate(pieces, axis=1))


def two_steps(u, geom, halo_geom, inverse, first, statics, table, state, low, high):
    v = inner_update(u, first, inverse)
    state[...] = v
    put_faces(first, low, high, 0)
    faces = face_action(v, geom, halo_geom, statics, table)
    low[:, WIDE : 2 * WIDE] = faces[0]
    high[:, WIDE : 2 * WIDE] = faces[1]


def second_kernel(state, geom, halo_geom, table, out):
    out[...] = action(state[...], geom, halo_geom, table)


STATIC = 2 * WIDE
NARROW = 3 * LANES


def halo_kernel(
    left, right, own_total, field, mass, geom, tables, halo_geom, state, mass_out, ends_out, low, high
):
    lane = lax.broadcasted_iota(jnp.int32, (NODES, LANES), 1)

    def spread(x, k):
        y = jnp.where(lane // HALO == k, x, 0.0)
        y = y + pltpu.roll(y, HALO, 1)
        return y + pltpu.roll(y, 2 * HALO, 1)

    left_others, right_others = left[1], right[1]
    geoms = []
    for k in range(3):
        g = jnp.concatenate([spread(left_others, k), spread(right_others, k)], axis=1)
        halo_geom[k] = g
        geoms.append(g)
    u = jnp.concatenate([left[0], right[0]], axis=1)
    (t,) = stiff_many([u], [tuple(geoms)], tables)
    parts = [own_total[:, c * LANES : (c + 1) * LANES] for c in range(C)]
    first = sum_nodes(shared_local(parts + [lanes_of(t, 0), lanes_of(t, 1)]))
    first = first.reshape(NODES, WIDE)
    m = mass[...]
    masses = sum_girth([m], spread(left_others, 3), spread(right_others, 3), [m] * C)
    lumped = sum_nodes(jnp.concatenate(masses, axis=1)).reshape(NODES, NARROW)
    mass_out[...] = lumped
    whole = [jnp.concatenate([geom[k], geoms[k]], axis=1) for k in range(3)]
    end = end_columns(NODES)
    ends = left_mul(axial_left_t(tables), whole[1] * jnp.concatenate([end] * 3, axis=1))
    ends_out[...] = ends
    for k, x in enumerate([lumped, whole[0], whole[2], ends]):
        put_faces(x, low, high, STATIC + k * NARROW)
    start = jnp.concatenate([field[c] for c in range(C)] + [u], axis=1)
    two_steps(start, geom, halo_geom, 1.0 / lumped, first, (low, high), tables, state, low, high)


def static_part(ref, k):
    return ref[:, STATIC + k * NARROW : STATIC + (k + 1) * NARROW]


def finish_pair(state, second, inverse, ends, statics, own, got, tables):
    low, high, got_low, got_high = statics
    own_low, own_high = own
    new_low, new_high = got
    w_low = -(own_low[:, :WIDE] + new_low[:, :WIDE]) * wide(
        1.0 / (static_part(low, 0) + static_part(got_low, 0))
    )
    w_high = -(own_high[:, :WIDE] + new_high[:, :WIDE]) * wide(
        1.0 / (static_part(high, 0) + static_part(got_high, 0))
    )
    w = jnp.concatenate([w_low, w_high], axis=0)
    radial, girthwise = [
        wide(jnp.concatenate([static_part(ref, k) for ref in statics], axis=0)) for k in (1, 2)
    ]
    slope = left_mul(radial_small(tables), w)
    face = left_mul(radial_small_t(tables), jnp.concatenate([slope, slope], axis=0) * radial)
    face = face + girth_faces(w, girthwise, 2, tables)
    other = jnp.concatenate([static_part(got_low, 3), static_part(got_high, 3)], axis=0)
    beyond = face[32:] + wide(other) * w
    beyond = sum_faces(beyond)
    beyond_low = beyond[0] + new_low[:, WIDE : 2 * WIDE]
    beyond_high = beyond[1] + new_high[:, WIDE : 2 * WIDE]
    node = lax.broadcasted_iota(jnp.int32, (16, 16, WIDE), 1)
    along = jnp.where(node < P_SIZE, w_low[:, None, :], w_high[:, None, :])
    change = wide(ends) * along.reshape(NODES, WIDE) + at_faces(face[:16], face[16:32], WIDE)
    change = sum_nodes(shared_local([lanes_of(change, k) for k in range(6)]))
    total = second + change.reshape(NODES, WIDE) + at_faces(beyond_low, beyond_high, WIDE)
    return state + at_faces(w_low, w_high, WIDE) - total * wide(inverse)


def middle_kernel(state, second, lumped, ends, low, high, got_low, got_high, geom, halo_geom, *refs):
    tables, state_out, inverse_out, next_low, next_high = refs
    inverse = 1.0 / (
        lumped[...] + at_faces(static_part(got_low, 0), static_part(got_high, 0), NARROW)
    )
    inverse_out[...] = inverse
    statics = (low, high, got_low, got_high)
    u = finish_pair(
        state[...], second[...], inverse, ends[...], statics, (low, high), (got_low, got_high), tables
    )
    first = action(u, geom, halo_geom, tables)
    two_steps(u, geom, halo_geom, inverse, first, (low, high), tables, state_out, next_low, next_high)


def last_kernel(
    state,
    second,
    inverse,
    ends,
    low,
    high,
    got_low,
    got_high,
    own_low,
    own_high,
    new_low,
    new_high,
    slab,
    girth_weight,
    select,
    header,
    tables,
    out,
    packed,
    probes_out,
):
    u = finish_pair(
        state[...],
        second[...],
        inverse[...],
        ends[...],
        (low, high, got_low, got_high),
        (own_low, own_high),
        (new_low, new_high),
        tables,
    )
    u = u[:, : C * LANES]
    for c in range(C):
        out[c] = lanes_of(u, c)
    slab_high, slab_low = split(slab[...])
    values = left_mul(jnp.concatenate([slab_high, slab_high, slab_low], axis=1), u)
    stacked = jnp.concatenate([lanes_of(values, c) for c in range(C)], axis=0)
    weight_high, weight_low = split(girth_weight[...])
    weights = jnp.concatenate([weight_high, weight_high, weight_low], axis=0)
    probes = right_mul(stacked, weights)
    slots = slab.shape[0]
    spread = jnp.concatenate([probes[c * slots : (c + 1) * slots] for c in range(C)], axis=1)
    probes_out[...] = spread
    high_part, low_part = split(spread)
    chosen = select[...].astype(BF16)
    rows = dot(
        jnp.concatenate([chosen, chosen], axis=1),
        jnp.concatenate([high_part, low_part], axis=0),
    )
    for c in range(C):
        block = lanes_of(rows, c).reshape(-1, SLOTS, LANES)
        if c == 0:
            place = lax.broadcasted_iota(jnp.int32, block.shape, 1)
            block = jnp.where(place == SLOTS - 1, header[...][:, None, :], block)
        packed[:, c * SLOTS : (c + 1) * SLOTS, :] = block


def weights_kernel(
    cycle_id, cycle_radial, cycle_axial, cycle_weights, az_elem, az_weights, slab, girth, select, header
):
    slots = cycle_id.shape[0]
    ids = cycle_id[...].reshape(1, slots)
    in_radial, in_axial = [x[...].reshape(1, slots) for x in (cycle_radial, cycle_axial)]
    radial, axial = [
        jnp.concatenate(
            [jnp.where(owner == e, cycle_weights[k], 0.0) for e in range(2)], axis=0
        )
        for k, owner in enumerate((in_radial, in_axial))
    ]
    slab[...] = jnp.transpose((radial[:, None, :] * axial[None, :, :]).reshape(NODES, slots))
    places = az_elem[...].reshape(1, 1, LANES)
    element = lax.broadcasted_iota(jnp.int32, (LANES // P_SIZE, P_SIZE, LANES), 0)
    girth[...] = jnp.where(element == places, az_weights[...][None], 0.0).reshape(LANES, LANES)
    used = ids >= 0
    target = jnp.where(used, lax.shift_right_logical(ids, 4), -1).astype(F32)
    across = jnp.broadcast_to(target, (slots, slots))
    down = jnp.transpose(across)
    before = lax.broadcasted_iota(jnp.int32, across.shape, 0) < lax.broadcasted_iota(
        jnp.int32, across.shape, 1
    )
    rank = jnp.sum(jnp.where((across == down) & before, 1.0, 0.0), axis=0, keepdims=True)
    position = jnp.where(used & (rank < SLOTS - 1.5), target * SLOTS + rank, -1.0)
    wanted = lax.broadcasted_iota(jnp.int32, select.shape, 0).astype(F32)
    select[...] = jnp.where(wanted == position, 1.0, 0.0)
    number = (ids & (ROWS_DEV - 1)).astype(F32) + 1.0
    owners = lax.broadcasted_iota(jnp.int32, (header.shape[0], slots), 0).astype(F32)
    named = jnp.where(owners == target, number, 0.0).astype(BF16)
    ranks = lax.broadcasted_iota(jnp.int32, (LANES, slots), 0).astype(F32)
    placed = jnp.where(ranks == rank, 1.0, 0.0).astype(BF16)
    numbers = lax.dot_general(
        named, placed, (((1,), (1,)), ((), ())), preferred_element_type=F32
    )
    overflow = jnp.max(jnp.where(used & (rank > SLOTS - 1.5), 1.0, 0.0), axis=1, keepdims=True)
    lane = lax.broadcasted_iota(jnp.int32, header.shape, 1)
    header[...] = jnp.where(
        lane >= SLOTS, overflow, jnp.where(lane < SLOTS - 1, numbers, 0.0)
    )


def unpack_kernel(pieces, out, crowded):
    sources = pieces.shape[0]
    heads = pieces[:, 0:SLOTS, :]
    head = jnp.broadcast_to(heads[:, SLOTS - 1 : SLOTS, :], heads.shape)
    place = lax.broadcasted_iota(jnp.int32, heads.shape, 1)
    lane = lax.broadcasted_iota(jnp.int32, heads.shape, 2)
    mine = jnp.where((lane == place) & (place < SLOTS - 1), head, 0.0)
    crowded[0, 0] = jnp.max(jnp.where(lane >= SLOTS, head, 0.0)).astype(jnp.int32)
    row = jnp.sum(mine.reshape(sources * SLOTS, LANES), axis=1, keepdims=True)
    column = lax.broadcasted_iota(jnp.int32, (sources * SLOTS, LANES), 1).astype(F32)
    chosen = jnp.transpose(jnp.where(row == column + 1.0, 1.0, 0.0))[:ROWS_DEV].astype(BF16)
    both = jnp.concatenate([chosen, chosen], axis=1)
    for c in range(C):
        x = pieces[:, c * SLOTS : (c + 1) * SLOTS, :].reshape(sources * SLOTS, LANES)
        high, low = split(x)
        out[c * ROWS_DEV : (c + 1) * ROWS_DEV, :] = dot(
            both, jnp.concatenate([high, low], axis=0)
        )


def dft_kernel(rows, phase, table_high, table_low, out):
    turn_re = phase[0:1, :]
    turn_im = phase[1:2, :]
    total = None
    for pair in range(8):
        x = jnp.concatenate([rows[2 * pair], rows[2 * pair + 1]], axis=1)
        z = jnp.concatenate([x * twice(turn_re), x * twice(turn_im)], axis=0)
        high, low = split(z)
        block = pl.ds(pair * 256, 256)
        th, tl = table_high[block, :], table_low[block, :]
        part = dot(high, th) + dot(low, th) + dot(high, tl)
        total = part if total is None else total + part
    n = C * ROWS_DEV
    re = total[:n, :LANES] + total[n:, LANES:]
    im = total[n:, :LANES] - total[:n, LANES:]
    for c in range(C):
        out[0, :, c, :] = re[c * ROWS_DEV : (c + 1) * ROWS_DEV]
        out[1, :, c, :] = im[c * ROWS_DEV : (c + 1) * ROWS_DEV]


def call(kernel, shapes, flops, *args):
    vmem = pl.BlockSpec(memory_space=pltpu.VMEM)
    out_shape = [jax.ShapeDtypeStruct(s, F32) for s in shapes]
    return pl.pallas_call(
        kernel,
        out_shape=out_shape,
        in_specs=[vmem] * len(args),
        out_specs=[vmem] * len(shapes),
        compiler_params=pltpu.CompilerParams(vmem_limit_bytes=VMEM_LIMIT),
        cost_estimate=pl.CostEstimate(flops=flops, bytes_accessed=2000000, transcendentals=0),
    )(*args)


def pack_halos(*args):
    hbm, vmem = [pl.BlockSpec(memory_space=m) for m in (pltpu.HBM, pltpu.VMEM)]
    return pl.pallas_call(
        pack_kernel,
        out_shape=[jax.ShapeDtypeStruct((2, NODES, LANES), F32)] * 2,
        in_specs=[hbm] * len(args),
        out_specs=[vmem] * 2,
        scratch_shapes=[pltpu.VMEM(x.shape, F32) for x in args]
        + [pltpu.SemaphoreType.DMA((len(args),))],
        compiler_params=pltpu.CompilerParams(vmem_limit_bytes=LOAD_LIMIT),
    )(*args)


def body(
    field, geometry, mass, cycle_id, cycle_radial, cycle_axial, cycle_weights, az_elem, az_weights
):
    axial_count, girth_count = lax.axis_size("axial"), lax.axis_size("girth")
    up = [(i, i + 1) for i in range(axial_count - 1)]
    down = [(j, i) for i, j in up]
    around = [(i, (i + 1) % girth_count) for i in range(girth_count)]
    back = [(j, i) for i, j in around]
    field = field.reshape(C, NODES, LANES)
    geom = geometry.reshape(3, NODES, LANES)
    mass = mass.reshape(NODES, LANES)
    table = jnp.asarray(stiffness_table())
    to_right, to_left = pack_halos(field, geom, mass)
    tile_flops = 18 * 2 * 256**3

    left = lax.ppermute(to_right, "girth", around)
    right = lax.ppermute(to_left, "girth", back)
    (own_total,) = call(own_kernel, [(NODES, C * LANES)], 2 * tile_flops, field, geom, table)

    def exchange(low, high):
        return lax.ppermute(high, "axial", up), lax.ppermute(low, "axial", down)

    whole, narrow = (NODES, WIDE), (NODES, NARROW)
    face_static = (16, STATIC + 4 * NARROW)
    halo_geom, state, lumped, ends, low, high = call(
        halo_kernel,
        [(3, NODES, 2 * LANES), whole, narrow, narrow, face_static, face_static],
        2 * tile_flops,
        left,
        right,
        own_total,
        field,
        mass,
        geom,
        table,
    )
    got_low, got_high = exchange(low, high)
    (second,) = call(second_kernel, [whole], 3 * tile_flops, state, geom, halo_geom, table)
    state, inverse, own_low, own_high = call(
        middle_kernel,
        [whole, narrow, (16, STATIC), (16, STATIC)],
        4 * tile_flops,
        state,
        second,
        lumped,
        ends,
        low,
        high,
        got_low,
        got_high,
        geom,
        halo_geom,
        table,
    )
    new_low, new_high = exchange(own_low, own_high)
    (second,) = call(second_kernel, [whole], 3 * tile_flops, state, geom, halo_geom, table)

    slot_count = cycle_id.shape[0]
    slab, girth_weight, select, header = call(
        weights_kernel,
        [
            (slot_count, NODES),
            (LANES, LANES),
            (SLOTS * axial_count, slot_count),
            (axial_count, LANES),
        ],
        1000000,
        cycle_id,
        cycle_radial,
        cycle_axial,
        cycle_weights,
        az_elem,
        az_weights,
    )

    final, packed, probes = call(
        last_kernel,
        [(C, NODES, LANES), (axial_count, C * SLOTS, LANES), (slot_count, C * LANES)],
        tile_flops,
        state,
        second,
        inverse,
        ends,
        low,
        high,
        got_low,
        got_high,
        own_low,
        own_high,
        new_low,
        new_high,
        slab,
        girth_weight,
        select,
        header,
        table,
    )
    pieces = lax.all_to_all(packed, "axial", 0, 0)

    vmem = pl.BlockSpec(memory_space=pltpu.VMEM)
    rows, crowded = pl.pallas_call(
        unpack_kernel,
        out_shape=[
            jax.ShapeDtypeStruct((C * ROWS_DEV, LANES), F32),
            jax.ShapeDtypeStruct((1, 1), jnp.int32),
        ],
        in_specs=[vmem],
        out_specs=[vmem, pl.BlockSpec(memory_space=pltpu.SMEM)],
        compiler_params=pltpu.CompilerParams(vmem_limit_bytes=VMEM_LIMIT),
    )(pieces)

    def dense(rows, probes, cycle_id):
        wanted = jnp.arange(ROWS_DEV * axial_count, dtype=jnp.int32)
        chosen = (wanted[:, None] == cycle_id[None, :]).astype(F32)
        rows = jnp.dot(chosen, probes, precision=lax.Precision.HIGHEST)
        rows = rows.reshape(axial_count, ROWS_DEV, C * LANES)
        rows = jnp.sum(lax.all_to_all(rows, "axial", 0, 0), axis=0)
        return rows.reshape(ROWS_DEV, C, LANES).swapaxes(0, 1).reshape(C * ROWS_DEV, LANES)

    rows = lax.cond(
        crowded[0, 0] > 0, dense, lambda rows, *_: rows, rows, probes, cycle_id
    )
    rows = lax.all_gather(rows, "girth")
    table_high, table_low, phases = dft_tables()
    phase = lax.dynamic_index_in_dim(
        jnp.asarray(phases), lax.axis_index("girth"), 0, keepdims=False
    )
    (spectrum,) = call(
        dft_kernel,
        [(2, ROWS_DEV, C, LANES)],
        tile_flops,
        rows,
        phase,
        jnp.asarray(table_high),
        jnp.asarray(table_low),
    )
    return final.reshape(C, 16, 16, LANES), spectrum


def solution(mesh):
    return jax.shard_map(
        body,
        mesh=mesh,
        in_specs=(
            P(None, None, "axial", "girth"),
            P(None, None, "axial", "girth"),
            P(None, "axial", "girth"),
            P("axial"),
            P("axial"),
            P("axial"),
            P(None, None, "axial"),
            P("girth"),
            P(None, "girth"),
        ),
        out_specs=(P(None, None, "axial", "girth"), P(None, "axial", None, "girth")),
        check_vma=False,
    )
```

```python
import math

import jax
import jax.numpy as jnp
import ml_dtypes
import numpy as np
from jax import lax
from jax.experimental import pallas as pl
from jax.experimental.pallas import tpu as pltpu
from jax.sharding import PartitionSpec as P

C = 4
P_SIZE = 8
LANES = 128
HALO = 32
NODES = 256
WIDE = 6 * LANES
ROWS_DEV = 16
SLOTS = 8
VMEM_LIMIT = 32 * 1024 * 1024
LOAD_LIMIT = 60000000
F32 = jnp.float32
BF16 = jnp.bfloat16

LOBATTO = (
    -1.0,
    -0.8717401485096066,
    -0.5917001814331423,
    -0.2092992179024789,
    0.2092992179024789,
    0.5917001814331423,
    0.8717401485096066,
    1.0,
)


def derivative_table():
    node_count = len(LOBATTO)
    barycentric = []
    for row_index in range(node_count):
        product = 1.0
        for col_index in range(node_count):
            if col_index != row_index:
                product = product * (LOBATTO[row_index] - LOBATTO[col_index])
        barycentric.append(1.0 / product)
    table_rows = []
    for row_index in range(node_count):
        entries = []
        for col_index in range(node_count):
            if col_index != row_index:
                entries.append(
                    barycentric[col_index]
                    / barycentric[row_index]
                    / (LOBATTO[row_index] - LOBATTO[col_index])
                )
            else:
                entries.append(0.0)
        entries[row_index] = -sum(entries)
        table_rows.append(entries)
    return np.asarray(table_rows, np.float32)


def np_split(table):
    table = np.asarray(table, np.float32)
    high = table.astype(ml_dtypes.bfloat16)
    low = (table - high.astype(np.float32)).astype(ml_dtypes.bfloat16)
    return high, low


def stiffness_table():
    d = derivative_table()
    eye = lambda n: np.eye(n, dtype=np.float32)
    axial = np.kron(eye(32), d)
    blocks = list(np_split(axial)) + list(np_split(axial.T))
    ends = axial.T.reshape(16, 16, NODES)[:, [0, 15]].swapaxes(0, 1).reshape(32, NODES)
    blocks += list(np_split(ends))
    for small in (np.kron(eye(4), d), np.kron(eye(8), d.T), np.kron(eye(4), d.T)):
        high, low = np_split(small)
        row = np.concatenate([high, high, low], axis=1)
        blocks.append(np.pad(row, ((0, 0), (0, NODES - row.shape[1]))))
    return np.concatenate(blocks, axis=0)


def dft_tables():
    a = np.arange(2048)[:, None]
    m = np.arange(LANES)[None, :]
    angle = 2.0 * np.pi * ((a * m) % 2048) / 2048.0
    table = np.concatenate([np.cos(angle), np.sin(angle)], axis=1)
    high, low = np_split(table)
    k = np.arange(16)[:, None]
    lane = np.arange(LANES)[None, :]
    turn = 2.0 * np.pi * ((k * lane) % 16) / 16.0
    phase = np.stack([np.cos(turn), -np.sin(turn)], axis=1) / math.sqrt(2048.0)
    return high, low, phase.astype(np.float32)


def split(x):
    high = x.astype(BF16)
    return high, (x - high.astype(F32)).astype(BF16)


def dot(a, b):
    return jnp.dot(a, b, preferred_element_type=F32)


def left_mul(table, x):
    high, low = split(x)
    return dot(table, jnp.concatenate([high, low, high], axis=0))


def right_mul(x, table):
    high, low = split(x)
    return dot(jnp.concatenate([high, low, high], axis=1), table)


def square(table, k):
    return table[k * NODES : (k + 1) * NODES, :]


def axial_left(table):
    return jnp.concatenate([square(table, 0), square(table, 0), square(table, 1)], axis=1)


def axial_left_t(table):
    return jnp.concatenate([square(table, 2), square(table, 2), square(table, 3)], axis=1)


def girth_right(table):
    return jnp.concatenate([square(table, 2), square(table, 2), square(table, 3)], axis=0)


def girth_right_t(table):
    return jnp.concatenate([square(table, 0), square(table, 0), square(table, 1)], axis=0)


SMALL = 4 * NODES


def ends_pair(table):
    return table[SMALL : SMALL + 64, :]


def radial_small(table):
    return table[SMALL + 64 : SMALL + 96, :96]


def radial_small_t(table):
    return table[SMALL + 96 : SMALL + 160, :192]


def radial_faces_t(table):
    return table[SMALL + 160 : SMALL + 192, :96]


def radial_apply(x, matrix):
    half = P_SIZE // 2
    odd_rows = 0.5 * (matrix[:half, :half] - matrix[:half, : half - 1 : -1])
    even_rows = 0.5 * (matrix[:half, :half] + matrix[:half, : half - 1 : -1])
    outs = {}
    for element in range(2):
        for part in range(2):
            for tile in range(x.shape[1] // LANES):
                nodes = []
                for i in range(P_SIZE):
                    row = (element * P_SIZE + i) * 16 + part * 8
                    nodes.append(x[row : row + 8, tile * LANES : (tile + 1) * LANES])
                even = [nodes[j] + nodes[P_SIZE - 1 - j] for j in range(half)]
                odd = [nodes[j] - nodes[P_SIZE - 1 - j] for j in range(half)]
                for i in range(half):
                    p = float(odd_rows[i, 0]) * odd[0]
                    q = float(even_rows[i, 0]) * even[0]
                    for j in range(1, half):
                        p = p + float(odd_rows[i, j]) * odd[j]
                        q = q + float(even_rows[i, j]) * even[j]
                    outs[element * P_SIZE + i, part, tile] = p + q
                    outs[element * P_SIZE + P_SIZE - 1 - i, part, tile] = p - q
    columns = []
    for tile in range(x.shape[1] // LANES):
        columns.append(
            jnp.concatenate([outs[i, part, tile] for i in range(16) for part in range(2)], axis=0)
        )
    return jnp.concatenate(columns, axis=1)


def end_columns(rows):
    d = derivative_table()
    values = [float(x) for x in np.concatenate([d[:, 0], d[:, 7]])]
    node = lax.broadcasted_iota(jnp.int32, (16, LANES), 0)
    column = jnp.full((16, LANES), values[0], F32)
    for k in range(1, 16):
        column = jnp.where(node == k, values[k], column)
    return jnp.broadcast_to(column[None], (16, 16, LANES)).reshape(rows, LANES)


def stiff_many(us, geoms, table):
    d = derivative_table()
    halves = [split(u) for u in us]
    rows = [jnp.concatenate([high, low, high], axis=1) for high, low in halves]
    girth = dot(jnp.concatenate(rows, axis=0), girth_right(table))
    girth = girth * jnp.concatenate([g[2] for g in geoms], axis=0)
    girth = right_mul(girth, girth_right_t(table))
    outs = []
    for k, (u, (high, low), (gr, ga, _)) in enumerate(zip(us, halves, geoms)):
        axial = dot(axial_left(table), jnp.concatenate([high, low, high], axis=0)) * ga
        radial = radial_apply(radial_apply(u, d) * gr, d.T)
        part = girth[k * NODES : (k + 1) * NODES]
        outs.append(left_mul(axial_left_t(table), axial) + part + radial)
    return outs


def left_pair(both, x):
    high, low = split(x)
    rows = both.shape[0] // 2
    first = dot(both, high)
    return first[:rows] + first[rows:] + dot(both[:rows], low)


def girth_faces(x, factor, repeat, table):
    rows = x.shape[0]
    stacked = jnp.concatenate([x[:, k * NODES : (k + 1) * NODES] for k in range(3)], axis=0)
    slope = right_mul(stacked, girth_right(table))
    scaled = []
    for k in range(3):
        part = slope[k * rows : (k + 1) * rows]
        part = jnp.concatenate([part] * repeat, axis=0)
        scaled.append(part * factor[:, k * NODES : (k + 1) * NODES])
    moved = right_mul(jnp.concatenate(scaled, axis=0), girth_right_t(table))
    rows = rows * repeat
    return jnp.concatenate([moved[k * rows : (k + 1) * rows] for k in range(3)], axis=1)


def twice(x):
    return jnp.concatenate([x, x], axis=1)


def sum_nodes(t):
    width = t.shape[1]
    v = t.reshape(16, 16, width)
    mid = v[7:8] + v[8:9]
    v = jnp.concatenate([v[:7], mid, mid, v[9:]], axis=0)
    pair = v[:, 7:8, :] + v[:, 8:9, :]
    node = lax.broadcasted_iota(jnp.int32, v.shape, 1)
    return jnp.where((node == 7) | (node == 8), pair, v)


def sum_girth(own, left, right, owners=None):
    lane = lax.broadcasted_iota(jnp.int32, left.shape, 1)
    first = lane % P_SIZE == 0
    last = lane % P_SIZE == P_SIZE - 1

    def inner(x):
        return jnp.where(
            first, pltpu.roll(x, 1, 1), jnp.where(last, pltpu.roll(x, LANES - 1, 1), 0.0)
        )

    sums = []
    for c, x in enumerate(own):
        p = inner(x)
        p = jnp.where(lane == 0, pltpu.roll(left, (LANES - HALO * c - HALO + 1) % LANES, 1), p)
        p = jnp.where(lane == LANES - 1, pltpu.roll(right, (LANES - 1 - HALO * c) % LANES, 1), p)
        sums.append(x + p)
    if owners is None:
        return sums
    p = inner(left)
    q = inner(right)
    for c, x in enumerate(owners):
        p = jnp.where(lane == HALO * c + HALO - 1, pltpu.roll(x, HALO * c + HALO - 1, 1), p)
        q = jnp.where(lane == HALO * c, pltpu.roll(x, (HALO * c + 1) % LANES, 1), q)
    return sums + [left + p, right + q]


def shared_local(parts):
    return jnp.concatenate(sum_girth(parts[:4], parts[4], parts[5], parts[:4]), axis=1)


def lanes_of(x, k):
    return x[:, k * LANES : (k + 1) * LANES]


def pack_kernel(field_in, geom_in, mass_in, to_right, to_left, field, geom, mass, sems):
    pairs = [(field_in.at[c], field.at[c]) for c in range(C)]
    pairs += [(geom_in.at[k], geom.at[k]) for k in range(3)] + [(mass_in, mass)]
    copies = [pltpu.make_async_copy(x, y, sems.at[k]) for k, (x, y) in enumerate(pairs)]
    for copy in copies:
        copy.start()
    lane = lax.broadcasted_iota(jnp.int32, (NODES, LANES), 1)

    def add(out, k, x, start):
        shift = (HALO * k - start) % LANES
        moved = pltpu.roll(x, shift, 1) if shift else x
        return moved if out is None else jnp.where(lane // HALO == k, moved, out)

    for group in range(2):
        right = left = None
        for k in range(4):
            copies[4 * group + k].wait()
            x = field[k] if group == 0 else (geom[k] if k < 3 else mass[...])
            right = add(right, k, x, LANES - HALO)
            left = add(left, k, x, 0)
        to_right[group] = right
        to_left[group] = left


def own_kernel(field, geom, table, out):
    geoms = tuple(twice(geom[k]) for k in range(3))
    us = [jnp.concatenate([field[2 * k], field[2 * k + 1]], axis=1) for k in range(2)]
    out[...] = jnp.concatenate(stiff_many(us, [geoms] * 2, table), axis=1)


def at_faces(low, high, width):
    shape = (16, 16, width)
    node = lax.broadcasted_iota(jnp.int32, shape, 1)
    both = jnp.where(
        node == 0, low[:, None, :], jnp.where(node == 15, high[:, None, :], 0.0)
    )
    return both.reshape(NODES, width)


def wide(x):
    own = lanes_of(x, 0)
    return jnp.concatenate([own] * C + [x[:, LANES:]], axis=1)


def put_faces(x, low, high, offset):
    width = x.shape[1]
    v = x.reshape(16, 16, width)
    low[:, offset : offset + width] = v[:, 0, :]
    high[:, offset : offset + width] = v[:, 15, :]


def action(u, geom, halo_geom, tables):
    own = tuple(twice(geom[k]) for k in range(3))
    geoms = [own, own, tuple(halo_geom[k] for k in range(3))]
    us = [u[:, k * NODES : (k + 1) * NODES] for k in range(3)]
    parts = []
    for t in stiff_many(us, geoms, tables):
        parts += [lanes_of(t, 0), lanes_of(t, 1)]
    return sum_nodes(shared_local(parts)).reshape(NODES, WIDE)


def inner_update(u, total, inverse):
    row = lax.broadcasted_iota(jnp.int32, u.shape, 0) % 16
    return jnp.where((row == 0) | (row == 15), u, u - total * wide(inverse))


def sum_faces(x):
    summed = shared_local([lanes_of(x, k) for k in range(6)]).reshape(2, 16, WIDE)
    pair = summed[:, 7:8, :] + summed[:, 8:9, :]
    node = lax.broadcasted_iota(jnp.int32, summed.shape, 1)
    return jnp.where((node == 7) | (node == 8), pair, summed)


def face_action(v, geom, halo_geom, statics, table):
    low, high = statics
    radial, girthwise = [
        wide(jnp.concatenate([static_part(low, k), static_part(high, k)], axis=0)) for k in (1, 2)
    ]
    nodes = v.reshape(16, 16, WIDE)
    ends = jnp.concatenate([nodes[:, 0, :], nodes[:, 15, :]], axis=0)
    face = left_mul(radial_faces_t(table), left_mul(radial_small(table), ends) * radial)
    face = face + girth_faces(ends, girthwise, 1, table)
    pieces = []
    for tile in range(3):
        ga = halo_geom[1] if tile == 2 else twice(geom[1])
        slope = left_pair(table[: 2 * NODES, :], v[:, tile * NODES : (tile + 1) * NODES]) * ga
        pieces.append(left_pair(ends_pair(table), slope))
    return sum_faces(face + jnp.concatenate(pieces, axis=1))


def two_steps(u, geom, halo_geom, inverse, first, statics, table, state, low, high):
    v = inner_update(u, first, inverse)
    state[...] = v
    put_faces(first, low, high, 0)
    faces = face_action(v, geom, halo_geom, statics, table)
    low[:, WIDE : 2 * WIDE] = faces[0]
    high[:, WIDE : 2 * WIDE] = faces[1]


def second_kernel(state, geom, halo_geom, table, out):
    out[...] = action(state[...], geom, halo_geom, table)


STATIC = 2 * WIDE
NARROW = 3 * LANES


def halo_kernel(
    left, right, own_total, field, mass, geom, tables, halo_geom, state, mass_out, ends_out, low, high
):
    lane = lax.broadcasted_iota(jnp.int32, (NODES, LANES), 1)

    def spread(x, k):
        y = jnp.where(lane // HALO == k, x, 0.0)
        y = y + pltpu.roll(y, HALO, 1)
        return y + pltpu.roll(y, 2 * HALO, 1)

    left_others, right_others = left[1], right[1]
    geoms = []
    for k in range(3):
        g = jnp.concatenate([spread(left_others, k), spread(right_others, k)], axis=1)
        halo_geom[k] = g
        geoms.append(g)
    u = jnp.concatenate([left[0], right[0]], axis=1)
    (t,) = stiff_many([u], [tuple(geoms)], tables)
    parts = [own_total[:, c * LANES : (c + 1) * LANES] for c in range(C)]
    first = sum_nodes(shared_local(parts + [lanes_of(t, 0), lanes_of(t, 1)]))
    first = first.reshape(NODES, WIDE)
    m = mass[...]
    masses = sum_girth([m], spread(left_others, 3), spread(right_others, 3), [m] * C)
    lumped = sum_nodes(jnp.concatenate(masses, axis=1)).reshape(NODES, NARROW)
    mass_out[...] = lumped
    whole = [jnp.concatenate([geom[k], geoms[k]], axis=1) for k in range(3)]
    end = end_columns(NODES)
    ends = left_mul(axial_left_t(tables), whole[1] * jnp.concatenate([end] * 3, axis=1))
    ends_out[...] = ends
    for k, x in enumerate([lumped, whole[0], whole[2], ends]):
        put_faces(x, low, high, STATIC + k * NARROW)
    start = jnp.concatenate([field[c] for c in range(C)] + [u], axis=1)
    two_steps(start, geom, halo_geom, 1.0 / lumped, first, (low, high), tables, state, low, high)


def static_part(ref, k):
    return ref[:, STATIC + k * NARROW : STATIC + (k + 1) * NARROW]


def finish_pair(state, second, inverse, ends, statics, own, got, tables, lanes=WIDE):
    low, high, got_low, got_high = statics
    own_low, own_high = own
    new_low, new_high = got
    w_low = -(own_low[:, :WIDE] + new_low[:, :WIDE]) * wide(
        1.0 / (static_part(low, 0) + static_part(got_low, 0))
    )
    w_high = -(own_high[:, :WIDE] + new_high[:, :WIDE]) * wide(
        1.0 / (static_part(high, 0) + static_part(got_high, 0))
    )
    w = jnp.concatenate([w_low, w_high], axis=0)
    radial, girthwise = [
        wide(jnp.concatenate([static_part(ref, k) for ref in statics], axis=0)) for k in (1, 2)
    ]
    slope = left_mul(radial_small(tables), w)
    face = left_mul(radial_small_t(tables), jnp.concatenate([slope, slope], axis=0) * radial)
    face = face + girth_faces(w, girthwise, 2, tables)
    other = jnp.concatenate([static_part(got_low, 3), static_part(got_high, 3)], axis=0)
    beyond = face[32:] + wide(other) * w
    beyond = sum_faces(beyond)
    beyond_low = beyond[0] + new_low[:, WIDE : 2 * WIDE]
    beyond_high = beyond[1] + new_high[:, WIDE : 2 * WIDE]
    node = lax.broadcasted_iota(jnp.int32, (16, 16, WIDE), 1)
    along = jnp.where(node < P_SIZE, w_low[:, None, :], w_high[:, None, :])
    change = wide(ends) * along.reshape(NODES, WIDE) + at_faces(face[:16], face[16:32], WIDE)
    parts = [lanes_of(change, k) for k in range(6)]
    owners = parts[:4] if lanes == WIDE else None
    summed = sum_girth(parts[:4], parts[4], parts[5], owners)
    change = sum_nodes(jnp.concatenate(summed, axis=1)).reshape(NODES, lanes)
    beyond = at_faces(beyond_low[:, :lanes], beyond_high[:, :lanes], lanes)
    total = second[:, :lanes] + change + beyond
    moved = state[:, :lanes] + at_faces(w_low[:, :lanes], w_high[:, :lanes], lanes)
    return moved - total * wide(inverse)[:, :lanes]


def middle_kernel(state, second, lumped, ends, low, high, got_low, got_high, geom, halo_geom, *refs):
    tables, state_out, inverse_out, next_low, next_high = refs
    inverse = 1.0 / (
        lumped[...] + at_faces(static_part(got_low, 0), static_part(got_high, 0), NARROW)
    )
    inverse_out[...] = inverse
    statics = (low, high, got_low, got_high)
    u = finish_pair(
        state[...], second[...], inverse, ends[...], statics, (low, high), (got_low, got_high), tables
    )
    first = action(u, geom, halo_geom, tables)
    two_steps(u, geom, halo_geom, inverse, first, (low, high), tables, state_out, next_low, next_high)


def last_kernel(
    state,
    second,
    inverse,
    ends,
    low,
    high,
    got_low,
    got_high,
    own_low,
    own_high,
    new_low,
    new_high,
    slab,
    girth_weight,
    select,
    header,
    tables,
    out,
    packed,
    probes_out,
):
    u = finish_pair(
        state[...],
        second[...],
        inverse[...],
        ends[...],
        (low, high, got_low, got_high),
        (own_low, own_high),
        (new_low, new_high),
        tables,
        C * LANES,
    )
    for c in range(C):
        out[c] = lanes_of(u, c)
    slab_high, slab_low = split(slab[...])
    values = left_pair(jnp.concatenate([slab_high, slab_low], axis=0), u)
    stacked = jnp.concatenate([lanes_of(values, c) for c in range(C)], axis=0)
    weight_high, weight_low = split(girth_weight[...])
    weights = jnp.concatenate([weight_high, weight_high, weight_low], axis=0)
    probes = right_mul(stacked, weights)
    slots = slab.shape[0]
    spread = jnp.concatenate([probes[c * slots : (c + 1) * slots] for c in range(C)], axis=1)
    probes_out[...] = spread
    high_part, low_part = split(spread)
    chosen = select[...].astype(BF16)
    rows = dot(
        jnp.concatenate([chosen, chosen], axis=1),
        jnp.concatenate([high_part, low_part], axis=0),
    )
    for c in range(C):
        block = lanes_of(rows, c).reshape(-1, SLOTS, LANES)
        if c == 0:
            place = lax.broadcasted_iota(jnp.int32, block.shape, 1)
            block = jnp.where(place == SLOTS - 1, header[...][:, None, :], block)
        packed[:, c * SLOTS : (c + 1) * SLOTS, :] = block


def weights_kernel(
    cycle_id, cycle_radial, cycle_axial, cycle_weights, az_elem, az_weights, slab, girth, select, header
):
    slots = cycle_id.shape[0]
    ids = cycle_id[...].reshape(1, slots)
    in_radial, in_axial = [x[...].reshape(1, slots) for x in (cycle_radial, cycle_axial)]
    radial, axial = [
        jnp.concatenate(
            [jnp.where(owner == e, cycle_weights[k], 0.0) for e in range(2)], axis=0
        )
        for k, owner in enumerate((in_radial, in_axial))
    ]
    slab[...] = jnp.transpose((radial[:, None, :] * axial[None, :, :]).reshape(NODES, slots))
    places = az_elem[...].reshape(1, 1, LANES)
    element = lax.broadcasted_iota(jnp.int32, (LANES // P_SIZE, P_SIZE, LANES), 0)
    girth[...] = jnp.where(element == places, az_weights[...][None], 0.0).reshape(LANES, LANES)
    used = ids >= 0
    target = jnp.where(used, lax.shift_right_logical(ids, 4), -1).astype(F32)
    across = jnp.broadcast_to(target, (slots, slots))
    down = jnp.transpose(across)
    before = lax.broadcasted_iota(jnp.int32, across.shape, 0) < lax.broadcasted_iota(
        jnp.int32, across.shape, 1
    )
    rank = jnp.sum(jnp.where((across == down) & before, 1.0, 0.0), axis=0, keepdims=True)
    position = jnp.where(used & (rank < SLOTS - 1.5), target * SLOTS + rank, -1.0)
    wanted = lax.broadcasted_iota(jnp.int32, select.shape, 0).astype(F32)
    select[...] = jnp.where(wanted == position, 1.0, 0.0)
    number = (ids & (ROWS_DEV - 1)).astype(F32) + 1.0
    owners = lax.broadcasted_iota(jnp.int32, (header.shape[0], slots), 0).astype(F32)
    named = jnp.where(owners == target, number, 0.0).astype(BF16)
    ranks = lax.broadcasted_iota(jnp.int32, (LANES, slots), 0).astype(F32)
    placed = jnp.where(ranks == rank, 1.0, 0.0).astype(BF16)
    numbers = lax.dot_general(
        named, placed, (((1,), (1,)), ((), ())), preferred_element_type=F32
    )
    overflow = jnp.max(jnp.where(used & (rank > SLOTS - 1.5), 1.0, 0.0), axis=1, keepdims=True)
    lane = lax.broadcasted_iota(jnp.int32, header.shape, 1)
    header[...] = jnp.where(
        lane >= SLOTS, overflow, jnp.where(lane < SLOTS - 1, numbers, 0.0)
    )


def unpack_kernel(pieces, out, crowded):
    sources = pieces.shape[0]
    heads = pieces[:, 0:SLOTS, :]
    head = jnp.broadcast_to(heads[:, SLOTS - 1 : SLOTS, :], heads.shape)
    place = lax.broadcasted_iota(jnp.int32, heads.shape, 1)
    lane = lax.broadcasted_iota(jnp.int32, heads.shape, 2)
    mine = jnp.where((lane == place) & (place < SLOTS - 1), head, 0.0)
    crowded[0, 0] = jnp.max(jnp.where(lane >= SLOTS, head, 0.0)).astype(jnp.int32)
    row = jnp.sum(mine.reshape(sources * SLOTS, LANES), axis=1, keepdims=True)
    column = lax.broadcasted_iota(jnp.int32, (sources * SLOTS, LANES), 1).astype(F32)
    chosen = jnp.transpose(jnp.where(row == column + 1.0, 1.0, 0.0))[:ROWS_DEV].astype(BF16)
    both = jnp.concatenate([chosen, chosen], axis=1)
    for c in range(C):
        x = pieces[:, c * SLOTS : (c + 1) * SLOTS, :].reshape(sources * SLOTS, LANES)
        high, low = split(x)
        out[c * ROWS_DEV : (c + 1) * ROWS_DEV, :] = dot(
            both, jnp.concatenate([high, low], axis=0)
        )


def dft_kernel(rows, phase, table_high, table_low, out):
    turn_re = phase[0:1, :]
    turn_im = phase[1:2, :]
    total = None
    for pair in range(8):
        x = jnp.concatenate([rows[2 * pair], rows[2 * pair + 1]], axis=1)
        z = jnp.concatenate([x * twice(turn_re), x * twice(turn_im)], axis=0)
        high, low = split(z)
        block = pl.ds(pair * 256, 256)
        th, tl = table_high[block, :], table_low[block, :]
        first = dot(jnp.concatenate([high, low], axis=0), th)
        half = first.shape[0] // 2
        part = first[:half] + first[half:] + dot(high, tl)
        total = part if total is None else total + part
    n = C * ROWS_DEV
    re = total[:n, :LANES] + total[n:, LANES:]
    im = total[n:, :LANES] - total[:n, LANES:]
    for c in range(C):
        out[0, :, c, :] = re[c * ROWS_DEV : (c + 1) * ROWS_DEV]
        out[1, :, c, :] = im[c * ROWS_DEV : (c + 1) * ROWS_DEV]


def call(kernel, shapes, flops, *args):
    vmem = pl.BlockSpec(memory_space=pltpu.VMEM)
    out_shape = [jax.ShapeDtypeStruct(s, F32) for s in shapes]
    return pl.pallas_call(
        kernel,
        out_shape=out_shape,
        in_specs=[vmem] * len(args),
        out_specs=[vmem] * len(shapes),
        compiler_params=pltpu.CompilerParams(vmem_limit_bytes=VMEM_LIMIT),
        cost_estimate=pl.CostEstimate(flops=flops, bytes_accessed=2000000, transcendentals=0),
    )(*args)


def pack_halos(*args):
    hbm, vmem = [pl.BlockSpec(memory_space=m) for m in (pltpu.HBM, pltpu.VMEM)]
    return pl.pallas_call(
        pack_kernel,
        out_shape=[jax.ShapeDtypeStruct((2, NODES, LANES), F32)] * 2,
        in_specs=[hbm] * len(args),
        out_specs=[vmem] * 2,
        scratch_shapes=[pltpu.VMEM(x.shape, F32) for x in args]
        + [pltpu.SemaphoreType.DMA((8,))],
        compiler_params=pltpu.CompilerParams(vmem_limit_bytes=LOAD_LIMIT),
    )(*args)


def body(
    field, geometry, mass, cycle_id, cycle_radial, cycle_axial, cycle_weights, az_elem, az_weights
):
    axial_count, girth_count = lax.axis_size("axial"), lax.axis_size("girth")
    up = [(i, i + 1) for i in range(axial_count - 1)]
    down = [(j, i) for i, j in up]
    around = [(i, (i + 1) % girth_count) for i in range(girth_count)]
    back = [(j, i) for i, j in around]
    field = field.reshape(C, NODES, LANES)
    geom = geometry.reshape(3, NODES, LANES)
    mass = mass.reshape(NODES, LANES)
    table = jnp.asarray(stiffness_table())
    to_right, to_left = pack_halos(field, geom, mass)
    tile_flops = 18 * 2 * 256**3

    left = lax.ppermute(to_right, "girth", around)
    right = lax.ppermute(to_left, "girth", back)
    (own_total,) = call(own_kernel, [(NODES, C * LANES)], 2 * tile_flops, field, geom, table)

    def exchange(low, high):
        return lax.ppermute(high, "axial", up), lax.ppermute(low, "axial", down)

    whole, narrow = (NODES, WIDE), (NODES, NARROW)
    face_static = (16, STATIC + 4 * NARROW)
    halo_geom, state, lumped, ends, low, high = call(
        halo_kernel,
        [(3, NODES, 2 * LANES), whole, narrow, narrow, face_static, face_static],
        2 * tile_flops,
        left,
        right,
        own_total,
        field,
        mass,
        geom,
        table,
    )
    got_low, got_high = exchange(low, high)
    (second,) = call(second_kernel, [whole], 3 * tile_flops, state, geom, halo_geom, table)
    state, inverse, own_low, own_high = call(
        middle_kernel,
        [whole, narrow, (16, STATIC), (16, STATIC)],
        4 * tile_flops,
        state,
        second,
        lumped,
        ends,
        low,
        high,
        got_low,
        got_high,
        geom,
        halo_geom,
        table,
    )
    new_low, new_high = exchange(own_low, own_high)
    (second,) = call(second_kernel, [whole], 3 * tile_flops, state, geom, halo_geom, table)

    slot_count = cycle_id.shape[0]
    slab, girth_weight, select, header = call(
        weights_kernel,
        [
            (slot_count, NODES),
            (LANES, LANES),
            (SLOTS * axial_count, slot_count),
            (axial_count, LANES),
        ],
        1000000,
        cycle_id,
        cycle_radial,
        cycle_axial,
        cycle_weights,
        az_elem,
        az_weights,
    )

    final, packed, probes = call(
        last_kernel,
        [(C, NODES, LANES), (axial_count, C * SLOTS, LANES), (slot_count, C * LANES)],
        tile_flops,
        state,
        second,
        inverse,
        ends,
        low,
        high,
        got_low,
        got_high,
        own_low,
        own_high,
        new_low,
        new_high,
        slab,
        girth_weight,
        select,
        header,
        table,
    )
    pieces = lax.all_to_all(packed, "axial", 0, 0)

    vmem = pl.BlockSpec(memory_space=pltpu.VMEM)
    rows, crowded = pl.pallas_call(
        unpack_kernel,
        out_shape=[
            jax.ShapeDtypeStruct((C * ROWS_DEV, LANES), F32),
            jax.ShapeDtypeStruct((1, 1), jnp.int32),
        ],
        in_specs=[vmem],
        out_specs=[vmem, pl.BlockSpec(memory_space=pltpu.SMEM)],
        compiler_params=pltpu.CompilerParams(vmem_limit_bytes=VMEM_LIMIT),
    )(pieces)

    def dense(rows, probes, cycle_id):
        wanted = jnp.arange(ROWS_DEV * axial_count, dtype=jnp.int32)
        chosen = (wanted[:, None] == cycle_id[None, :]).astype(F32)
        rows = jnp.dot(chosen, probes, precision=lax.Precision.HIGHEST)
        rows = rows.reshape(axial_count, ROWS_DEV, C * LANES)
        rows = jnp.sum(lax.all_to_all(rows, "axial", 0, 0), axis=0)
        return rows.reshape(ROWS_DEV, C, LANES).swapaxes(0, 1).reshape(C * ROWS_DEV, LANES)

    rows = lax.cond(
        crowded[0, 0] > 0, dense, lambda rows, *_: rows, rows, probes, cycle_id
    )
    rows = lax.all_gather(rows, "girth")
    table_high, table_low, phases = dft_tables()
    phase = lax.dynamic_index_in_dim(
        jnp.asarray(phases), lax.axis_index("girth"), 0, keepdims=False
    )
    (spectrum,) = call(
        dft_kernel,
        [(2, ROWS_DEV, C, LANES)],
        tile_flops,
        rows,
        phase,
        jnp.asarray(table_high),
        jnp.asarray(table_low),
    )
    return final.reshape(C, 16, 16, LANES), spectrum


def solution(mesh):
    return jax.shard_map(
        body,
        mesh=mesh,
        in_specs=(
            P(None, None, "axial", "girth"),
            P(None, None, "axial", "girth"),
            P(None, "axial", "girth"),
            P("axial"),
            P("axial"),
            P("axial"),
            P(None, None, "axial"),
            P("girth"),
            P(None, "girth"),
        ),
        out_specs=(P(None, None, "axial", "girth"), P(None, "axial", None, "girth")),
        check_vma=False,
    )
```

```python
import math

import jax
import jax.numpy as jnp
import ml_dtypes
import numpy as np
from jax import lax
from jax.experimental import pallas as pl
from jax.experimental.pallas import tpu as pltpu
from jax.sharding import PartitionSpec as P

C = 4
P_SIZE = 8
LANES = 128
HALO = 32
NODES = 256
WIDE = 6 * LANES
ROWS_DEV = 16
SLOTS = 8
VMEM_LIMIT = 32 * 1024 * 1024
LOAD_LIMIT = 60000000
F32 = jnp.float32
BF16 = jnp.bfloat16

LOBATTO = (
    -1.0,
    -0.8717401485096066,
    -0.5917001814331423,
    -0.2092992179024789,
    0.2092992179024789,
    0.5917001814331423,
    0.8717401485096066,
    1.0,
)


def derivative_table():
    node_count = len(LOBATTO)
    barycentric = []
    for row_index in range(node_count):
        product = 1.0
        for col_index in range(node_count):
            if col_index != row_index:
                product = product * (LOBATTO[row_index] - LOBATTO[col_index])
        barycentric.append(1.0 / product)
    table_rows = []
    for row_index in range(node_count):
        entries = []
        for col_index in range(node_count):
            if col_index != row_index:
                entries.append(
                    barycentric[col_index]
                    / barycentric[row_index]
                    / (LOBATTO[row_index] - LOBATTO[col_index])
                )
            else:
                entries.append(0.0)
        entries[row_index] = -sum(entries)
        table_rows.append(entries)
    return np.asarray(table_rows, np.float32)


def np_split(table):
    table = np.asarray(table, np.float32)
    high = table.astype(ml_dtypes.bfloat16)
    low = (table - high.astype(np.float32)).astype(ml_dtypes.bfloat16)
    return high, low


def stiffness_table():
    d = derivative_table()
    eye = lambda n: np.eye(n, dtype=np.float32)
    axial = np.kron(eye(32), d)
    blocks = list(np_split(axial)) + list(np_split(axial.T))
    ends = axial.T.reshape(16, 16, NODES)[:, [0, 15]].swapaxes(0, 1).reshape(32, NODES)
    blocks += list(np_split(ends))
    for small in (np.kron(eye(4), d), np.kron(eye(8), d.T), np.kron(eye(4), d.T)):
        high, low = np_split(small)
        row = np.concatenate([high, high, low], axis=1)
        blocks.append(np.pad(row, ((0, 0), (0, NODES - row.shape[1]))))
    return np.concatenate(blocks, axis=0)


def dft_tables():
    a = np.arange(2048)[:, None]
    m = np.arange(LANES)[None, :]
    angle = 2.0 * np.pi * ((a * m) % 2048) / 2048.0
    table = np.concatenate([np.cos(angle), np.sin(angle)], axis=1)
    high, low = np_split(table)
    k = np.arange(16)[:, None]
    lane = np.arange(LANES)[None, :]
    turn = 2.0 * np.pi * ((k * lane) % 16) / 16.0
    phase = np.stack([np.cos(turn), -np.sin(turn)], axis=1) / math.sqrt(2048.0)
    return high, low, phase.astype(np.float32)


def split(x):
    high = x.astype(BF16)
    return high, (x - high.astype(F32)).astype(BF16)


def dot(a, b):
    return jnp.dot(a, b, preferred_element_type=F32)


def left_mul(table, x):
    high, low = split(x)
    return dot(table, jnp.concatenate([high, low, high], axis=0))


def right_mul(x, table):
    high, low = split(x)
    return dot(jnp.concatenate([high, low, high], axis=1), table)


def square(table, k):
    return table[k * NODES : (k + 1) * NODES, :]


def axial_left(table):
    return jnp.concatenate([square(table, 0), square(table, 0), square(table, 1)], axis=1)


def axial_left_t(table):
    return jnp.concatenate([square(table, 2), square(table, 2), square(table, 3)], axis=1)


def girth_right(table):
    return jnp.concatenate([square(table, 2), square(table, 2), square(table, 3)], axis=0)


def girth_right_t(table):
    return jnp.concatenate([square(table, 0), square(table, 0), square(table, 1)], axis=0)


SMALL = 4 * NODES


def ends_pair(table):
    return table[SMALL : SMALL + 64, :]


def radial_small(table):
    return table[SMALL + 64 : SMALL + 96, :96]


def radial_small_t(table):
    return table[SMALL + 96 : SMALL + 160, :192]


def radial_faces_t(table):
    return table[SMALL + 160 : SMALL + 192, :96]


def radial_apply(x, matrix):
    half = P_SIZE // 2
    odd_rows = 0.5 * (matrix[:half, :half] - matrix[:half, : half - 1 : -1])
    even_rows = 0.5 * (matrix[:half, :half] + matrix[:half, : half - 1 : -1])
    outs = {}
    for element in range(2):
        for part in range(2):
            for tile in range(x.shape[1] // LANES):
                nodes = []
                for i in range(P_SIZE):
                    row = (element * P_SIZE + i) * 16 + part * 8
                    nodes.append(x[row : row + 8, tile * LANES : (tile + 1) * LANES])
                even = [nodes[j] + nodes[P_SIZE - 1 - j] for j in range(half)]
                odd = [nodes[j] - nodes[P_SIZE - 1 - j] for j in range(half)]
                for i in range(half):
                    p = float(odd_rows[i, 0]) * odd[0]
                    q = float(even_rows[i, 0]) * even[0]
                    for j in range(1, half):
                        p = p + float(odd_rows[i, j]) * odd[j]
                        q = q + float(even_rows[i, j]) * even[j]
                    outs[element * P_SIZE + i, part, tile] = p + q
                    outs[element * P_SIZE + P_SIZE - 1 - i, part, tile] = p - q
    columns = []
    for tile in range(x.shape[1] // LANES):
        columns.append(
            jnp.concatenate([outs[i, part, tile] for i in range(16) for part in range(2)], axis=0)
        )
    return jnp.concatenate(columns, axis=1)


def end_columns(rows):
    d = derivative_table()
    values = [float(x) for x in np.concatenate([d[:, 0], d[:, 7]])]
    node = lax.broadcasted_iota(jnp.int32, (16, LANES), 0)
    column = jnp.full((16, LANES), values[0], F32)
    for k in range(1, 16):
        column = jnp.where(node == k, values[k], column)
    return jnp.broadcast_to(column[None], (16, 16, LANES)).reshape(rows, LANES)


def stiff_many(us, geoms, table):
    d = derivative_table()
    halves = [split(u) for u in us]
    rows = [jnp.concatenate([high, low, high], axis=1) for high, low in halves]
    girth = dot(jnp.concatenate(rows, axis=0), girth_right(table))
    girth = girth * jnp.concatenate([g[2] for g in geoms], axis=0)
    girth = right_mul(girth, girth_right_t(table))
    outs = []
    for k, (u, (high, low), (gr, ga, _)) in enumerate(zip(us, halves, geoms)):
        axial = dot(axial_left(table), jnp.concatenate([high, low, high], axis=0)) * ga
        radial = radial_apply(radial_apply(u, d) * gr, d.T)
        part = girth[k * NODES : (k + 1) * NODES]
        outs.append(left_mul(axial_left_t(table), axial) + part + radial)
    return outs


def left_pair(both, x):
    high, low = split(x)
    rows = both.shape[0] // 2
    first = dot(both, high)
    return first[:rows] + first[rows:] + dot(both[:rows], low)


def girth_faces(x, factor, repeat, table):
    rows = x.shape[0]
    stacked = jnp.concatenate([x[:, k * NODES : (k + 1) * NODES] for k in range(3)], axis=0)
    slope = right_mul(stacked, girth_right(table))
    scaled = []
    for k in range(3):
        part = slope[k * rows : (k + 1) * rows]
        part = jnp.concatenate([part] * repeat, axis=0)
        scaled.append(part * factor[:, k * NODES : (k + 1) * NODES])
    moved = right_mul(jnp.concatenate(scaled, axis=0), girth_right_t(table))
    rows = rows * repeat
    return jnp.concatenate([moved[k * rows : (k + 1) * rows] for k in range(3)], axis=1)


def twice(x):
    return jnp.concatenate([x, x], axis=1)


def sum_nodes(t):
    width = t.shape[1]
    v = t.reshape(16, 16, width)
    mid = v[7:8] + v[8:9]
    v = jnp.concatenate([v[:7], mid, mid, v[9:]], axis=0)
    pair = v[:, 7:8, :] + v[:, 8:9, :]
    node = lax.broadcasted_iota(jnp.int32, v.shape, 1)
    return jnp.where((node == 7) | (node == 8), pair, v)


def sum_girth(own, left, right, owners=None):
    lane = lax.broadcasted_iota(jnp.int32, left.shape, 1)
    first = lane % P_SIZE == 0
    last = lane % P_SIZE == P_SIZE - 1

    def inner(x):
        return jnp.where(
            first, pltpu.roll(x, 1, 1), jnp.where(last, pltpu.roll(x, LANES - 1, 1), 0.0)
        )

    sums = []
    for c, x in enumerate(own):
        p = inner(x)
        p = jnp.where(lane == 0, pltpu.roll(left, (LANES - HALO * c - HALO + 1) % LANES, 1), p)
        p = jnp.where(lane == LANES - 1, pltpu.roll(right, (LANES - 1 - HALO * c) % LANES, 1), p)
        sums.append(x + p)
    if owners is None:
        return sums
    p = inner(left)
    q = inner(right)
    for c, x in enumerate(owners):
        p = jnp.where(lane == HALO * c + HALO - 1, pltpu.roll(x, HALO * c + HALO - 1, 1), p)
        q = jnp.where(lane == HALO * c, pltpu.roll(x, (HALO * c + 1) % LANES, 1), q)
    return sums + [left + p, right + q]


def shared_local(parts):
    return jnp.concatenate(sum_girth(parts[:4], parts[4], parts[5], parts[:4]), axis=1)


def lanes_of(x, k):
    return x[:, k * LANES : (k + 1) * LANES]


def pack_kernel(field_in, geom_in, mass_in, to_right, to_left, field, geom, mass, sems):
    copies = [
        pltpu.make_async_copy(field_in, field, sems.at[0]),
        pltpu.make_async_copy(geom_in, geom, sems.at[1]),
        pltpu.make_async_copy(mass_in, mass, sems.at[2]),
    ]
    for copy in copies:
        copy.start()
    lane = lax.broadcasted_iota(jnp.int32, (NODES, LANES), 1)

    def pack(arrays, start):
        out = None
        for k, x in enumerate(arrays):
            moved = pltpu.roll(x, (HALO * k - start) % LANES, 1) if (HALO * k - start) else x
            out = moved if out is None else jnp.where(lane // HALO == k, moved, out)
        return out

    copies[0].wait()
    fields = [field[c] for c in range(C)]
    to_right[0] = pack(fields, LANES - HALO)
    to_left[0] = pack(fields, 0)
    copies[1].wait()
    copies[2].wait()
    others = [geom[k] for k in range(3)] + [mass[...]]
    to_right[1] = pack(others, LANES - HALO)
    to_left[1] = pack(others, 0)


def own_kernel(field, geom, table, out):
    geoms = tuple(twice(geom[k]) for k in range(3))
    us = [jnp.concatenate([field[2 * k], field[2 * k + 1]], axis=1) for k in range(2)]
    out[...] = jnp.concatenate(stiff_many(us, [geoms] * 2, table), axis=1)


def at_faces(low, high, width):
    shape = (16, 16, width)
    node = lax.broadcasted_iota(jnp.int32, shape, 1)
    both = jnp.where(
        node == 0, low[:, None, :], jnp.where(node == 15, high[:, None, :], 0.0)
    )
    return both.reshape(NODES, width)


def wide(x):
    own = lanes_of(x, 0)
    return jnp.concatenate([own] * C + [x[:, LANES:]], axis=1)


def put_faces(x, low, high, offset):
    width = x.shape[1]
    v = x.reshape(16, 16, width)
    low[:, offset : offset + width] = v[:, 0, :]
    high[:, offset : offset + width] = v[:, 15, :]


def action(u, geom, halo_geom, tables):
    own = tuple(twice(geom[k]) for k in range(3))
    geoms = [own, own, tuple(halo_geom[k] for k in range(3))]
    us = [u[:, k * NODES : (k + 1) * NODES] for k in range(3)]
    parts = []
    for t in stiff_many(us, geoms, tables):
        parts += [lanes_of(t, 0), lanes_of(t, 1)]
    return sum_nodes(shared_local(parts)).reshape(NODES, WIDE)


def inner_update(u, total, inverse):
    row = lax.broadcasted_iota(jnp.int32, u.shape, 0) % 16
    return jnp.where((row == 0) | (row == 15), u, u - total * wide(inverse))


def sum_faces(x):
    summed = shared_local([lanes_of(x, k) for k in range(6)]).reshape(2, 16, WIDE)
    pair = summed[:, 7:8, :] + summed[:, 8:9, :]
    node = lax.broadcasted_iota(jnp.int32, summed.shape, 1)
    return jnp.where((node == 7) | (node == 8), pair, summed)


def face_action(v, geom, halo_geom, statics, table):
    low, high = statics
    radial, girthwise = [
        wide(jnp.concatenate([static_part(low, k), static_part(high, k)], axis=0)) for k in (1, 2)
    ]
    nodes = v.reshape(16, 16, WIDE)
    ends = jnp.concatenate([nodes[:, 0, :], nodes[:, 15, :]], axis=0)
    face = left_mul(radial_faces_t(table), left_mul(radial_small(table), ends) * radial)
    face = face + girth_faces(ends, girthwise, 1, table)
    pieces = []
    for tile in range(3):
        ga = halo_geom[1] if tile == 2 else twice(geom[1])
        slope = left_pair(table[: 2 * NODES, :], v[:, tile * NODES : (tile + 1) * NODES]) * ga
        pieces.append(left_pair(ends_pair(table), slope))
    return sum_faces(face + jnp.concatenate(pieces, axis=1))


def two_steps(u, geom, halo_geom, inverse, first, statics, table, state, low, high):
    v = inner_update(u, first, inverse)
    state[...] = v
    put_faces(first, low, high, 0)
    faces = face_action(v, geom, halo_geom, statics, table)
    low[:, WIDE : 2 * WIDE] = faces[0]
    high[:, WIDE : 2 * WIDE] = faces[1]


def second_kernel(state, geom, halo_geom, table, out):
    out[...] = action(state[...], geom, halo_geom, table)


STATIC = 2 * WIDE
NARROW = 3 * LANES


def spread(x, k):
    lane = lax.broadcasted_iota(jnp.int32, x.shape, 1)
    y = jnp.where(lane // HALO == k, x, 0.0)
    y = y + pltpu.roll(y, HALO, 1)
    return y + pltpu.roll(y, 2 * HALO, 1)


def to_send(face, out):
    out[:, :STATIC] = face[:, :STATIC]
    lane = lax.broadcasted_iota(jnp.int32, (16, LANES), 1) // HALO
    for k in range(4):
        out[:, STATIC + k * LANES : STATIC + (k + 1) * LANES] = static_part(face, k)[:, :LANES]
    for k in range(2):
        parts = []
        for j in (2 * k, 2 * k + 1):
            parts += [static_part(face, j)[:, LANES : 2 * LANES], static_part(face, j)[:, 2 * LANES :]]
        block = parts[3]
        for j in range(3):
            block = jnp.where(lane == j, parts[j], block)
        out[:, STATIC + (4 + k) * LANES : STATIC + (5 + k) * LANES] = block


def as_sent(got):
    pieces = [got[:, :STATIC]]
    for k in range(4):
        halos = got[:, STATIC + (4 + k // 2) * LANES : STATIC + (5 + k // 2) * LANES]
        place = 2 * (k % 2)
        pieces.append(got[:, STATIC + k * LANES : STATIC + (k + 1) * LANES])
        pieces += [spread(halos, place), spread(halos, place + 1)]
    return jnp.concatenate(pieces, axis=1)


def halo_kernel(
    left, right, own_total, field, mass, geom, tables, halo_geom, state, mass_out, ends_out, low, high, *sent
):
    left_others, right_others = left[1], right[1]
    geoms = []
    for k in range(3):
        g = jnp.concatenate([spread(left_others, k), spread(right_others, k)], axis=1)
        halo_geom[k] = g
        geoms.append(g)
    u = jnp.concatenate([left[0], right[0]], axis=1)
    (t,) = stiff_many([u], [tuple(geoms)], tables)
    parts = [own_total[:, c * LANES : (c + 1) * LANES] for c in range(C)]
    first = sum_nodes(shared_local(parts + [lanes_of(t, 0), lanes_of(t, 1)]))
    first = first.reshape(NODES, WIDE)
    m = mass[...]
    masses = sum_girth([m], spread(left_others, 3), spread(right_others, 3), [m] * C)
    lumped = sum_nodes(jnp.concatenate(masses, axis=1)).reshape(NODES, NARROW)
    mass_out[...] = lumped
    whole = [jnp.concatenate([geom[k], geoms[k]], axis=1) for k in range(3)]
    end = end_columns(NODES)
    ends = left_mul(axial_left_t(tables), whole[1] * jnp.concatenate([end] * 3, axis=1))
    ends_out[...] = ends
    for k, x in enumerate([lumped, whole[0], whole[2], ends]):
        put_faces(x, low, high, STATIC + k * NARROW)
    start = jnp.concatenate([field[c] for c in range(C)] + [u], axis=1)
    two_steps(start, geom, halo_geom, 1.0 / lumped, first, (low, high), tables, state, low, high)
    to_send(low, sent[0])
    to_send(high, sent[1])


def static_part(ref, k):
    return ref[:, STATIC + k * NARROW : STATIC + (k + 1) * NARROW]


def finish_pair(state, second, inverse, ends, statics, own, got, tables, lanes=WIDE):
    low, high, got_low, got_high = statics
    own_low, own_high = own
    new_low, new_high = got
    w_low = -(own_low[:, :WIDE] + new_low[:, :WIDE]) * wide(
        1.0 / (static_part(low, 0) + static_part(got_low, 0))
    )
    w_high = -(own_high[:, :WIDE] + new_high[:, :WIDE]) * wide(
        1.0 / (static_part(high, 0) + static_part(got_high, 0))
    )
    w = jnp.concatenate([w_low, w_high], axis=0)
    radial, girthwise = [
        wide(jnp.concatenate([static_part(ref, k) for ref in statics], axis=0)) for k in (1, 2)
    ]
    slope = left_mul(radial_small(tables), w)
    face = left_mul(radial_small_t(tables), jnp.concatenate([slope, slope], axis=0) * radial)
    face = face + girth_faces(w, girthwise, 2, tables)
    other = jnp.concatenate([static_part(got_low, 3), static_part(got_high, 3)], axis=0)
    beyond = face[32:] + wide(other) * w
    beyond = sum_faces(beyond)
    beyond_low = beyond[0] + new_low[:, WIDE : 2 * WIDE]
    beyond_high = beyond[1] + new_high[:, WIDE : 2 * WIDE]
    node = lax.broadcasted_iota(jnp.int32, (16, 16, WIDE), 1)
    along = jnp.where(node < P_SIZE, w_low[:, None, :], w_high[:, None, :])
    change = wide(ends) * along.reshape(NODES, WIDE) + at_faces(face[:16], face[16:32], WIDE)
    parts = [lanes_of(change, k) for k in range(6)]
    owners = parts[:4] if lanes == WIDE else None
    summed = sum_girth(parts[:4], parts[4], parts[5], owners)
    change = sum_nodes(jnp.concatenate(summed, axis=1)).reshape(NODES, lanes)
    beyond = at_faces(beyond_low[:, :lanes], beyond_high[:, :lanes], lanes)
    total = second[:, :lanes] + change + beyond
    moved = state[:, :lanes] + at_faces(w_low[:, :lanes], w_high[:, :lanes], lanes)
    return moved - total * wide(inverse)[:, :lanes]


def middle_kernel(state, second, lumped, ends, low, high, got_low, got_high, geom, halo_geom, *refs):
    tables, state_out, inverse_out, next_low, next_high = refs
    got_low, got_high = as_sent(got_low), as_sent(got_high)
    inverse = 1.0 / (
        lumped[...] + at_faces(static_part(got_low, 0), static_part(got_high, 0), NARROW)
    )
    inverse_out[...] = inverse
    statics = (low, high, got_low, got_high)
    u = finish_pair(
        state[...], second[...], inverse, ends[...], statics, (low, high), (got_low, got_high), tables
    )
    first = action(u, geom, halo_geom, tables)
    two_steps(u, geom, halo_geom, inverse, first, (low, high), tables, state_out, next_low, next_high)


def last_kernel(
    state,
    second,
    inverse,
    ends,
    low,
    high,
    got_low,
    got_high,
    own_low,
    own_high,
    new_low,
    new_high,
    slab,
    girth_weight,
    select,
    header,
    tables,
    out,
    packed,
    probes_out,
):
    u = finish_pair(
        state[...],
        second[...],
        inverse[...],
        ends[...],
        (low, high, as_sent(got_low), as_sent(got_high)),
        (own_low, own_high),
        (new_low, new_high),
        tables,
        C * LANES,
    )
    for c in range(C):
        out[c] = lanes_of(u, c)
    slab_high, slab_low = split(slab[...])
    values = left_pair(jnp.concatenate([slab_high, slab_low], axis=0), u)
    stacked = jnp.concatenate([lanes_of(values, c) for c in range(C)], axis=0)
    weight_high, weight_low = split(girth_weight[...])
    weights = jnp.concatenate([weight_high, weight_high, weight_low], axis=0)
    probes = right_mul(stacked, weights)
    slots = slab.shape[0]
    spread = jnp.concatenate([probes[c * slots : (c + 1) * slots] for c in range(C)], axis=1)
    probes_out[...] = spread
    high_part, low_part = split(spread)
    chosen = select[...].astype(BF16)
    rows = dot(
        jnp.concatenate([chosen, chosen], axis=1),
        jnp.concatenate([high_part, low_part], axis=0),
    )
    for c in range(C):
        block = lanes_of(rows, c).reshape(-1, SLOTS, LANES)
        if c == 0:
            place = lax.broadcasted_iota(jnp.int32, block.shape, 1)
            block = jnp.where(place == SLOTS - 1, header[...][:, None, :], block)
        packed[:, c * SLOTS : (c + 1) * SLOTS, :] = block


def weights_kernel(
    cycle_id, cycle_radial, cycle_axial, cycle_weights, az_elem, az_weights, slab, girth, select, header
):
    slots = cycle_id.shape[0]
    ids = cycle_id[...].reshape(1, slots)
    in_radial, in_axial = [x[...].reshape(1, slots) for x in (cycle_radial, cycle_axial)]
    radial, axial = [
        jnp.concatenate(
            [jnp.where(owner == e, cycle_weights[k], 0.0) for e in range(2)], axis=0
        )
        for k, owner in enumerate((in_radial, in_axial))
    ]
    slab[...] = jnp.transpose((radial[:, None, :] * axial[None, :, :]).reshape(NODES, slots))
    places = az_elem[...].reshape(1, 1, LANES)
    element = lax.broadcasted_iota(jnp.int32, (LANES // P_SIZE, P_SIZE, LANES), 0)
    girth[...] = jnp.where(element == places, az_weights[...][None], 0.0).reshape(LANES, LANES)
    used = ids >= 0
    target = jnp.where(used, lax.shift_right_logical(ids, 4), -1).astype(F32)
    across = jnp.broadcast_to(target, (slots, slots))
    down = jnp.transpose(across)
    before = lax.broadcasted_iota(jnp.int32, across.shape, 0) < lax.broadcasted_iota(
        jnp.int32, across.shape, 1
    )
    rank = jnp.sum(jnp.where((across == down) & before, 1.0, 0.0), axis=0, keepdims=True)
    position = jnp.where(used & (rank < SLOTS - 1.5), target * SLOTS + rank, -1.0)
    wanted = lax.broadcasted_iota(jnp.int32, select.shape, 0).astype(F32)
    select[...] = jnp.where(wanted == position, 1.0, 0.0)
    number = (ids & (ROWS_DEV - 1)).astype(F32) + 1.0
    owners = lax.broadcasted_iota(jnp.int32, (header.shape[0], slots), 0).astype(F32)
    named = jnp.where(owners == target, number, 0.0).astype(BF16)
    ranks = lax.broadcasted_iota(jnp.int32, (LANES, slots), 0).astype(F32)
    placed = jnp.where(ranks == rank, 1.0, 0.0).astype(BF16)
    numbers = lax.dot_general(
        named, placed, (((1,), (1,)), ((), ())), preferred_element_type=F32
    )
    overflow = jnp.max(jnp.where(used & (rank > SLOTS - 1.5), 1.0, 0.0), axis=1, keepdims=True)
    lane = lax.broadcasted_iota(jnp.int32, header.shape, 1)
    header[...] = jnp.where(
        lane >= SLOTS, overflow, jnp.where(lane < SLOTS - 1, numbers, 0.0)
    )


def unpack_kernel(pieces, out, crowded):
    sources = pieces.shape[0]
    heads = pieces[:, 0:SLOTS, :]
    head = jnp.broadcast_to(heads[:, SLOTS - 1 : SLOTS, :], heads.shape)
    place = lax.broadcasted_iota(jnp.int32, heads.shape, 1)
    lane = lax.broadcasted_iota(jnp.int32, heads.shape, 2)
    mine = jnp.where((lane == place) & (place < SLOTS - 1), head, 0.0)
    crowded[0, 0] = jnp.max(jnp.where(lane >= SLOTS, head, 0.0)).astype(jnp.int32)
    row = jnp.sum(mine.reshape(sources * SLOTS, LANES), axis=1, keepdims=True)
    column = lax.broadcasted_iota(jnp.int32, (sources * SLOTS, LANES), 1).astype(F32)
    chosen = jnp.transpose(jnp.where(row == column + 1.0, 1.0, 0.0))[:ROWS_DEV].astype(BF16)
    both = jnp.concatenate([chosen, chosen], axis=1)
    for c in range(C):
        x = pieces[:, c * SLOTS : (c + 1) * SLOTS, :].reshape(sources * SLOTS, LANES)
        high, low = split(x)
        out[c * ROWS_DEV : (c + 1) * ROWS_DEV, :] = dot(
            both, jnp.concatenate([high, low], axis=0)
        )


def dft_kernel(rows, phase, table_high, table_low, out):
    turn_re = phase[0:1, :]
    turn_im = phase[1:2, :]
    total = None
    for pair in range(8):
        x = jnp.concatenate([rows[2 * pair], rows[2 * pair + 1]], axis=1)
        z = jnp.concatenate([x * twice(turn_re), x * twice(turn_im)], axis=0)
        high, low = split(z)
        block = pl.ds(pair * 256, 256)
        th, tl = table_high[block, :], table_low[block, :]
        first = dot(jnp.concatenate([high, low], axis=0), th)
        half = first.shape[0] // 2
        part = first[:half] + first[half:] + dot(high, tl)
        total = part if total is None else total + part
    n = C * ROWS_DEV
    re = total[:n, :LANES] + total[n:, LANES:]
    im = total[n:, :LANES] - total[:n, LANES:]
    for c in range(C):
        out[0, :, c, :] = re[c * ROWS_DEV : (c + 1) * ROWS_DEV]
        out[1, :, c, :] = im[c * ROWS_DEV : (c + 1) * ROWS_DEV]


def call(kernel, shapes, flops, *args):
    vmem = pl.BlockSpec(memory_space=pltpu.VMEM)
    out_shape = [jax.ShapeDtypeStruct(s, F32) for s in shapes]
    return pl.pallas_call(
        kernel,
        out_shape=out_shape,
        in_specs=[vmem] * len(args),
        out_specs=[vmem] * len(shapes),
        compiler_params=pltpu.CompilerParams(vmem_limit_bytes=VMEM_LIMIT),
        cost_estimate=pl.CostEstimate(flops=flops, bytes_accessed=2000000, transcendentals=0),
    )(*args)


def pack_halos(*args):
    hbm, vmem = [pl.BlockSpec(memory_space=m) for m in (pltpu.HBM, pltpu.VMEM)]
    return pl.pallas_call(
        pack_kernel,
        out_shape=[jax.ShapeDtypeStruct((2, NODES, LANES), F32)] * 2,
        in_specs=[hbm] * len(args),
        out_specs=[vmem] * 2,
        scratch_shapes=[pltpu.VMEM(x.shape, F32) for x in args]
        + [pltpu.SemaphoreType.DMA((len(args),))],
        compiler_params=pltpu.CompilerParams(vmem_limit_bytes=LOAD_LIMIT),
    )(*args)


def body(
    field, geometry, mass, cycle_id, cycle_radial, cycle_axial, cycle_weights, az_elem, az_weights
):
    axial_count, girth_count = lax.axis_size("axial"), lax.axis_size("girth")
    up = [(i, i + 1) for i in range(axial_count - 1)]
    down = [(j, i) for i, j in up]
    around = [(i, (i + 1) % girth_count) for i in range(girth_count)]
    back = [(j, i) for i, j in around]
    field = field.reshape(C, NODES, LANES)
    geom = geometry.reshape(3, NODES, LANES)
    mass = mass.reshape(NODES, LANES)
    table = jnp.asarray(stiffness_table())
    to_right, to_left = pack_halos(field, geom, mass)
    tile_flops = 18 * 2 * 256**3

    left = lax.ppermute(to_right, "girth", around)
    right = lax.ppermute(to_left, "girth", back)
    (own_total,) = call(own_kernel, [(NODES, C * LANES)], 2 * tile_flops, field, geom, table)

    def exchange(low, high):
        return lax.ppermute(high, "axial", up), lax.ppermute(low, "axial", down)

    whole, narrow = (NODES, WIDE), (NODES, NARROW)
    face_static, sent = (16, STATIC + 4 * NARROW), (16, STATIC + 6 * LANES)
    halo_geom, state, lumped, ends, low, high, send_low, send_high = call(
        halo_kernel,
        [(3, NODES, 2 * LANES), whole, narrow, narrow, face_static, face_static, sent, sent],
        2 * tile_flops,
        left,
        right,
        own_total,
        field,
        mass,
        geom,
        table,
    )
    got_low, got_high = exchange(send_low, send_high)
    (second,) = call(second_kernel, [whole], 3 * tile_flops, state, geom, halo_geom, table)
    state, inverse, own_low, own_high = call(
        middle_kernel,
        [whole, narrow, (16, STATIC), (16, STATIC)],
        4 * tile_flops,
        state,
        second,
        lumped,
        ends,
        low,
        high,
        got_low,
        got_high,
        geom,
        halo_geom,
        table,
    )
    new_low, new_high = exchange(own_low, own_high)
    (second,) = call(second_kernel, [whole], 3 * tile_flops, state, geom, halo_geom, table)

    slot_count = cycle_id.shape[0]
    slab, girth_weight, select, header = call(
        weights_kernel,
        [
            (slot_count, NODES),
            (LANES, LANES),
            (SLOTS * axial_count, slot_count),
            (axial_count, LANES),
        ],
        1000000,
        cycle_id,
        cycle_radial,
        cycle_axial,
        cycle_weights,
        az_elem,
        az_weights,
    )

    final, packed, probes = call(
        last_kernel,
        [(C, NODES, LANES), (axial_count, C * SLOTS, LANES), (slot_count, C * LANES)],
        tile_flops,
        state,
        second,
        inverse,
        ends,
        low,
        high,
        got_low,
        got_high,
        own_low,
        own_high,
        new_low,
        new_high,
        slab,
        girth_weight,
        select,
        header,
        table,
    )
    pieces = lax.all_to_all(packed, "axial", 0, 0)

    vmem = pl.BlockSpec(memory_space=pltpu.VMEM)
    rows, crowded = pl.pallas_call(
        unpack_kernel,
        out_shape=[
            jax.ShapeDtypeStruct((C * ROWS_DEV, LANES), F32),
            jax.ShapeDtypeStruct((1, 1), jnp.int32),
        ],
        in_specs=[vmem],
        out_specs=[vmem, pl.BlockSpec(memory_space=pltpu.SMEM)],
        compiler_params=pltpu.CompilerParams(vmem_limit_bytes=VMEM_LIMIT),
    )(pieces)

    def dense(rows, probes, cycle_id):
        wanted = jnp.arange(ROWS_DEV * axial_count, dtype=jnp.int32)
        chosen = (wanted[:, None] == cycle_id[None, :]).astype(F32)
        rows = jnp.dot(chosen, probes, precision=lax.Precision.HIGHEST)
        rows = rows.reshape(axial_count, ROWS_DEV, C * LANES)
        rows = jnp.sum(lax.all_to_all(rows, "axial", 0, 0), axis=0)
        return rows.reshape(ROWS_DEV, C, LANES).swapaxes(0, 1).reshape(C * ROWS_DEV, LANES)

    rows = lax.cond(
        crowded[0, 0] > 0, dense, lambda rows, *_: rows, rows, probes, cycle_id
    )
    rows = lax.all_gather(rows, "girth")
    table_high, table_low, phases = dft_tables()
    phase = lax.dynamic_index_in_dim(
        jnp.asarray(phases), lax.axis_index("girth"), 0, keepdims=False
    )
    (spectrum,) = call(
        dft_kernel,
        [(2, ROWS_DEV, C, LANES)],
        tile_flops,
        rows,
        phase,
        jnp.asarray(table_high),
        jnp.asarray(table_low),
    )
    return final.reshape(C, 16, 16, LANES), spectrum


def solution(mesh):
    return jax.shard_map(
        body,
        mesh=mesh,
        in_specs=(
            P(None, None, "axial", "girth"),
            P(None, None, "axial", "girth"),
            P(None, "axial", "girth"),
            P("axial"),
            P("axial"),
            P("axial"),
            P(None, None, "axial"),
            P("girth"),
            P(None, "girth"),
        ),
        out_specs=(P(None, None, "axial", "girth"), P(None, "axial", None, "girth")),
        check_vma=False,
    )
```

```python
import math

import jax
import jax.numpy as jnp
import ml_dtypes
import numpy as np
from jax import lax
from jax.experimental import pallas as pl
from jax.experimental.pallas import tpu as pltpu
from jax.sharding import PartitionSpec as P

C = 4
P_SIZE = 8
LANES = 128
HALO = 32
NODES = 256
WIDE = 6 * LANES
ROWS_DEV = 16
SLOTS = 8
VMEM_LIMIT = 32 * 1024 * 1024
LOAD_LIMIT = 60000000
F32 = jnp.float32
BF16 = jnp.bfloat16

LOBATTO = (
    -1.0,
    -0.8717401485096066,
    -0.5917001814331423,
    -0.2092992179024789,
    0.2092992179024789,
    0.5917001814331423,
    0.8717401485096066,
    1.0,
)


def derivative_table():
    node_count = len(LOBATTO)
    barycentric = []
    for row_index in range(node_count):
        product = 1.0
        for col_index in range(node_count):
            if col_index != row_index:
                product = product * (LOBATTO[row_index] - LOBATTO[col_index])
        barycentric.append(1.0 / product)
    table_rows = []
    for row_index in range(node_count):
        entries = []
        for col_index in range(node_count):
            if col_index != row_index:
                entries.append(
                    barycentric[col_index]
                    / barycentric[row_index]
                    / (LOBATTO[row_index] - LOBATTO[col_index])
                )
            else:
                entries.append(0.0)
        entries[row_index] = -sum(entries)
        table_rows.append(entries)
    return np.asarray(table_rows, np.float32)


def np_split(table):
    table = np.asarray(table, np.float32)
    high = table.astype(ml_dtypes.bfloat16)
    low = (table - high.astype(np.float32)).astype(ml_dtypes.bfloat16)
    return high, low


def stiffness_table():
    d = derivative_table()
    eye = lambda n: np.eye(n, dtype=np.float32)
    axial = np.kron(eye(32), d)
    blocks = list(np_split(axial)) + list(np_split(axial.T))
    ends = axial.T.reshape(16, 16, NODES)[:, [0, 15]].swapaxes(0, 1).reshape(32, NODES)
    blocks += list(np_split(ends))
    for small in (np.kron(eye(4), d), np.kron(eye(8), d.T), np.kron(eye(4), d.T)):
        high, low = np_split(small)
        row = np.concatenate([high, high, low], axis=1)
        blocks.append(np.pad(row, ((0, 0), (0, NODES - row.shape[1]))))
    return np.concatenate(blocks, axis=0)


def dft_tables():
    a = np.arange(2048)[:, None]
    m = np.arange(LANES)[None, :]
    angle = 2.0 * np.pi * ((a * m) % 2048) / 2048.0
    table = np.concatenate([np.cos(angle), np.sin(angle)], axis=1)
    high, low = np_split(table)
    k = np.arange(16)[:, None]
    lane = np.arange(LANES)[None, :]
    turn = 2.0 * np.pi * ((k * lane) % 16) / 16.0
    phase = np.stack([np.cos(turn), -np.sin(turn)], axis=1) / math.sqrt(2048.0)
    return high, low, phase.astype(np.float32)


def split(x):
    high = x.astype(BF16)
    return high, (x - high.astype(F32)).astype(BF16)


def dot(a, b):
    return jnp.dot(a, b, preferred_element_type=F32)


def left_mul(table, x):
    high, low = split(x)
    return dot(table, jnp.concatenate([high, low, high], axis=0))


def right_mul(x, table):
    high, low = split(x)
    return dot(jnp.concatenate([high, low, high], axis=1), table)


def square(table, k):
    return table[k * NODES : (k + 1) * NODES, :]


def axial_left(table):
    return jnp.concatenate([square(table, 0), square(table, 0), square(table, 1)], axis=1)


def axial_left_t(table):
    return jnp.concatenate([square(table, 2), square(table, 2), square(table, 3)], axis=1)


def girth_right(table):
    return jnp.concatenate([square(table, 2), square(table, 2), square(table, 3)], axis=0)


def girth_right_t(table):
    return jnp.concatenate([square(table, 0), square(table, 0), square(table, 1)], axis=0)


SMALL = 4 * NODES


def ends_pair(table):
    return table[SMALL : SMALL + 64, :]


def radial_small(table):
    return table[SMALL + 64 : SMALL + 96, :96]


def radial_small_t(table):
    return table[SMALL + 96 : SMALL + 160, :192]


def radial_faces_t(table):
    return table[SMALL + 160 : SMALL + 192, :96]


def radial_apply(x, matrix):
    half = P_SIZE // 2
    odd_rows = 0.5 * (matrix[:half, :half] - matrix[:half, : half - 1 : -1])
    even_rows = 0.5 * (matrix[:half, :half] + matrix[:half, : half - 1 : -1])
    outs = {}
    for element in range(2):
        for part in range(2):
            for tile in range(x.shape[1] // LANES):
                nodes = []
                for i in range(P_SIZE):
                    row = (element * P_SIZE + i) * 16 + part * 8
                    nodes.append(x[row : row + 8, tile * LANES : (tile + 1) * LANES])
                even = [nodes[j] + nodes[P_SIZE - 1 - j] for j in range(half)]
                odd = [nodes[j] - nodes[P_SIZE - 1 - j] for j in range(half)]
                for i in range(half):
                    p = float(odd_rows[i, 0]) * odd[0]
                    q = float(even_rows[i, 0]) * even[0]
                    for j in range(1, half):
                        p = p + float(odd_rows[i, j]) * odd[j]
                        q = q + float(even_rows[i, j]) * even[j]
                    outs[element * P_SIZE + i, part, tile] = p + q
                    outs[element * P_SIZE + P_SIZE - 1 - i, part, tile] = p - q
    columns = []
    for tile in range(x.shape[1] // LANES):
        columns.append(
            jnp.concatenate([outs[i, part, tile] for i in range(16) for part in range(2)], axis=0)
        )
    return jnp.concatenate(columns, axis=1)


def end_columns(rows):
    d = derivative_table()
    values = [float(x) for x in np.concatenate([d[:, 0], d[:, 7]])]
    node = lax.broadcasted_iota(jnp.int32, (16, LANES), 0)
    column = jnp.full((16, LANES), values[0], F32)
    for k in range(1, 16):
        column = jnp.where(node == k, values[k], column)
    return jnp.broadcast_to(column[None], (16, 16, LANES)).reshape(rows, LANES)


def axial_apply(x, matrix):
    v = x.reshape(-1, P_SIZE, x.shape[1])
    node = lax.broadcasted_iota(jnp.int32, (P_SIZE, x.shape[1]), 0)
    out = None
    for k in range(P_SIZE):
        values = [float(matrix[i, (i - k) % P_SIZE]) for i in range(P_SIZE)]
        factor = jnp.full(node.shape, values[0], F32)
        for i in range(1, P_SIZE):
            factor = jnp.where(node == i, values[i], factor)
        term = factor[None] * (pltpu.roll(v, k, 1) if k else v)
        out = term if out is None else out + term
    return out.reshape(x.shape)


def stiff_many(us, geoms, table):
    d = derivative_table()
    halves = [split(u) for u in us]
    rows = [jnp.concatenate([high, low, high], axis=1) for high, low in halves]
    girth = dot(jnp.concatenate(rows, axis=0), girth_right(table))
    girth = girth * jnp.concatenate([g[2] for g in geoms], axis=0)
    girth = right_mul(girth, girth_right_t(table))
    outs = []
    for k, (u, (high, low), (gr, ga, _)) in enumerate(zip(us, halves, geoms)):
        axial = dot(axial_left(table), jnp.concatenate([high, low, high], axis=0)) * ga
        radial = radial_apply(radial_apply(u, d) * gr, d.T)
        part = girth[k * NODES : (k + 1) * NODES]
        outs.append(axial_apply(axial, d.T) + part + radial)
    return outs


def left_pair(both, x):
    high, low = split(x)
    rows = both.shape[0] // 2
    first = dot(both, high)
    return first[:rows] + first[rows:] + dot(both[:rows], low)


def girth_faces(x, factor, repeat, table):
    rows = x.shape[0]
    stacked = jnp.concatenate([x[:, k * NODES : (k + 1) * NODES] for k in range(3)], axis=0)
    slope = right_mul(stacked, girth_right(table))
    scaled = []
    for k in range(3):
        part = slope[k * rows : (k + 1) * rows]
        part = jnp.concatenate([part] * repeat, axis=0)
        scaled.append(part * factor[:, k * NODES : (k + 1) * NODES])
    moved = right_mul(jnp.concatenate(scaled, axis=0), girth_right_t(table))
    rows = rows * repeat
    return jnp.concatenate([moved[k * rows : (k + 1) * rows] for k in range(3)], axis=1)


def twice(x):
    return jnp.concatenate([x, x], axis=1)


def sum_nodes(t):
    width = t.shape[1]
    v = t.reshape(16, 16, width)
    mid = v[7:8] + v[8:9]
    v = jnp.concatenate([v[:7], mid, mid, v[9:]], axis=0)
    pair = v[:, 7:8, :] + v[:, 8:9, :]
    node = lax.broadcasted_iota(jnp.int32, v.shape, 1)
    return jnp.where((node == 7) | (node == 8), pair, v)


def sum_girth(own, left, right, owners=None):
    lane = lax.broadcasted_iota(jnp.int32, left.shape, 1)
    first = lane % P_SIZE == 0
    last = lane % P_SIZE == P_SIZE - 1

    def inner(x):
        return jnp.where(
            first, pltpu.roll(x, 1, 1), jnp.where(last, pltpu.roll(x, LANES - 1, 1), 0.0)
        )

    sums = []
    for c, x in enumerate(own):
        p = inner(x)
        p = jnp.where(lane == 0, pltpu.roll(left, (LANES - HALO * c - HALO + 1) % LANES, 1), p)
        p = jnp.where(lane == LANES - 1, pltpu.roll(right, (LANES - 1 - HALO * c) % LANES, 1), p)
        sums.append(x + p)
    if owners is None:
        return sums
    p = inner(left)
    q = inner(right)
    for c, x in enumerate(owners):
        p = jnp.where(lane == HALO * c + HALO - 1, pltpu.roll(x, HALO * c + HALO - 1, 1), p)
        q = jnp.where(lane == HALO * c, pltpu.roll(x, (HALO * c + 1) % LANES, 1), q)
    return sums + [left + p, right + q]


def shared_local(parts):
    return jnp.concatenate(sum_girth(parts[:4], parts[4], parts[5], parts[:4]), axis=1)


def lanes_of(x, k):
    return x[:, k * LANES : (k + 1) * LANES]


def pack_kernel(field_in, geom_in, mass_in, to_right, to_left, field, geom, mass, sems):
    copies = [
        pltpu.make_async_copy(field_in, field, sems.at[0]),
        pltpu.make_async_copy(geom_in, geom, sems.at[1]),
        pltpu.make_async_copy(mass_in, mass, sems.at[2]),
    ]
    for copy in copies:
        copy.start()
    lane = lax.broadcasted_iota(jnp.int32, (NODES, LANES), 1)

    def pack(arrays, start):
        out = None
        for k, x in enumerate(arrays):
            moved = pltpu.roll(x, (HALO * k - start) % LANES, 1) if (HALO * k - start) else x
            out = moved if out is None else jnp.where(lane // HALO == k, moved, out)
        return out

    copies[0].wait()
    fields = [field[c] for c in range(C)]
    to_right[0] = pack(fields, LANES - HALO)
    to_left[0] = pack(fields, 0)
    copies[1].wait()
    copies[2].wait()
    others = [geom[k] for k in range(3)] + [mass[...]]
    to_right[1] = pack(others, LANES - HALO)
    to_left[1] = pack(others, 0)


def own_kernel(field, geom, table, out):
    geoms = tuple(twice(geom[k]) for k in range(3))
    us = [jnp.concatenate([field[2 * k], field[2 * k + 1]], axis=1) for k in range(2)]
    out[...] = jnp.concatenate(stiff_many(us, [geoms] * 2, table), axis=1)


def at_faces(low, high, width):
    shape = (16, 16, width)
    node = lax.broadcasted_iota(jnp.int32, shape, 1)
    both = jnp.where(
        node == 0, low[:, None, :], jnp.where(node == 15, high[:, None, :], 0.0)
    )
    return both.reshape(NODES, width)


def wide(x):
    own = lanes_of(x, 0)
    return jnp.concatenate([own] * C + [x[:, LANES:]], axis=1)


def put_faces(x, low, high, offset):
    width = x.shape[1]
    v = x.reshape(16, 16, width)
    low[:, offset : offset + width] = v[:, 0, :]
    high[:, offset : offset + width] = v[:, 15, :]


def action(u, geom, halo_geom, tables):
    own = tuple(twice(geom[k]) for k in range(3))
    geoms = [own, own, tuple(halo_geom[k] for k in range(3))]
    us = [u[:, k * NODES : (k + 1) * NODES] for k in range(3)]
    parts = []
    for t in stiff_many(us, geoms, tables):
        parts += [lanes_of(t, 0), lanes_of(t, 1)]
    return sum_nodes(shared_local(parts)).reshape(NODES, WIDE)


def inner_update(u, total, inverse):
    row = lax.broadcasted_iota(jnp.int32, u.shape, 0) % 16
    return jnp.where((row == 0) | (row == 15), u, u - total * wide(inverse))


def sum_faces(x):
    summed = shared_local([lanes_of(x, k) for k in range(6)]).reshape(2, 16, WIDE)
    pair = summed[:, 7:8, :] + summed[:, 8:9, :]
    node = lax.broadcasted_iota(jnp.int32, summed.shape, 1)
    return jnp.where((node == 7) | (node == 8), pair, summed)


def face_action(v, geom, halo_geom, statics, table):
    low, high = statics
    radial, girthwise = [
        wide(jnp.concatenate([static_part(low, k), static_part(high, k)], axis=0)) for k in (1, 2)
    ]
    nodes = v.reshape(16, 16, WIDE)
    ends = jnp.concatenate([nodes[:, 0, :], nodes[:, 15, :]], axis=0)
    face = left_mul(radial_faces_t(table), left_mul(radial_small(table), ends) * radial)
    face = face + girth_faces(ends, girthwise, 1, table)
    pieces = []
    for tile in range(3):
        ga = halo_geom[1] if tile == 2 else twice(geom[1])
        slope = left_pair(table[: 2 * NODES, :], v[:, tile * NODES : (tile + 1) * NODES]) * ga
        pieces.append(left_pair(ends_pair(table), slope))
    return sum_faces(face + jnp.concatenate(pieces, axis=1))


def two_steps(u, geom, halo_geom, inverse, first, statics, table, state, low, high):
    v = inner_update(u, first, inverse)
    state[...] = v
    put_faces(first, low, high, 0)
    faces = face_action(v, geom, halo_geom, statics, table)
    low[:, WIDE : 2 * WIDE] = faces[0]
    high[:, WIDE : 2 * WIDE] = faces[1]


def second_kernel(state, geom, halo_geom, table, out):
    out[...] = action(state[...], geom, halo_geom, table)


STATIC = 2 * WIDE
NARROW = 3 * LANES


def spread(x, k):
    lane = lax.broadcasted_iota(jnp.int32, x.shape, 1)
    y = jnp.where(lane // HALO == k, x, 0.0)
    y = y + pltpu.roll(y, HALO, 1)
    return y + pltpu.roll(y, 2 * HALO, 1)


def to_send(face, out):
    out[:, :STATIC] = face[:, :STATIC]
    lane = lax.broadcasted_iota(jnp.int32, (16, LANES), 1) // HALO
    for k in range(4):
        out[:, STATIC + k * LANES : STATIC + (k + 1) * LANES] = static_part(face, k)[:, :LANES]
    for k in range(2):
        parts = []
        for j in (2 * k, 2 * k + 1):
            parts += [static_part(face, j)[:, LANES : 2 * LANES], static_part(face, j)[:, 2 * LANES :]]
        block = parts[3]
        for j in range(3):
            block = jnp.where(lane == j, parts[j], block)
        out[:, STATIC + (4 + k) * LANES : STATIC + (5 + k) * LANES] = block


def as_sent(got):
    pieces = [got[:, :STATIC]]
    for k in range(4):
        halos = got[:, STATIC + (4 + k // 2) * LANES : STATIC + (5 + k // 2) * LANES]
        place = 2 * (k % 2)
        pieces.append(got[:, STATIC + k * LANES : STATIC + (k + 1) * LANES])
        pieces += [spread(halos, place), spread(halos, place + 1)]
    return jnp.concatenate(pieces, axis=1)


def halo_kernel(
    left, right, own_total, field, mass, geom, tables, halo_geom, state, mass_out, ends_out, low, high, *sent
):
    left_others, right_others = left[1], right[1]
    geoms = []
    for k in range(3):
        g = jnp.concatenate([spread(left_others, k), spread(right_others, k)], axis=1)
        halo_geom[k] = g
        geoms.append(g)
    u = jnp.concatenate([left[0], right[0]], axis=1)
    (t,) = stiff_many([u], [tuple(geoms)], tables)
    parts = [own_total[:, c * LANES : (c + 1) * LANES] for c in range(C)]
    first = sum_nodes(shared_local(parts + [lanes_of(t, 0), lanes_of(t, 1)]))
    first = first.reshape(NODES, WIDE)
    m = mass[...]
    masses = sum_girth([m], spread(left_others, 3), spread(right_others, 3), [m] * C)
    lumped = sum_nodes(jnp.concatenate(masses, axis=1)).reshape(NODES, NARROW)
    mass_out[...] = lumped
    whole = [jnp.concatenate([geom[k], geoms[k]], axis=1) for k in range(3)]
    end = end_columns(NODES)
    ends = left_mul(axial_left_t(tables), whole[1] * jnp.concatenate([end] * 3, axis=1))
    ends_out[...] = ends
    for k, x in enumerate([lumped, whole[0], whole[2], ends]):
        put_faces(x, low, high, STATIC + k * NARROW)
    start = jnp.concatenate([field[c] for c in range(C)] + [u], axis=1)
    two_steps(start, geom, halo_geom, 1.0 / lumped, first, (low, high), tables, state, low, high)
    to_send(low, sent[0])
    to_send(high, sent[1])


def static_part(ref, k):
    return ref[:, STATIC + k * NARROW : STATIC + (k + 1) * NARROW]


def finish_pair(state, second, inverse, ends, statics, own, got, tables, lanes=WIDE):
    low, high, got_low, got_high = statics
    own_low, own_high = own
    new_low, new_high = got
    w_low = -(own_low[:, :WIDE] + new_low[:, :WIDE]) * wide(
        1.0 / (static_part(low, 0) + static_part(got_low, 0))
    )
    w_high = -(own_high[:, :WIDE] + new_high[:, :WIDE]) * wide(
        1.0 / (static_part(high, 0) + static_part(got_high, 0))
    )
    w = jnp.concatenate([w_low, w_high], axis=0)
    radial, girthwise = [
        wide(jnp.concatenate([static_part(ref, k) for ref in statics], axis=0)) for k in (1, 2)
    ]
    slope = left_mul(radial_small(tables), w)
    face = left_mul(radial_small_t(tables), jnp.concatenate([slope, slope], axis=0) * radial)
    face = face + girth_faces(w, girthwise, 2, tables)
    other = jnp.concatenate([static_part(got_low, 3), static_part(got_high, 3)], axis=0)
    beyond = face[32:] + wide(other) * w
    beyond = sum_faces(beyond)
    beyond_low = beyond[0] + new_low[:, WIDE : 2 * WIDE]
    beyond_high = beyond[1] + new_high[:, WIDE : 2 * WIDE]
    node = lax.broadcasted_iota(jnp.int32, (16, 16, WIDE), 1)
    along = jnp.where(node < P_SIZE, w_low[:, None, :], w_high[:, None, :])
    change = wide(ends) * along.reshape(NODES, WIDE) + at_faces(face[:16], face[16:32], WIDE)
    parts = [lanes_of(change, k) for k in range(6)]
    owners = parts[:4] if lanes == WIDE else None
    summed = sum_girth(parts[:4], parts[4], parts[5], owners)
    change = sum_nodes(jnp.concatenate(summed, axis=1)).reshape(NODES, lanes)
    beyond = at_faces(beyond_low[:, :lanes], beyond_high[:, :lanes], lanes)
    total = second[:, :lanes] + change + beyond
    moved = state[:, :lanes] + at_faces(w_low[:, :lanes], w_high[:, :lanes], lanes)
    return moved - total * wide(inverse)[:, :lanes]


def middle_kernel(state, second, lumped, ends, low, high, got_low, got_high, geom, halo_geom, *refs):
    tables, state_out, inverse_out, next_low, next_high = refs
    got_low, got_high = as_sent(got_low), as_sent(got_high)
    inverse = 1.0 / (
        lumped[...] + at_faces(static_part(got_low, 0), static_part(got_high, 0), NARROW)
    )
    inverse_out[...] = inverse
    statics = (low, high, got_low, got_high)
    u = finish_pair(
        state[...], second[...], inverse, ends[...], statics, (low, high), (got_low, got_high), tables
    )
    first = action(u, geom, halo_geom, tables)
    two_steps(u, geom, halo_geom, inverse, first, (low, high), tables, state_out, next_low, next_high)


def last_kernel(
    state,
    second,
    inverse,
    ends,
    low,
    high,
    got_low,
    got_high,
    own_low,
    own_high,
    new_low,
    new_high,
    slab,
    girth_weight,
    select,
    header,
    tables,
    out,
    packed,
    probes_out,
):
    u = finish_pair(
        state[...],
        second[...],
        inverse[...],
        ends[...],
        (low, high, as_sent(got_low), as_sent(got_high)),
        (own_low, own_high),
        (new_low, new_high),
        tables,
        C * LANES,
    )
    for c in range(C):
        out[c] = lanes_of(u, c)
    slab_high, slab_low = split(slab[...])
    values = left_pair(jnp.concatenate([slab_high, slab_low], axis=0), u)
    stacked = jnp.concatenate([lanes_of(values, c) for c in range(C)], axis=0)
    weight_high, weight_low = split(girth_weight[...])
    weights = jnp.concatenate([weight_high, weight_high, weight_low], axis=0)
    probes = right_mul(stacked, weights)
    slots = slab.shape[0]
    spread = jnp.concatenate([probes[c * slots : (c + 1) * slots] for c in range(C)], axis=1)
    probes_out[...] = spread
    high_part, low_part = split(spread)
    chosen = select[...].astype(BF16)
    rows = dot(
        jnp.concatenate([chosen, chosen], axis=1),
        jnp.concatenate([high_part, low_part], axis=0),
    )
    for c in range(C):
        block = lanes_of(rows, c).reshape(-1, SLOTS, LANES)
        if c == 0:
            place = lax.broadcasted_iota(jnp.int32, block.shape, 1)
            block = jnp.where(place == SLOTS - 1, header[...][:, None, :], block)
        packed[:, c * SLOTS : (c + 1) * SLOTS, :] = block


def weights_kernel(
    cycle_id, cycle_radial, cycle_axial, cycle_weights, az_elem, az_weights, slab, girth, select, header
):
    slots = cycle_id.shape[0]
    ids = cycle_id[...].reshape(1, slots)
    in_radial, in_axial = [x[...].reshape(1, slots) for x in (cycle_radial, cycle_axial)]
    radial, axial = [
        jnp.concatenate(
            [jnp.where(owner == e, cycle_weights[k], 0.0) for e in range(2)], axis=0
        )
        for k, owner in enumerate((in_radial, in_axial))
    ]
    slab[...] = jnp.transpose((radial[:, None, :] * axial[None, :, :]).reshape(NODES, slots))
    places = az_elem[...].reshape(1, 1, LANES)
    element = lax.broadcasted_iota(jnp.int32, (LANES // P_SIZE, P_SIZE, LANES), 0)
    girth[...] = jnp.where(element == places, az_weights[...][None], 0.0).reshape(LANES, LANES)
    used = ids >= 0
    target = jnp.where(used, lax.shift_right_logical(ids, 4), -1).astype(F32)
    across = jnp.broadcast_to(target, (slots, slots))
    down = jnp.transpose(across)
    before = lax.broadcasted_iota(jnp.int32, across.shape, 0) < lax.broadcasted_iota(
        jnp.int32, across.shape, 1
    )
    rank = jnp.sum(jnp.where((across == down) & before, 1.0, 0.0), axis=0, keepdims=True)
    position = jnp.where(used & (rank < SLOTS - 1.5), target * SLOTS + rank, -1.0)
    wanted = lax.broadcasted_iota(jnp.int32, select.shape, 0).astype(F32)
    select[...] = jnp.where(wanted == position, 1.0, 0.0)
    number = (ids & (ROWS_DEV - 1)).astype(F32) + 1.0
    owners = lax.broadcasted_iota(jnp.int32, (header.shape[0], slots), 0).astype(F32)
    named = jnp.where(owners == target, number, 0.0).astype(BF16)
    ranks = lax.broadcasted_iota(jnp.int32, (LANES, slots), 0).astype(F32)
    placed = jnp.where(ranks == rank, 1.0, 0.0).astype(BF16)
    numbers = lax.dot_general(
        named, placed, (((1,), (1,)), ((), ())), preferred_element_type=F32
    )
    overflow = jnp.max(jnp.where(used & (rank > SLOTS - 1.5), 1.0, 0.0), axis=1, keepdims=True)
    lane = lax.broadcasted_iota(jnp.int32, header.shape, 1)
    header[...] = jnp.where(
        lane >= SLOTS, overflow, jnp.where(lane < SLOTS - 1, numbers, 0.0)
    )


def unpack_kernel(pieces, out, crowded):
    sources = pieces.shape[0]
    heads = pieces[:, 0:SLOTS, :]
    head = jnp.broadcast_to(heads[:, SLOTS - 1 : SLOTS, :], heads.shape)
    place = lax.broadcasted_iota(jnp.int32, heads.shape, 1)
    lane = lax.broadcasted_iota(jnp.int32, heads.shape, 2)
    mine = jnp.where((lane == place) & (place < SLOTS - 1), head, 0.0)
    crowded[0, 0] = jnp.max(jnp.where(lane >= SLOTS, head, 0.0)).astype(jnp.int32)
    row = jnp.sum(mine.reshape(sources * SLOTS, LANES), axis=1, keepdims=True)
    column = lax.broadcasted_iota(jnp.int32, (sources * SLOTS, LANES), 1).astype(F32)
    chosen = jnp.transpose(jnp.where(row == column + 1.0, 1.0, 0.0))[:ROWS_DEV].astype(BF16)
    both = jnp.concatenate([chosen, chosen], axis=1)
    for c in range(C):
        x = pieces[:, c * SLOTS : (c + 1) * SLOTS, :].reshape(sources * SLOTS, LANES)
        high, low = split(x)
        out[c * ROWS_DEV : (c + 1) * ROWS_DEV, :] = dot(
            both, jnp.concatenate([high, low], axis=0)
        )


def dft_kernel(rows, phase, table_high, table_low, out):
    turn_re = phase[0:1, :]
    turn_im = phase[1:2, :]
    total = None
    for pair in range(8):
        x = jnp.concatenate([rows[2 * pair], rows[2 * pair + 1]], axis=1)
        z = jnp.concatenate([x * twice(turn_re), x * twice(turn_im)], axis=0)
        high, low = split(z)
        block = pl.ds(pair * 256, 256)
        th, tl = table_high[block, :], table_low[block, :]
        first = dot(jnp.concatenate([high, low], axis=0), th)
        half = first.shape[0] // 2
        part = first[:half] + first[half:] + dot(high, tl)
        total = part if total is None else total + part
    n = C * ROWS_DEV
    re = total[:n, :LANES] + total[n:, LANES:]
    im = total[n:, :LANES] - total[:n, LANES:]
    for c in range(C):
        out[0, :, c, :] = re[c * ROWS_DEV : (c + 1) * ROWS_DEV]
        out[1, :, c, :] = im[c * ROWS_DEV : (c + 1) * ROWS_DEV]


def call(kernel, shapes, flops, *args):
    vmem = pl.BlockSpec(memory_space=pltpu.VMEM)
    out_shape = [jax.ShapeDtypeStruct(s, F32) for s in shapes]
    return pl.pallas_call(
        kernel,
        out_shape=out_shape,
        in_specs=[vmem] * len(args),
        out_specs=[vmem] * len(shapes),
        compiler_params=pltpu.CompilerParams(vmem_limit_bytes=VMEM_LIMIT),
        cost_estimate=pl.CostEstimate(flops=flops, bytes_accessed=2000000, transcendentals=0),
    )(*args)


def pack_halos(*args):
    hbm, vmem = [pl.BlockSpec(memory_space=m) for m in (pltpu.HBM, pltpu.VMEM)]
    return pl.pallas_call(
        pack_kernel,
        out_shape=[jax.ShapeDtypeStruct((2, NODES, LANES), F32)] * 2,
        in_specs=[hbm] * len(args),
        out_specs=[vmem] * 2,
        scratch_shapes=[pltpu.VMEM(x.shape, F32) for x in args]
        + [pltpu.SemaphoreType.DMA((len(args),))],
        compiler_params=pltpu.CompilerParams(vmem_limit_bytes=LOAD_LIMIT),
    )(*args)


def body(
    field, geometry, mass, cycle_id, cycle_radial, cycle_axial, cycle_weights, az_elem, az_weights
):
    axial_count, girth_count = lax.axis_size("axial"), lax.axis_size("girth")
    up = [(i, i + 1) for i in range(axial_count - 1)]
    down = [(j, i) for i, j in up]
    around = [(i, (i + 1) % girth_count) for i in range(girth_count)]
    back = [(j, i) for i, j in around]
    field = field.reshape(C, NODES, LANES)
    geom = geometry.reshape(3, NODES, LANES)
    mass = mass.reshape(NODES, LANES)
    table = jnp.asarray(stiffness_table())
    to_right, to_left = pack_halos(field, geom, mass)
    tile_flops = 18 * 2 * 256**3

    left = lax.ppermute(to_right, "girth", around)
    right = lax.ppermute(to_left, "girth", back)
    (own_total,) = call(own_kernel, [(NODES, C * LANES)], 2 * tile_flops, field, geom, table)

    def exchange(low, high):
        return lax.ppermute(high, "axial", up), lax.ppermute(low, "axial", down)

    whole, narrow = (NODES, WIDE), (NODES, NARROW)
    face_static, sent = (16, STATIC + 4 * NARROW), (16, STATIC + 6 * LANES)
    halo_geom, state, lumped, ends, low, high, send_low, send_high = call(
        halo_kernel,
        [(3, NODES, 2 * LANES), whole, narrow, narrow, face_static, face_static, sent, sent],
        2 * tile_flops,
        left,
        right,
        own_total,
        field,
        mass,
        geom,
        table,
    )
    got_low, got_high = exchange(send_low, send_high)
    (second,) = call(second_kernel, [whole], 3 * tile_flops, state, geom, halo_geom, table)
    state, inverse, own_low, own_high = call(
        middle_kernel,
        [whole, narrow, (16, STATIC), (16, STATIC)],
        4 * tile_flops,
        state,
        second,
        lumped,
        ends,
        low,
        high,
        got_low,
        got_high,
        geom,
        halo_geom,
        table,
    )
    new_low, new_high = exchange(own_low, own_high)
    (second,) = call(second_kernel, [whole], 3 * tile_flops, state, geom, halo_geom, table)

    slot_count = cycle_id.shape[0]
    slab, girth_weight, select, header = call(
        weights_kernel,
        [
            (slot_count, NODES),
            (LANES, LANES),
            (SLOTS * axial_count, slot_count),
            (axial_count, LANES),
        ],
        1000000,
        cycle_id,
        cycle_radial,
        cycle_axial,
        cycle_weights,
        az_elem,
        az_weights,
    )

    final, packed, probes = call(
        last_kernel,
        [(C, NODES, LANES), (axial_count, C * SLOTS, LANES), (slot_count, C * LANES)],
        tile_flops,
        state,
        second,
        inverse,
        ends,
        low,
        high,
        got_low,
        got_high,
        own_low,
        own_high,
        new_low,
        new_high,
        slab,
        girth_weight,
        select,
        header,
        table,
    )
    pieces = lax.all_to_all(packed, "axial", 0, 0)

    vmem = pl.BlockSpec(memory_space=pltpu.VMEM)
    rows, crowded = pl.pallas_call(
        unpack_kernel,
        out_shape=[
            jax.ShapeDtypeStruct((C * ROWS_DEV, LANES), F32),
            jax.ShapeDtypeStruct((1, 1), jnp.int32),
        ],
        in_specs=[vmem],
        out_specs=[vmem, pl.BlockSpec(memory_space=pltpu.SMEM)],
        compiler_params=pltpu.CompilerParams(vmem_limit_bytes=VMEM_LIMIT),
    )(pieces)

    def dense(rows, probes, cycle_id):
        wanted = jnp.arange(ROWS_DEV * axial_count, dtype=jnp.int32)
        chosen = (wanted[:, None] == cycle_id[None, :]).astype(F32)
        rows = jnp.dot(chosen, probes, precision=lax.Precision.HIGHEST)
        rows = rows.reshape(axial_count, ROWS_DEV, C * LANES)
        rows = jnp.sum(lax.all_to_all(rows, "axial", 0, 0), axis=0)
        return rows.reshape(ROWS_DEV, C, LANES).swapaxes(0, 1).reshape(C * ROWS_DEV, LANES)

    rows = lax.cond(
        crowded[0, 0] > 0, dense, lambda rows, *_: rows, rows, probes, cycle_id
    )
    rows = lax.all_gather(rows, "girth")
    table_high, table_low, phases = dft_tables()
    phase = lax.dynamic_index_in_dim(
        jnp.asarray(phases), lax.axis_index("girth"), 0, keepdims=False
    )
    (spectrum,) = call(
        dft_kernel,
        [(2, ROWS_DEV, C, LANES)],
        tile_flops,
        rows,
        phase,
        jnp.asarray(table_high),
        jnp.asarray(table_low),
    )
    return final.reshape(C, 16, 16, LANES), spectrum


def solution(mesh):
    return jax.shard_map(
        body,
        mesh=mesh,
        in_specs=(
            P(None, None, "axial", "girth"),
            P(None, None, "axial", "girth"),
            P(None, "axial", "girth"),
            P("axial"),
            P("axial"),
            P("axial"),
            P(None, None, "axial"),
            P("girth"),
            P(None, "girth"),
        ),
        out_specs=(P(None, None, "axial", "girth"), P(None, "axial", None, "girth")),
        check_vma=False,
    )
```

```python
import math

import jax
import jax.numpy as jnp
import ml_dtypes
import numpy as np
from jax import lax
from jax.experimental import pallas as pl
from jax.experimental.pallas import tpu as pltpu
from jax.sharding import PartitionSpec as P

C = 4
P_SIZE = 8
LANES = 128
HALO = 32
NODES = 256
WIDE = 6 * LANES
ROWS_DEV = 16
SLOTS = 8
VMEM_LIMIT = 32 * 1024 * 1024
LOAD_LIMIT = 60000000
F32 = jnp.float32
BF16 = jnp.bfloat16

LOBATTO = (
    -1.0,
    -0.8717401485096066,
    -0.5917001814331423,
    -0.2092992179024789,
    0.2092992179024789,
    0.5917001814331423,
    0.8717401485096066,
    1.0,
)


def derivative_table():
    node_count = len(LOBATTO)
    barycentric = []
    for row_index in range(node_count):
        product = 1.0
        for col_index in range(node_count):
            if col_index != row_index:
                product = product * (LOBATTO[row_index] - LOBATTO[col_index])
        barycentric.append(1.0 / product)
    table_rows = []
    for row_index in range(node_count):
        entries = []
        for col_index in range(node_count):
            if col_index != row_index:
                entries.append(
                    barycentric[col_index]
                    / barycentric[row_index]
                    / (LOBATTO[row_index] - LOBATTO[col_index])
                )
            else:
                entries.append(0.0)
        entries[row_index] = -sum(entries)
        table_rows.append(entries)
    return np.asarray(table_rows, np.float32)


def np_split(table):
    table = np.asarray(table, np.float32)
    high = table.astype(ml_dtypes.bfloat16)
    low = (table - high.astype(np.float32)).astype(ml_dtypes.bfloat16)
    return high, low


def stiffness_table():
    d = derivative_table()
    eye = lambda n: np.eye(n, dtype=np.float32)
    axial = np.kron(eye(32), d)
    blocks = list(np_split(axial)) + list(np_split(axial.T))
    ends = axial.T.reshape(16, 16, NODES)[:, [0, 15]].swapaxes(0, 1).reshape(32, NODES)
    blocks += list(np_split(ends))
    for small in (np.kron(eye(4), d), np.kron(eye(8), d.T), np.kron(eye(4), d.T)):
        high, low = np_split(small)
        row = np.concatenate([high, high, low], axis=1)
        blocks.append(np.pad(row, ((0, 0), (0, NODES - row.shape[1]))))
    return np.concatenate(blocks, axis=0)


def dft_tables():
    a = np.arange(2048)[:, None]
    m = np.arange(LANES)[None, :]
    angle = 2.0 * np.pi * ((a * m) % 2048) / 2048.0
    table = np.concatenate([np.cos(angle), np.sin(angle)], axis=1)
    high, low = np_split(table)
    k = np.arange(16)[:, None]
    lane = np.arange(LANES)[None, :]
    turn = 2.0 * np.pi * ((k * lane) % 16) / 16.0
    phase = np.stack([np.cos(turn), -np.sin(turn)], axis=1) / math.sqrt(2048.0)
    return high, low, phase.astype(np.float32)


def split(x):
    high = x.astype(BF16)
    return high, (x - high.astype(F32)).astype(BF16)


def dot(a, b):
    return jnp.dot(a, b, preferred_element_type=F32)


def left_mul(table, x):
    high, low = split(x)
    return dot(table, jnp.concatenate([high, low, high], axis=0))


def right_mul(x, table):
    high, low = split(x)
    return dot(jnp.concatenate([high, low, high], axis=1), table)


def square(table, k):
    return table[k * NODES : (k + 1) * NODES, :]


def axial_left(table):
    return jnp.concatenate([square(table, 0), square(table, 0), square(table, 1)], axis=1)


def axial_left_t(table):
    return jnp.concatenate([square(table, 2), square(table, 2), square(table, 3)], axis=1)


def girth_right(table):
    return jnp.concatenate([square(table, 2), square(table, 2), square(table, 3)], axis=0)


def girth_right_t(table):
    return jnp.concatenate([square(table, 0), square(table, 0), square(table, 1)], axis=0)


SMALL = 4 * NODES


def ends_pair(table):
    return table[SMALL : SMALL + 64, :]


def radial_small(table):
    return table[SMALL + 64 : SMALL + 96, :96]


def radial_small_t(table):
    return table[SMALL + 96 : SMALL + 160, :192]


def radial_faces_t(table):
    return table[SMALL + 160 : SMALL + 192, :96]


def radial_apply(x, matrix):
    half = P_SIZE // 2
    odd_rows = 0.5 * (matrix[:half, :half] - matrix[:half, : half - 1 : -1])
    even_rows = 0.5 * (matrix[:half, :half] + matrix[:half, : half - 1 : -1])
    outs = {}
    for element in range(2):
        for part in range(2):
            for tile in range(x.shape[1] // LANES):
                nodes = []
                for i in range(P_SIZE):
                    row = (element * P_SIZE + i) * 16 + part * 8
                    nodes.append(x[row : row + 8, tile * LANES : (tile + 1) * LANES])
                even = [nodes[j] + nodes[P_SIZE - 1 - j] for j in range(half)]
                odd = [nodes[j] - nodes[P_SIZE - 1 - j] for j in range(half)]
                for i in range(half):
                    p = float(odd_rows[i, 0]) * odd[0]
                    q = float(even_rows[i, 0]) * even[0]
                    for j in range(1, half):
                        p = p + float(odd_rows[i, j]) * odd[j]
                        q = q + float(even_rows[i, j]) * even[j]
                    outs[element * P_SIZE + i, part, tile] = p + q
                    outs[element * P_SIZE + P_SIZE - 1 - i, part, tile] = p - q
    columns = []
    for tile in range(x.shape[1] // LANES):
        columns.append(
            jnp.concatenate([outs[i, part, tile] for i in range(16) for part in range(2)], axis=0)
        )
    return jnp.concatenate(columns, axis=1)


def end_columns(rows):
    d = derivative_table()
    values = [float(x) for x in np.concatenate([d[:, 0], d[:, 7]])]
    node = lax.broadcasted_iota(jnp.int32, (16, LANES), 0)
    column = jnp.full((16, LANES), values[0], F32)
    for k in range(1, 16):
        column = jnp.where(node == k, values[k], column)
    return jnp.broadcast_to(column[None], (16, 16, LANES)).reshape(rows, LANES)


def stiff_many(us, geoms, table):
    d = derivative_table()
    halves = [split(u) for u in us]
    rows = [jnp.concatenate([high, low, high], axis=1) for high, low in halves]
    girth = dot(jnp.concatenate(rows, axis=0), girth_right(table))
    girth = girth * jnp.concatenate([g[2] for g in geoms], axis=0)
    girth = right_mul(girth, girth_right_t(table))
    outs = []
    for k, (u, (high, low), (gr, ga, _)) in enumerate(zip(us, halves, geoms)):
        axial = dot(axial_left(table), jnp.concatenate([high, low, high], axis=0)) * ga
        radial = radial_apply(radial_apply(u, d) * gr, d.T)
        part = girth[k * NODES : (k + 1) * NODES]
        outs.append(left_mul(axial_left_t(table), axial) + part + radial)
    return outs


def left_pair(both, x):
    high, low = split(x)
    rows = both.shape[0] // 2
    first = dot(both, high)
    return first[:rows] + first[rows:] + dot(both[:rows], low)


def girth_faces(x, factor, repeat, table):
    rows = x.shape[0]
    stacked = jnp.concatenate([x[:, k * NODES : (k + 1) * NODES] for k in range(3)], axis=0)
    slope = right_mul(stacked, girth_right(table))
    scaled = []
    for k in range(3):
        part = slope[k * rows : (k + 1) * rows]
        part = jnp.concatenate([part] * repeat, axis=0)
        scaled.append(part * factor[:, k * NODES : (k + 1) * NODES])
    moved = right_mul(jnp.concatenate(scaled, axis=0), girth_right_t(table))
    rows = rows * repeat
    return jnp.concatenate([moved[k * rows : (k + 1) * rows] for k in range(3)], axis=1)


def twice(x):
    return jnp.concatenate([x, x], axis=1)


def sum_nodes(t):
    width = t.shape[1]
    v = t.reshape(16, 16, width)
    mid = v[7:8] + v[8:9]
    v = jnp.concatenate([v[:7], mid, mid, v[9:]], axis=0)
    pair = v[:, 7:8, :] + v[:, 8:9, :]
    node = lax.broadcasted_iota(jnp.int32, v.shape, 1)
    return jnp.where((node == 7) | (node == 8), pair, v)


def sum_girth(own, left, right, owners=None):
    lane = lax.broadcasted_iota(jnp.int32, left.shape, 1)
    first = lane % P_SIZE == 0
    last = lane % P_SIZE == P_SIZE - 1

    def inner(x):
        return jnp.where(
            first, pltpu.roll(x, 1, 1), jnp.where(last, pltpu.roll(x, LANES - 1, 1), 0.0)
        )

    sums = []
    for c, x in enumerate(own):
        p = inner(x)
        p = jnp.where(lane == 0, pltpu.roll(left, (LANES - HALO * c - HALO + 1) % LANES, 1), p)
        p = jnp.where(lane == LANES - 1, pltpu.roll(right, (LANES - 1 - HALO * c) % LANES, 1), p)
        sums.append(x + p)
    if owners is None:
        return sums
    p = inner(left)
    q = inner(right)
    for c, x in enumerate(owners):
        p = jnp.where(lane == HALO * c + HALO - 1, pltpu.roll(x, HALO * c + HALO - 1, 1), p)
        q = jnp.where(lane == HALO * c, pltpu.roll(x, (HALO * c + 1) % LANES, 1), q)
    return sums + [left + p, right + q]


def shared_local(parts):
    return jnp.concatenate(sum_girth(parts[:4], parts[4], parts[5], parts[:4]), axis=1)


def lanes_of(x, k):
    return x[:, k * LANES : (k + 1) * LANES]


def pack_kernel(field_in, geom_in, mass_in, to_right, to_left, field, geom, mass, sems):
    copies = [
        pltpu.make_async_copy(field_in, field, sems.at[0]),
        pltpu.make_async_copy(geom_in, geom, sems.at[1]),
        pltpu.make_async_copy(mass_in, mass, sems.at[2]),
    ]
    for copy in copies:
        copy.start()
    lane = lax.broadcasted_iota(jnp.int32, (NODES, LANES), 1)

    def pack(arrays, start):
        out = None
        for k, x in enumerate(arrays):
            moved = pltpu.roll(x, (HALO * k - start) % LANES, 1) if (HALO * k - start) else x
            out = moved if out is None else jnp.where(lane // HALO == k, moved, out)
        return out

    copies[0].wait()
    fields = [field[c] for c in range(C)]
    to_right[0] = pack(fields, LANES - HALO)
    to_left[0] = pack(fields, 0)
    copies[1].wait()
    copies[2].wait()
    others = [geom[k] for k in range(3)] + [mass[...]]
    to_right[1] = pack(others, LANES - HALO)
    to_left[1] = pack(others, 0)


def own_kernel(field, geom, table, out):
    geoms = tuple(twice(geom[k]) for k in range(3))
    us = [jnp.concatenate([field[2 * k], field[2 * k + 1]], axis=1) for k in range(2)]
    out[...] = jnp.concatenate(stiff_many(us, [geoms] * 2, table), axis=1)


def at_faces(low, high, width):
    shape = (16, 16, width)
    node = lax.broadcasted_iota(jnp.int32, shape, 1)
    both = jnp.where(
        node == 0, low[:, None, :], jnp.where(node == 15, high[:, None, :], 0.0)
    )
    return both.reshape(NODES, width)


def wide(x):
    own = lanes_of(x, 0)
    return jnp.concatenate([own] * C + [x[:, LANES:]], axis=1)


def put_faces(x, low, high, offset):
    width = x.shape[1]
    v = x.reshape(16, 16, width)
    low[:, offset : offset + width] = v[:, 0, :]
    high[:, offset : offset + width] = v[:, 15, :]


def action(u, geom, halo_geom, tables):
    own = tuple(twice(geom[k]) for k in range(3))
    geoms = [own, own, tuple(halo_geom[k] for k in range(3))]
    us = [u[:, k * NODES : (k + 1) * NODES] for k in range(3)]
    parts = []
    for t in stiff_many(us, geoms, tables):
        parts += [lanes_of(t, 0), lanes_of(t, 1)]
    return sum_nodes(shared_local(parts)).reshape(NODES, WIDE)


def inner_update(u, total, inverse):
    row = lax.broadcasted_iota(jnp.int32, u.shape, 0) % 16
    return jnp.where((row == 0) | (row == 15), u, u - total * wide(inverse))


def sum_faces(x):
    summed = shared_local([lanes_of(x, k) for k in range(6)]).reshape(2, 16, WIDE)
    pair = summed[:, 7:8, :] + summed[:, 8:9, :]
    node = lax.broadcasted_iota(jnp.int32, summed.shape, 1)
    return jnp.where((node == 7) | (node == 8), pair, summed)


def face_action(v, geom, halo_geom, statics, table):
    low, high = statics
    radial, girthwise = [
        wide(jnp.concatenate([static_part(low, k), static_part(high, k)], axis=0)) for k in (1, 2)
    ]
    nodes = v.reshape(16, 16, WIDE)
    ends = jnp.concatenate([nodes[:, 0, :], nodes[:, 15, :]], axis=0)
    face = left_mul(radial_faces_t(table), left_mul(radial_small(table), ends) * radial)
    face = face + girth_faces(ends, girthwise, 1, table)
    pieces = []
    for tile in range(3):
        ga = halo_geom[1] if tile == 2 else twice(geom[1])
        slope = left_pair(table[: 2 * NODES, :], v[:, tile * NODES : (tile + 1) * NODES]) * ga
        pieces.append(left_pair(ends_pair(table), slope))
    return sum_faces(face + jnp.concatenate(pieces, axis=1))


def two_steps(u, geom, halo_geom, inverse, first, statics, table, state, low, high):
    v = inner_update(u, first, inverse)
    state[...] = v
    put_faces(first, low, high, 0)
    faces = face_action(v, geom, halo_geom, statics, table)
    low[:, WIDE : 2 * WIDE] = faces[0]
    high[:, WIDE : 2 * WIDE] = faces[1]


def second_kernel(state, geom, halo_geom, table, out):
    out[...] = action(state[...], geom, halo_geom, table)


STATIC = 2 * WIDE
NARROW = 3 * LANES


def spread(x, k):
    lane = lax.broadcasted_iota(jnp.int32, x.shape, 1)
    y = jnp.where(lane // HALO == k, x, 0.0)
    y = y + pltpu.roll(y, HALO, 1)
    return y + pltpu.roll(y, 2 * HALO, 1)


OWN = C * LANES
FIRST_SENT = WIDE + OWN + LANES
SECOND_SENT = OWN + LANES + OWN


def near(shape):
    return lax.broadcasted_iota(jnp.int32, shape, 1) % HALO >= HALO // 2


def join_halves(x):
    return jnp.where(near((16, LANES)), x[:, :LANES], x[:, LANES:])


def part_halves(x):
    inside = near(x.shape)
    return [jnp.where(inside, x, 0.0), jnp.where(inside, 0.0, x)]


def to_send(face, out):
    out[:, : WIDE + OWN] = face[:, : WIDE + OWN]
    out[:, WIDE + OWN : FIRST_SENT] = join_halves(face[:, WIDE + OWN : STATIC])
    lane = lax.broadcasted_iota(jnp.int32, (16, LANES), 1) // HALO
    for k in range(4):
        at = FIRST_SENT + k * LANES
        out[:, at : at + LANES] = static_part(face, k)[:, :LANES]
    for k in range(2):
        parts = []
        for j in (2 * k, 2 * k + 1):
            parts += [static_part(face, j)[:, LANES : 2 * LANES], static_part(face, j)[:, 2 * LANES :]]
        block = parts[3]
        for j in range(3):
            block = jnp.where(lane == j, parts[j], block)
        at = FIRST_SENT + (4 + k) * LANES
        out[:, at : at + LANES] = block


def as_sent(got):
    pieces = [got[:, : WIDE + OWN]] + part_halves(got[:, WIDE + OWN : FIRST_SENT])
    for k in range(4):
        at = FIRST_SENT + (4 + k // 2) * LANES
        halos = got[:, at : at + LANES]
        place = 2 * (k % 2)
        pieces.append(got[:, FIRST_SENT + k * LANES : FIRST_SENT + (k + 1) * LANES])
        pieces += [spread(halos, place), spread(halos, place + 1)]
    return jnp.concatenate(pieces, axis=1)


def to_send_second(face, out):
    out[:, :OWN] = face[:, :OWN]
    out[:, OWN : OWN + LANES] = join_halves(face[:, OWN:WIDE])
    out[:, OWN + LANES :] = face[:, WIDE : WIDE + OWN]


def second_as_sent(got):
    pieces = [got[:, :OWN]] + part_halves(got[:, OWN : OWN + LANES])
    pieces += [got[:, OWN + LANES :], jnp.zeros((16, 2 * LANES), F32)]
    return jnp.concatenate(pieces, axis=1)


def halo_kernel(
    left, right, own_total, field, mass, geom, tables, halo_geom, state, mass_out, ends_out, low, high, *sent
):
    left_others, right_others = left[1], right[1]
    geoms = []
    for k in range(3):
        g = jnp.concatenate([spread(left_others, k), spread(right_others, k)], axis=1)
        halo_geom[k] = g
        geoms.append(g)
    u = jnp.concatenate([left[0], right[0]], axis=1)
    (t,) = stiff_many([u], [tuple(geoms)], tables)
    parts = [own_total[:, c * LANES : (c + 1) * LANES] for c in range(C)]
    first = sum_nodes(shared_local(parts + [lanes_of(t, 0), lanes_of(t, 1)]))
    first = first.reshape(NODES, WIDE)
    m = mass[...]
    masses = sum_girth([m], spread(left_others, 3), spread(right_others, 3), [m] * C)
    lumped = sum_nodes(jnp.concatenate(masses, axis=1)).reshape(NODES, NARROW)
    mass_out[...] = lumped
    whole = [jnp.concatenate([geom[k], geoms[k]], axis=1) for k in range(3)]
    end = end_columns(NODES)
    ends = left_mul(axial_left_t(tables), whole[1] * jnp.concatenate([end] * 3, axis=1))
    ends_out[...] = ends
    for k, x in enumerate([lumped, whole[0], whole[2], ends]):
        put_faces(x, low, high, STATIC + k * NARROW)
    start = jnp.concatenate([field[c] for c in range(C)] + [u], axis=1)
    two_steps(start, geom, halo_geom, 1.0 / lumped, first, (low, high), tables, state, low, high)
    to_send(low, sent[0])
    to_send(high, sent[1])


def static_part(ref, k):
    return ref[:, STATIC + k * NARROW : STATIC + (k + 1) * NARROW]


def finish_pair(state, second, inverse, ends, statics, own, got, tables, lanes=WIDE):
    low, high, got_low, got_high = statics
    own_low, own_high = own
    new_low, new_high = got
    w_low = -(own_low[:, :WIDE] + new_low[:, :WIDE]) * wide(
        1.0 / (static_part(low, 0) + static_part(got_low, 0))
    )
    w_high = -(own_high[:, :WIDE] + new_high[:, :WIDE]) * wide(
        1.0 / (static_part(high, 0) + static_part(got_high, 0))
    )
    w = jnp.concatenate([w_low, w_high], axis=0)
    radial, girthwise = [
        wide(jnp.concatenate([static_part(ref, k) for ref in statics], axis=0)) for k in (1, 2)
    ]
    slope = left_mul(radial_small(tables), w)
    face = left_mul(radial_small_t(tables), jnp.concatenate([slope, slope], axis=0) * radial)
    face = face + girth_faces(w, girthwise, 2, tables)
    other = jnp.concatenate([static_part(got_low, 3), static_part(got_high, 3)], axis=0)
    beyond = face[32:] + wide(other) * w
    beyond = sum_faces(beyond)
    beyond_low = beyond[0] + new_low[:, WIDE : 2 * WIDE]
    beyond_high = beyond[1] + new_high[:, WIDE : 2 * WIDE]
    node = lax.broadcasted_iota(jnp.int32, (16, 16, WIDE), 1)
    along = jnp.where(node < P_SIZE, w_low[:, None, :], w_high[:, None, :])
    change = wide(ends) * along.reshape(NODES, WIDE) + at_faces(face[:16], face[16:32], WIDE)
    parts = [lanes_of(change, k) for k in range(6)]
    owners = parts[:4] if lanes == WIDE else None
    summed = sum_girth(parts[:4], parts[4], parts[5], owners)
    change = sum_nodes(jnp.concatenate(summed, axis=1)).reshape(NODES, lanes)
    beyond = at_faces(beyond_low[:, :lanes], beyond_high[:, :lanes], lanes)
    total = second[:, :lanes] + change + beyond
    moved = state[:, :lanes] + at_faces(w_low[:, :lanes], w_high[:, :lanes], lanes)
    return moved - total * wide(inverse)[:, :lanes]


def middle_kernel(state, second, lumped, ends, low, high, got_low, got_high, geom, halo_geom, *refs):
    tables, state_out, inverse_out, next_low, next_high, *sent = refs
    got_low, got_high = as_sent(got_low), as_sent(got_high)
    inverse = 1.0 / (
        lumped[...] + at_faces(static_part(got_low, 0), static_part(got_high, 0), NARROW)
    )
    inverse_out[...] = inverse
    statics = (low, high, got_low, got_high)
    u = finish_pair(
        state[...], second[...], inverse, ends[...], statics, (low, high), (got_low, got_high), tables
    )
    first = action(u, geom, halo_geom, tables)
    two_steps(u, geom, halo_geom, inverse, first, (low, high), tables, state_out, next_low, next_high)
    to_send_second(next_low, sent[0])
    to_send_second(next_high, sent[1])


def last_kernel(
    state,
    second,
    inverse,
    ends,
    low,
    high,
    got_low,
    got_high,
    own_low,
    own_high,
    new_low,
    new_high,
    slab,
    girth_weight,
    select,
    header,
    tables,
    out,
    packed,
    probes_out,
):
    u = finish_pair(
        state[...],
        second[...],
        inverse[...],
        ends[...],
        (low, high, as_sent(got_low), as_sent(got_high)),
        (own_low, own_high),
        (second_as_sent(new_low), second_as_sent(new_high)),
        tables,
        C * LANES,
    )
    for c in range(C):
        out[c] = lanes_of(u, c)
    slab_high, slab_low = split(slab[...])
    values = left_pair(jnp.concatenate([slab_high, slab_low], axis=0), u)
    stacked = jnp.concatenate([lanes_of(values, c) for c in range(C)], axis=0)
    weight_high, weight_low = split(girth_weight[...])
    weights = jnp.concatenate([weight_high, weight_high, weight_low], axis=0)
    probes = right_mul(stacked, weights)
    slots = slab.shape[0]
    spread = jnp.concatenate([probes[c * slots : (c + 1) * slots] for c in range(C)], axis=1)
    probes_out[...] = spread
    high_part, low_part = split(spread)
    chosen = select[...].astype(BF16)
    rows = dot(
        jnp.concatenate([chosen, chosen], axis=1),
        jnp.concatenate([high_part, low_part], axis=0),
    )
    for c in range(C):
        block = lanes_of(rows, c).reshape(-1, SLOTS, LANES)
        if c == 0:
            place = lax.broadcasted_iota(jnp.int32, block.shape, 1)
            block = jnp.where(place == SLOTS - 1, header[...][:, None, :], block)
        packed[:, c * SLOTS : (c + 1) * SLOTS, :] = block


def weights_kernel(
    cycle_id, cycle_radial, cycle_axial, cycle_weights, az_elem, az_weights, slab, girth, select, header
):
    slots = cycle_id.shape[0]
    ids = cycle_id[...].reshape(1, slots)
    in_radial, in_axial = [x[...].reshape(1, slots) for x in (cycle_radial, cycle_axial)]
    radial, axial = [
        jnp.concatenate(
            [jnp.where(owner == e, cycle_weights[k], 0.0) for e in range(2)], axis=0
        )
        for k, owner in enumerate((in_radial, in_axial))
    ]
    slab[...] = jnp.transpose((radial[:, None, :] * axial[None, :, :]).reshape(NODES, slots))
    places = az_elem[...].reshape(1, 1, LANES)
    element = lax.broadcasted_iota(jnp.int32, (LANES // P_SIZE, P_SIZE, LANES), 0)
    girth[...] = jnp.where(element == places, az_weights[...][None], 0.0).reshape(LANES, LANES)
    used = ids >= 0
    target = jnp.where(used, lax.shift_right_logical(ids, 4), -1).astype(F32)
    across = jnp.broadcast_to(target, (slots, slots))
    down = jnp.transpose(across)
    before = lax.broadcasted_iota(jnp.int32, across.shape, 0) < lax.broadcasted_iota(
        jnp.int32, across.shape, 1
    )
    rank = jnp.sum(jnp.where((across == down) & before, 1.0, 0.0), axis=0, keepdims=True)
    position = jnp.where(used & (rank < SLOTS - 1.5), target * SLOTS + rank, -1.0)
    wanted = lax.broadcasted_iota(jnp.int32, select.shape, 0).astype(F32)
    select[...] = jnp.where(wanted == position, 1.0, 0.0)
    number = (ids & (ROWS_DEV - 1)).astype(F32) + 1.0
    owners = lax.broadcasted_iota(jnp.int32, (header.shape[0], slots), 0).astype(F32)
    named = jnp.where(owners == target, number, 0.0).astype(BF16)
    ranks = lax.broadcasted_iota(jnp.int32, (LANES, slots), 0).astype(F32)
    placed = jnp.where(ranks == rank, 1.0, 0.0).astype(BF16)
    numbers = lax.dot_general(
        named, placed, (((1,), (1,)), ((), ())), preferred_element_type=F32
    )
    overflow = jnp.max(jnp.where(used & (rank > SLOTS - 1.5), 1.0, 0.0), axis=1, keepdims=True)
    lane = lax.broadcasted_iota(jnp.int32, header.shape, 1)
    header[...] = jnp.where(
        lane >= SLOTS, overflow, jnp.where(lane < SLOTS - 1, numbers, 0.0)
    )


def unpack_kernel(pieces, out, crowded):
    sources = pieces.shape[0]
    heads = pieces[:, 0:SLOTS, :]
    head = jnp.broadcast_to(heads[:, SLOTS - 1 : SLOTS, :], heads.shape)
    place = lax.broadcasted_iota(jnp.int32, heads.shape, 1)
    lane = lax.broadcasted_iota(jnp.int32, heads.shape, 2)
    mine = jnp.where((lane == place) & (place < SLOTS - 1), head, 0.0)
    crowded[0, 0] = jnp.max(jnp.where(lane >= SLOTS, head, 0.0)).astype(jnp.int32)
    row = jnp.sum(mine.reshape(sources * SLOTS, LANES), axis=1, keepdims=True)
    column = lax.broadcasted_iota(jnp.int32, (sources * SLOTS, LANES), 1).astype(F32)
    chosen = jnp.transpose(jnp.where(row == column + 1.0, 1.0, 0.0))[:ROWS_DEV].astype(BF16)
    both = jnp.concatenate([chosen, chosen], axis=1)
    for c in range(C):
        x = pieces[:, c * SLOTS : (c + 1) * SLOTS, :].reshape(sources * SLOTS, LANES)
        high, low = split(x)
        out[c * ROWS_DEV : (c + 1) * ROWS_DEV, :] = dot(
            both, jnp.concatenate([high, low], axis=0)
        )


def dft_kernel(rows, phase, table_high, table_low, out):
    turn_re = phase[0:1, :]
    turn_im = phase[1:2, :]
    total = None
    for pair in range(8):
        x = jnp.concatenate([rows[2 * pair], rows[2 * pair + 1]], axis=1)
        z = jnp.concatenate([x * twice(turn_re), x * twice(turn_im)], axis=0)
        high, low = split(z)
        block = pl.ds(pair * 256, 256)
        th, tl = table_high[block, :], table_low[block, :]
        first = dot(jnp.concatenate([high, low], axis=0), th)
        half = first.shape[0] // 2
        part = first[:half] + first[half:] + dot(high, tl)
        total = part if total is None else total + part
    n = C * ROWS_DEV
    re = total[:n, :LANES] + total[n:, LANES:]
    im = total[n:, :LANES] - total[:n, LANES:]
    for c in range(C):
        out[0, :, c, :] = re[c * ROWS_DEV : (c + 1) * ROWS_DEV]
        out[1, :, c, :] = im[c * ROWS_DEV : (c + 1) * ROWS_DEV]


def call(kernel, shapes, flops, *args):
    vmem = pl.BlockSpec(memory_space=pltpu.VMEM)
    out_shape = [jax.ShapeDtypeStruct(s, F32) for s in shapes]
    return pl.pallas_call(
        kernel,
        out_shape=out_shape,
        in_specs=[vmem] * len(args),
        out_specs=[vmem] * len(shapes),
        compiler_params=pltpu.CompilerParams(vmem_limit_bytes=VMEM_LIMIT),
        cost_estimate=pl.CostEstimate(flops=flops, bytes_accessed=2000000, transcendentals=0),
    )(*args)


def pack_halos(*args):
    hbm, vmem = [pl.BlockSpec(memory_space=m) for m in (pltpu.HBM, pltpu.VMEM)]
    return pl.pallas_call(
        pack_kernel,
        out_shape=[jax.ShapeDtypeStruct((2, NODES, LANES), F32)] * 2,
        in_specs=[hbm] * len(args),
        out_specs=[vmem] * 2,
        scratch_shapes=[pltpu.VMEM(x.shape, F32) for x in args]
        + [pltpu.SemaphoreType.DMA((len(args),))],
        compiler_params=pltpu.CompilerParams(vmem_limit_bytes=LOAD_LIMIT),
    )(*args)


def body(
    field, geometry, mass, cycle_id, cycle_radial, cycle_axial, cycle_weights, az_elem, az_weights
):
    axial_count, girth_count = lax.axis_size("axial"), lax.axis_size("girth")
    up = [(i, i + 1) for i in range(axial_count - 1)]
    down = [(j, i) for i, j in up]
    around = [(i, (i + 1) % girth_count) for i in range(girth_count)]
    back = [(j, i) for i, j in around]
    field = field.reshape(C, NODES, LANES)
    geom = geometry.reshape(3, NODES, LANES)
    mass = mass.reshape(NODES, LANES)
    table = jnp.asarray(stiffness_table())
    to_right, to_left = pack_halos(field, geom, mass)
    tile_flops = 18 * 2 * 256**3

    left = lax.ppermute(to_right, "girth", around)
    right = lax.ppermute(to_left, "girth", back)
    (own_total,) = call(own_kernel, [(NODES, C * LANES)], 2 * tile_flops, field, geom, table)

    def exchange(low, high):
        return lax.ppermute(high, "axial", up), lax.ppermute(low, "axial", down)

    whole, narrow = (NODES, WIDE), (NODES, NARROW)
    face_static, sent = (16, STATIC + 4 * NARROW), (16, FIRST_SENT + 6 * LANES)
    halo_geom, state, lumped, ends, low, high, send_low, send_high = call(
        halo_kernel,
        [(3, NODES, 2 * LANES), whole, narrow, narrow, face_static, face_static, sent, sent],
        2 * tile_flops,
        left,
        right,
        own_total,
        field,
        mass,
        geom,
        table,
    )
    got_low, got_high = exchange(send_low, send_high)
    (second,) = call(second_kernel, [whole], 3 * tile_flops, state, geom, halo_geom, table)
    state, inverse, own_low, own_high, send_low, send_high = call(
        middle_kernel,
        [whole, narrow, (16, STATIC), (16, STATIC), (16, SECOND_SENT), (16, SECOND_SENT)],
        4 * tile_flops,
        state,
        second,
        lumped,
        ends,
        low,
        high,
        got_low,
        got_high,
        geom,
        halo_geom,
        table,
    )
    new_low, new_high = exchange(send_low, send_high)
    (second,) = call(second_kernel, [whole], 3 * tile_flops, state, geom, halo_geom, table)

    slot_count = cycle_id.shape[0]
    slab, girth_weight, select, header = call(
        weights_kernel,
        [
            (slot_count, NODES),
            (LANES, LANES),
            (SLOTS * axial_count, slot_count),
            (axial_count, LANES),
        ],
        1000000,
        cycle_id,
        cycle_radial,
        cycle_axial,
        cycle_weights,
        az_elem,
        az_weights,
    )

    final, packed, probes = call(
        last_kernel,
        [(C, NODES, LANES), (axial_count, C * SLOTS, LANES), (slot_count, C * LANES)],
        tile_flops,
        state,
        second,
        inverse,
        ends,
        low,
        high,
        got_low,
        got_high,
        own_low,
        own_high,
        new_low,
        new_high,
        slab,
        girth_weight,
        select,
        header,
        table,
    )
    pieces = lax.all_to_all(packed, "axial", 0, 0)

    vmem = pl.BlockSpec(memory_space=pltpu.VMEM)
    rows, crowded = pl.pallas_call(
        unpack_kernel,
        out_shape=[
            jax.ShapeDtypeStruct((C * ROWS_DEV, LANES), F32),
            jax.ShapeDtypeStruct((1, 1), jnp.int32),
        ],
        in_specs=[vmem],
        out_specs=[vmem, pl.BlockSpec(memory_space=pltpu.SMEM)],
        compiler_params=pltpu.CompilerParams(vmem_limit_bytes=VMEM_LIMIT),
    )(pieces)

    def dense(rows, probes, cycle_id):
        wanted = jnp.arange(ROWS_DEV * axial_count, dtype=jnp.int32)
        chosen = (wanted[:, None] == cycle_id[None, :]).astype(F32)
        rows = jnp.dot(chosen, probes, precision=lax.Precision.HIGHEST)
        rows = rows.reshape(axial_count, ROWS_DEV, C * LANES)
        rows = jnp.sum(lax.all_to_all(rows, "axial", 0, 0), axis=0)
        return rows.reshape(ROWS_DEV, C, LANES).swapaxes(0, 1).reshape(C * ROWS_DEV, LANES)

    rows = lax.cond(
        crowded[0, 0] > 0, dense, lambda rows, *_: rows, rows, probes, cycle_id
    )
    rows = lax.all_gather(rows, "girth")
    table_high, table_low, phases = dft_tables()
    phase = lax.dynamic_index_in_dim(
        jnp.asarray(phases), lax.axis_index("girth"), 0, keepdims=False
    )
    (spectrum,) = call(
        dft_kernel,
        [(2, ROWS_DEV, C, LANES)],
        tile_flops,
        rows,
        phase,
        jnp.asarray(table_high),
        jnp.asarray(table_low),
    )
    return final.reshape(C, 16, 16, LANES), spectrum


def solution(mesh):
    return jax.shard_map(
        body,
        mesh=mesh,
        in_specs=(
            P(None, None, "axial", "girth"),
            P(None, None, "axial", "girth"),
            P(None, "axial", "girth"),
            P("axial"),
            P("axial"),
            P("axial"),
            P(None, None, "axial"),
            P("girth"),
            P(None, "girth"),
        ),
        out_specs=(P(None, None, "axial", "girth"), P(None, "axial", None, "girth")),
        check_vma=False,
    )
```

```python
import math

import jax
import jax.numpy as jnp
import ml_dtypes
import numpy as np
from jax import lax
from jax.experimental import pallas as pl
from jax.experimental.pallas import tpu as pltpu
from jax.sharding import PartitionSpec as P

C = 4
P_SIZE = 8
LANES = 128
HALO = 32
NODES = 256
WIDE = 6 * LANES
ROWS_DEV = 16
SLOTS = 8
VMEM_LIMIT = 32 * 1024 * 1024
LOAD_LIMIT = 60000000
F32 = jnp.float32
BF16 = jnp.bfloat16

LOBATTO = (
    -1.0,
    -0.8717401485096066,
    -0.5917001814331423,
    -0.2092992179024789,
    0.2092992179024789,
    0.5917001814331423,
    0.8717401485096066,
    1.0,
)


def derivative_table():
    node_count = len(LOBATTO)
    barycentric = []
    for row_index in range(node_count):
        product = 1.0
        for col_index in range(node_count):
            if col_index != row_index:
                product = product * (LOBATTO[row_index] - LOBATTO[col_index])
        barycentric.append(1.0 / product)
    table_rows = []
    for row_index in range(node_count):
        entries = []
        for col_index in range(node_count):
            if col_index != row_index:
                entries.append(
                    barycentric[col_index]
                    / barycentric[row_index]
                    / (LOBATTO[row_index] - LOBATTO[col_index])
                )
            else:
                entries.append(0.0)
        entries[row_index] = -sum(entries)
        table_rows.append(entries)
    return np.asarray(table_rows, np.float32)


def np_split(table):
    table = np.asarray(table, np.float32)
    high = table.astype(ml_dtypes.bfloat16)
    low = (table - high.astype(np.float32)).astype(ml_dtypes.bfloat16)
    return high, low


def stiffness_table():
    d = derivative_table()
    eye = lambda n: np.eye(n, dtype=np.float32)
    axial = np.kron(eye(32), d)
    blocks = list(np_split(axial)) + list(np_split(axial.T))
    ends = axial.T.reshape(16, 16, NODES)[:, [0, 15]].swapaxes(0, 1).reshape(32, NODES)
    blocks += list(np_split(ends))
    for small in (np.kron(eye(4), d), np.kron(eye(8), d.T), np.kron(eye(4), d.T)):
        high, low = np_split(small)
        row = np.concatenate([high, high, low], axis=1)
        blocks.append(np.pad(row, ((0, 0), (0, NODES - row.shape[1]))))
    return np.concatenate(blocks, axis=0)


def dft_tables():
    a = np.arange(2048)[:, None]
    m = np.arange(LANES)[None, :]
    angle = 2.0 * np.pi * ((a * m) % 2048) / 2048.0
    table = np.concatenate([np.cos(angle), np.sin(angle)], axis=1)
    high, low = np_split(table)
    k = np.arange(16)[:, None]
    lane = np.arange(LANES)[None, :]
    turn = 2.0 * np.pi * ((k * lane) % 16) / 16.0
    phase = np.stack([np.cos(turn), -np.sin(turn)], axis=1) / math.sqrt(2048.0)
    return high, low, phase.astype(np.float32)


def split(x):
    high = x.astype(BF16)
    return high, (x - high.astype(F32)).astype(BF16)


def dot(a, b):
    return jnp.dot(a, b, preferred_element_type=F32)


def left_mul(table, x):
    high, low = split(x)
    return dot(table, jnp.concatenate([high, low, high], axis=0))


def right_mul(x, table):
    high, low = split(x)
    return dot(jnp.concatenate([high, low, high], axis=1), table)


def square(table, k):
    return table[k * NODES : (k + 1) * NODES, :]


def axial_left(table):
    return jnp.concatenate([square(table, 0), square(table, 0), square(table, 1)], axis=1)


def axial_left_t(table):
    return jnp.concatenate([square(table, 2), square(table, 2), square(table, 3)], axis=1)


def girth_right(table):
    return jnp.concatenate([square(table, 2), square(table, 2), square(table, 3)], axis=0)


def girth_right_t(table):
    return jnp.concatenate([square(table, 0), square(table, 0), square(table, 1)], axis=0)


SMALL = 4 * NODES


def ends_pair(table):
    return table[SMALL : SMALL + 64, :]


def radial_small(table):
    return table[SMALL + 64 : SMALL + 96, :96]


def radial_small_t(table):
    return table[SMALL + 96 : SMALL + 160, :192]


def radial_faces_t(table):
    return table[SMALL + 160 : SMALL + 192, :96]


def radial_apply(x, matrix):
    half = P_SIZE // 2
    odd_rows = 0.5 * (matrix[:half, :half] - matrix[:half, : half - 1 : -1])
    even_rows = 0.5 * (matrix[:half, :half] + matrix[:half, : half - 1 : -1])
    outs = {}
    for element in range(2):
        for part in range(2):
            for tile in range(x.shape[1] // LANES):
                nodes = []
                for i in range(P_SIZE):
                    row = (element * P_SIZE + i) * 16 + part * 8
                    nodes.append(x[row : row + 8, tile * LANES : (tile + 1) * LANES])
                even = [nodes[j] + nodes[P_SIZE - 1 - j] for j in range(half)]
                odd = [nodes[j] - nodes[P_SIZE - 1 - j] for j in range(half)]
                for i in range(half):
                    p = float(odd_rows[i, 0]) * odd[0]
                    q = float(even_rows[i, 0]) * even[0]
                    for j in range(1, half):
                        p = p + float(odd_rows[i, j]) * odd[j]
                        q = q + float(even_rows[i, j]) * even[j]
                    outs[element * P_SIZE + i, part, tile] = p + q
                    outs[element * P_SIZE + P_SIZE - 1 - i, part, tile] = p - q
    columns = []
    for tile in range(x.shape[1] // LANES):
        columns.append(
            jnp.concatenate([outs[i, part, tile] for i in range(16) for part in range(2)], axis=0)
        )
    return jnp.concatenate(columns, axis=1)


def end_columns(rows):
    d = derivative_table()
    values = [float(x) for x in np.concatenate([d[:, 0], d[:, 7]])]
    node = lax.broadcasted_iota(jnp.int32, (16, LANES), 0)
    column = jnp.full((16, LANES), values[0], F32)
    for k in range(1, 16):
        column = jnp.where(node == k, values[k], column)
    return jnp.broadcast_to(column[None], (16, 16, LANES)).reshape(rows, LANES)


def stiff_many(us, geoms, table):
    d = derivative_table()
    halves = [split(u) for u in us]
    rows = [jnp.concatenate([high, low, high], axis=1) for high, low in halves]
    girth = dot(jnp.concatenate(rows, axis=0), girth_right(table))
    girth = girth * jnp.concatenate([g[2] for g in geoms], axis=0)
    girth = right_mul(girth, girth_right_t(table))
    outs = []
    for k, (u, (high, low), (gr, ga, _)) in enumerate(zip(us, halves, geoms)):
        axial = dot(axial_left(table), jnp.concatenate([high, low, high], axis=0)) * ga
        radial = radial_apply(radial_apply(u, d) * gr, d.T)
        part = girth[k * NODES : (k + 1) * NODES]
        outs.append(left_mul(axial_left_t(table), axial) + part + radial)
    return outs


def left_pair(both, x):
    high, low = split(x)
    rows = both.shape[0] // 2
    first = dot(both, high)
    return first[:rows] + first[rows:] + dot(both[:rows], low)


def girth_faces(x, factor, repeat, table):
    rows = x.shape[0]
    stacked = jnp.concatenate([x[:, k * NODES : (k + 1) * NODES] for k in range(3)], axis=0)
    slope = right_mul(stacked, girth_right(table))
    scaled = []
    for k in range(3):
        part = slope[k * rows : (k + 1) * rows]
        part = jnp.concatenate([part] * repeat, axis=0)
        scaled.append(part * factor[:, k * NODES : (k + 1) * NODES])
    moved = right_mul(jnp.concatenate(scaled, axis=0), girth_right_t(table))
    rows = rows * repeat
    return jnp.concatenate([moved[k * rows : (k + 1) * rows] for k in range(3)], axis=1)


def twice(x):
    return jnp.concatenate([x, x], axis=1)


def sum_nodes(t):
    width = t.shape[1]
    v = t.reshape(16, 16, width)
    mid = v[7:8] + v[8:9]
    v = jnp.concatenate([v[:7], mid, mid, v[9:]], axis=0)
    pair = v[:, 7:8, :] + v[:, 8:9, :]
    node = lax.broadcasted_iota(jnp.int32, v.shape, 1)
    return jnp.where((node == 7) | (node == 8), pair, v)


def sum_girth(own, left, right, owners=None):
    lane = lax.broadcasted_iota(jnp.int32, left.shape, 1)
    first = lane % P_SIZE == 0
    last = lane % P_SIZE == P_SIZE - 1

    def inner(x):
        return jnp.where(
            first, pltpu.roll(x, 1, 1), jnp.where(last, pltpu.roll(x, LANES - 1, 1), 0.0)
        )

    sums = []
    for c, x in enumerate(own):
        p = inner(x)
        p = jnp.where(lane == 0, pltpu.roll(left, (LANES - HALO * c - HALO + 1) % LANES, 1), p)
        p = jnp.where(lane == LANES - 1, pltpu.roll(right, (LANES - 1 - HALO * c) % LANES, 1), p)
        sums.append(x + p)
    if owners is None:
        return sums
    p = inner(left)
    q = inner(right)
    for c, x in enumerate(owners):
        p = jnp.where(lane == HALO * c + HALO - 1, pltpu.roll(x, HALO * c + HALO - 1, 1), p)
        q = jnp.where(lane == HALO * c, pltpu.roll(x, (HALO * c + 1) % LANES, 1), q)
    return sums + [left + p, right + q]


def shared_local(parts):
    return jnp.concatenate(sum_girth(parts[:4], parts[4], parts[5], parts[:4]), axis=1)


def lanes_of(x, k):
    return x[:, k * LANES : (k + 1) * LANES]


def pack_kernel(field_in, geom_in, mass_in, to_right, to_left, field, geom, mass, sems):
    copies = [
        pltpu.make_async_copy(field_in, field, sems.at[0]),
        pltpu.make_async_copy(geom_in, geom, sems.at[1]),
        pltpu.make_async_copy(mass_in, mass, sems.at[2]),
    ]
    for copy in copies:
        copy.start()
    lane = lax.broadcasted_iota(jnp.int32, (NODES, LANES), 1)

    def pack(arrays, start):
        out = None
        for k, x in enumerate(arrays):
            moved = pltpu.roll(x, (HALO * k - start) % LANES, 1) if (HALO * k - start) else x
            out = moved if out is None else jnp.where(lane // HALO == k, moved, out)
        return out

    copies[0].wait()
    fields = [field[c] for c in range(C)]
    to_right[0] = pack(fields, LANES - HALO)
    to_left[0] = pack(fields, 0)
    copies[1].wait()
    copies[2].wait()
    others = [geom[k] for k in range(3)] + [mass[...]]
    to_right[1] = pack(others, LANES - HALO)
    to_left[1] = pack(others, 0)


def own_kernel(field, geom, table, out):
    geoms = tuple(twice(geom[k]) for k in range(3))
    us = [jnp.concatenate([field[2 * k], field[2 * k + 1]], axis=1) for k in range(2)]
    out[...] = jnp.concatenate(stiff_many(us, [geoms] * 2, table), axis=1)


def at_faces(low, high, width):
    shape = (16, 16, width)
    node = lax.broadcasted_iota(jnp.int32, shape, 1)
    both = jnp.where(
        node == 0, low[:, None, :], jnp.where(node == 15, high[:, None, :], 0.0)
    )
    return both.reshape(NODES, width)


def wide(x):
    own = lanes_of(x, 0)
    return jnp.concatenate([own] * C + [x[:, LANES:]], axis=1)


def put_faces(x, low, high, offset):
    width = x.shape[1]
    v = x.reshape(16, 16, width)
    low[:, offset : offset + width] = v[:, 0, :]
    high[:, offset : offset + width] = v[:, 15, :]


def action(u, geom, halo_geom, tables):
    own = tuple(twice(geom[k]) for k in range(3))
    geoms = [own, own, tuple(halo_geom[k] for k in range(3))]
    us = [u[:, k * NODES : (k + 1) * NODES] for k in range(3)]
    parts = []
    for t in stiff_many(us, geoms, tables):
        parts += [lanes_of(t, 0), lanes_of(t, 1)]
    return sum_nodes(shared_local(parts)).reshape(NODES, WIDE)


def inner_update(u, total, inverse):
    row = lax.broadcasted_iota(jnp.int32, u.shape, 0) % 16
    return jnp.where((row == 0) | (row == 15), u, u - total * wide(inverse))


def sum_faces(x):
    summed = shared_local([lanes_of(x, k) for k in range(6)]).reshape(2, 16, WIDE)
    pair = summed[:, 7:8, :] + summed[:, 8:9, :]
    node = lax.broadcasted_iota(jnp.int32, summed.shape, 1)
    return jnp.where((node == 7) | (node == 8), pair, summed)


def face_action(v, geom, halo_geom, statics, table):
    low, high = statics
    radial, girthwise = [
        wide(jnp.concatenate([static_part(low, k), static_part(high, k)], axis=0)) for k in (1, 2)
    ]
    nodes = v.reshape(16, 16, WIDE)
    ends = jnp.concatenate([nodes[:, 0, :], nodes[:, 15, :]], axis=0)
    face = left_mul(radial_faces_t(table), left_mul(radial_small(table), ends) * radial)
    face = face + girth_faces(ends, girthwise, 1, table)
    pieces = []
    for tile in range(3):
        ga = halo_geom[1] if tile == 2 else twice(geom[1])
        slope = left_pair(table[: 2 * NODES, :], v[:, tile * NODES : (tile + 1) * NODES]) * ga
        pieces.append(left_pair(ends_pair(table), slope))
    return sum_faces(face + jnp.concatenate(pieces, axis=1))


def two_steps(u, geom, halo_geom, inverse, first, statics, table, state, low, high):
    v = inner_update(u, first, inverse)
    state[...] = v
    put_faces(first, low, high, 0)
    faces = face_action(v, geom, halo_geom, statics, table)
    low[:, WIDE : 2 * WIDE] = faces[0]
    high[:, WIDE : 2 * WIDE] = faces[1]


def second_kernel(state, geom, halo_geom, table, out):
    out[...] = action(state[...], geom, halo_geom, table)


STATIC = 2 * WIDE
NARROW = 3 * LANES


def spread(x, k):
    lane = lax.broadcasted_iota(jnp.int32, x.shape, 1)
    y = jnp.where(lane // HALO == k, x, 0.0)
    y = y + pltpu.roll(y, HALO, 1)
    return y + pltpu.roll(y, 2 * HALO, 1)


OWN = C * LANES
FIRST_SENT = WIDE + OWN + LANES
SECOND_SENT = OWN + LANES + OWN


def near(shape):
    return lax.broadcasted_iota(jnp.int32, shape, 1) % HALO >= HALO // 2


def join_halves(x):
    return jnp.where(near((16, LANES)), x[:, :LANES], x[:, LANES:])


def part_halves(x):
    inside = near(x.shape)
    return [jnp.where(inside, x, 0.0), jnp.where(inside, 0.0, x)]


def to_send(face, out):
    out[:, : WIDE + OWN] = face[:, : WIDE + OWN]
    out[:, WIDE + OWN : FIRST_SENT] = join_halves(face[:, WIDE + OWN : STATIC])
    lane = lax.broadcasted_iota(jnp.int32, (16, LANES), 1) // HALO
    for k in range(4):
        at = FIRST_SENT + k * LANES
        out[:, at : at + LANES] = static_part(face, k)[:, :LANES]
    for k in range(2):
        parts = []
        for j in (2 * k, 2 * k + 1):
            parts += [static_part(face, j)[:, LANES : 2 * LANES], static_part(face, j)[:, 2 * LANES :]]
        block = parts[3]
        for j in range(3):
            block = jnp.where(lane == j, parts[j], block)
        at = FIRST_SENT + (4 + k) * LANES
        out[:, at : at + LANES] = block


def as_sent(got):
    pieces = [got[:, : WIDE + OWN]] + part_halves(got[:, WIDE + OWN : FIRST_SENT])
    for k in range(4):
        at = FIRST_SENT + (4 + k // 2) * LANES
        halos = got[:, at : at + LANES]
        place = 2 * (k % 2)
        pieces.append(got[:, FIRST_SENT + k * LANES : FIRST_SENT + (k + 1) * LANES])
        pieces += [spread(halos, place), spread(halos, place + 1)]
    return jnp.concatenate(pieces, axis=1)


def to_send_second(face, out):
    out[:, :OWN] = face[:, :OWN]
    out[:, OWN : OWN + LANES] = join_halves(face[:, OWN:WIDE])
    out[:, OWN + LANES :] = face[:, WIDE : WIDE + OWN]


def second_as_sent(got):
    pieces = [got[:, :OWN]] + part_halves(got[:, OWN : OWN + LANES])
    pieces += [got[:, OWN + LANES :], jnp.zeros((16, 2 * LANES), F32)]
    return jnp.concatenate(pieces, axis=1)


def halo_kernel(
    left, right, own_total, field, mass, geom, tables, halo_geom, state, mass_out, ends_out, low, high, *sent
):
    left_others, right_others = left[1], right[1]
    geoms = []
    for k in range(3):
        g = jnp.concatenate([spread(left_others, k), spread(right_others, k)], axis=1)
        halo_geom[k] = g
        geoms.append(g)
    u = jnp.concatenate([left[0], right[0]], axis=1)
    (t,) = stiff_many([u], [tuple(geoms)], tables)
    parts = [own_total[:, c * LANES : (c + 1) * LANES] for c in range(C)]
    first = sum_nodes(shared_local(parts + [lanes_of(t, 0), lanes_of(t, 1)]))
    first = first.reshape(NODES, WIDE)
    m = mass[...]
    masses = sum_girth([m], spread(left_others, 3), spread(right_others, 3), [m] * C)
    lumped = sum_nodes(jnp.concatenate(masses, axis=1)).reshape(NODES, NARROW)
    mass_out[...] = lumped
    whole = [jnp.concatenate([geom[k], geoms[k]], axis=1) for k in range(3)]
    end = end_columns(NODES)
    ends = left_mul(axial_left_t(tables), whole[1] * jnp.concatenate([end] * 3, axis=1))
    ends_out[...] = ends
    for k, x in enumerate([lumped, whole[0], whole[2], ends]):
        put_faces(x, low, high, STATIC + k * NARROW)
    start = jnp.concatenate([field[c] for c in range(C)] + [u], axis=1)
    two_steps(start, geom, halo_geom, 1.0 / lumped, first, (low, high), tables, state, low, high)
    to_send(low, sent[0])
    to_send(high, sent[1])


def static_part(ref, k):
    return ref[:, STATIC + k * NARROW : STATIC + (k + 1) * NARROW]


def finish_pair(state, second, inverse, ends, statics, own, got, tables, lanes=WIDE):
    low, high, got_low, got_high = statics
    own_low, own_high = own
    new_low, new_high = got
    w_low = -(own_low[:, :WIDE] + new_low[:, :WIDE]) * wide(
        1.0 / (static_part(low, 0) + static_part(got_low, 0))
    )
    w_high = -(own_high[:, :WIDE] + new_high[:, :WIDE]) * wide(
        1.0 / (static_part(high, 0) + static_part(got_high, 0))
    )
    w = jnp.concatenate([w_low, w_high], axis=0)
    radial, girthwise = [
        wide(jnp.concatenate([static_part(ref, k) for ref in statics], axis=0)) for k in (1, 2)
    ]
    slope = left_mul(radial_small(tables), w)
    face = left_mul(radial_small_t(tables), jnp.concatenate([slope, slope], axis=0) * radial)
    face = face + girth_faces(w, girthwise, 2, tables)
    other = jnp.concatenate([static_part(got_low, 3), static_part(got_high, 3)], axis=0)
    beyond = face[32:] + wide(other) * w
    beyond = sum_faces(beyond)
    beyond_low = beyond[0] + new_low[:, WIDE : 2 * WIDE]
    beyond_high = beyond[1] + new_high[:, WIDE : 2 * WIDE]
    node = lax.broadcasted_iota(jnp.int32, (16, 16, WIDE), 1)
    along = jnp.where(node < P_SIZE, w_low[:, None, :], w_high[:, None, :])
    change = wide(ends) * along.reshape(NODES, WIDE) + at_faces(face[:16], face[16:32], WIDE)
    parts = [lanes_of(change, k) for k in range(6)]
    owners = parts[:4] if lanes == WIDE else None
    summed = sum_girth(parts[:4], parts[4], parts[5], owners)
    change = sum_nodes(jnp.concatenate(summed, axis=1)).reshape(NODES, lanes)
    beyond = at_faces(beyond_low[:, :lanes], beyond_high[:, :lanes], lanes)
    total = second[:, :lanes] + change + beyond
    moved = state[:, :lanes] + at_faces(w_low[:, :lanes], w_high[:, :lanes], lanes)
    return moved - total * wide(inverse)[:, :lanes]


def middle_kernel(state, second, lumped, ends, low, high, got_low, got_high, geom, halo_geom, *refs):
    tables, state_out, inverse_out, next_low, next_high, *sent = refs
    got_low, got_high = as_sent(got_low), as_sent(got_high)
    inverse = 1.0 / (
        lumped[...] + at_faces(static_part(got_low, 0), static_part(got_high, 0), NARROW)
    )
    inverse_out[...] = inverse
    statics = (low, high, got_low, got_high)
    u = finish_pair(
        state[...], second[...], inverse, ends[...], statics, (low, high), (got_low, got_high), tables
    )
    first = action(u, geom, halo_geom, tables)
    two_steps(u, geom, halo_geom, inverse, first, (low, high), tables, state_out, next_low, next_high)
    to_send_second(next_low, sent[0])
    to_send_second(next_high, sent[1])


def last_kernel(
    state,
    second,
    inverse,
    ends,
    low,
    high,
    got_low,
    got_high,
    own_low,
    own_high,
    new_low,
    new_high,
    slab,
    girth_weight,
    select,
    header,
    tables,
    out,
    packed,
    probes_out,
):
    u = finish_pair(
        state[...],
        second[...],
        inverse[...],
        ends[...],
        (low, high, as_sent(got_low), as_sent(got_high)),
        (own_low, own_high),
        (second_as_sent(new_low), second_as_sent(new_high)),
        tables,
        C * LANES,
    )
    for c in range(C):
        out[c] = lanes_of(u, c)
    slab_high, slab_low = split(slab[...])
    values = left_pair(jnp.concatenate([slab_high, slab_low], axis=0), u)
    stacked = jnp.concatenate([lanes_of(values, c) for c in range(C)], axis=0)
    weight_high, weight_low = split(girth_weight[...])
    weights = jnp.concatenate([weight_high, weight_high, weight_low], axis=0)
    probes = right_mul(stacked, weights)
    slots = slab.shape[0]
    spread = jnp.concatenate([probes[c * slots : (c + 1) * slots] for c in range(C)], axis=1)
    probes_out[...] = spread
    high_part, low_part = split(spread)
    chosen = select[...].astype(BF16)
    rows = dot(
        jnp.concatenate([chosen, chosen], axis=1),
        jnp.concatenate([high_part, low_part], axis=0),
    )
    for c in range(C):
        block = lanes_of(rows, c).reshape(-1, SLOTS, LANES)
        if c == 0:
            place = lax.broadcasted_iota(jnp.int32, block.shape, 1)
            block = jnp.where(place == SLOTS - 1, header[...][:, None, :], block)
        packed[:, c * SLOTS : (c + 1) * SLOTS, :] = block


def weights_kernel(
    cycle_id, cycle_radial, cycle_axial, cycle_weights, az_elem, az_weights, slab, girth, select, header
):
    slots = cycle_id.shape[0]
    ids = cycle_id[...].reshape(1, slots)
    in_radial, in_axial = [x[...].reshape(1, slots) for x in (cycle_radial, cycle_axial)]
    radial, axial = [
        jnp.concatenate(
            [jnp.where(owner == e, cycle_weights[k], 0.0) for e in range(2)], axis=0
        )
        for k, owner in enumerate((in_radial, in_axial))
    ]
    slab[...] = jnp.transpose((radial[:, None, :] * axial[None, :, :]).reshape(NODES, slots))
    places = az_elem[...].reshape(1, 1, LANES)
    element = lax.broadcasted_iota(jnp.int32, (LANES // P_SIZE, P_SIZE, LANES), 0)
    girth[...] = jnp.where(element == places, az_weights[...][None], 0.0).reshape(LANES, LANES)
    used = ids >= 0
    target = jnp.where(used, lax.shift_right_logical(ids, 4), -1).astype(F32)
    across = jnp.broadcast_to(target, (slots, slots))
    down = jnp.transpose(across)
    before = lax.broadcasted_iota(jnp.int32, across.shape, 0) < lax.broadcasted_iota(
        jnp.int32, across.shape, 1
    )
    rank = jnp.sum(jnp.where((across == down) & before, 1.0, 0.0), axis=0, keepdims=True)
    position = jnp.where(used & (rank < SLOTS - 1.5), target * SLOTS + rank, -1.0)
    wanted = lax.broadcasted_iota(jnp.int32, select.shape, 0).astype(F32)
    select[...] = jnp.where(wanted == position, 1.0, 0.0)
    number = (ids & (ROWS_DEV - 1)).astype(F32) + 1.0
    owners = lax.broadcasted_iota(jnp.int32, (header.shape[0], slots), 0).astype(F32)
    named = jnp.where(owners == target, number, 0.0).astype(BF16)
    ranks = lax.broadcasted_iota(jnp.int32, (LANES, slots), 0).astype(F32)
    placed = jnp.where(ranks == rank, 1.0, 0.0).astype(BF16)
    numbers = lax.dot_general(
        named, placed, (((1,), (1,)), ((), ())), preferred_element_type=F32
    )
    overflow = jnp.max(jnp.where(used & (rank > SLOTS - 1.5), 1.0, 0.0), axis=1, keepdims=True)
    lane = lax.broadcasted_iota(jnp.int32, header.shape, 1)
    header[...] = jnp.where(
        lane >= SLOTS, overflow, jnp.where(lane < SLOTS - 1, numbers, 0.0)
    )


def unpack_kernel(pieces, out, crowded):
    sources = pieces.shape[0]
    heads = pieces[:, 0:SLOTS, :]
    head = jnp.broadcast_to(heads[:, SLOTS - 1 : SLOTS, :], heads.shape)
    place = lax.broadcasted_iota(jnp.int32, heads.shape, 1)
    lane = lax.broadcasted_iota(jnp.int32, heads.shape, 2)
    mine = jnp.where((lane == place) & (place < SLOTS - 1), head, 0.0)
    crowded[0, 0] = jnp.max(jnp.where(lane >= SLOTS, head, 0.0)).astype(jnp.int32)
    row = jnp.sum(mine.reshape(sources * SLOTS, LANES), axis=1, keepdims=True)
    column = lax.broadcasted_iota(jnp.int32, (sources * SLOTS, LANES), 1).astype(F32)
    chosen = jnp.transpose(jnp.where(row == column + 1.0, 1.0, 0.0))[:ROWS_DEV].astype(BF16)
    both = jnp.concatenate([chosen, chosen], axis=1)
    columns = [
        pieces[:, c * SLOTS : (c + 1) * SLOTS, :].reshape(sources * SLOTS, LANES) for c in range(C)
    ]
    high, low = split(jnp.concatenate(columns, axis=1))
    rows = dot(both, jnp.concatenate([high, low], axis=0))
    for c in range(C):
        out[c * ROWS_DEV : (c + 1) * ROWS_DEV, :] = lanes_of(rows, c)


def dft_kernel(rows, phase, table_high, table_low, out):
    turn_re = phase[0:1, :]
    turn_im = phase[1:2, :]
    total = None
    for pair in range(8):
        x = jnp.concatenate([rows[2 * pair], rows[2 * pair + 1]], axis=1)
        z = jnp.concatenate([x * twice(turn_re), x * twice(turn_im)], axis=0)
        high, low = split(z)
        block = pl.ds(pair * 256, 256)
        th, tl = table_high[block, :], table_low[block, :]
        first = dot(jnp.concatenate([high, low], axis=0), th)
        half = first.shape[0] // 2
        part = first[:half] + first[half:] + dot(high, tl)
        total = part if total is None else total + part
    n = C * ROWS_DEV
    re = total[:n, :LANES] + total[n:, LANES:]
    im = total[n:, :LANES] - total[:n, LANES:]
    for c in range(C):
        out[0, :, c, :] = re[c * ROWS_DEV : (c + 1) * ROWS_DEV]
        out[1, :, c, :] = im[c * ROWS_DEV : (c + 1) * ROWS_DEV]


def call(kernel, shapes, flops, *args):
    vmem = pl.BlockSpec(memory_space=pltpu.VMEM)
    out_shape = [jax.ShapeDtypeStruct(s, F32) for s in shapes]
    return pl.pallas_call(
        kernel,
        out_shape=out_shape,
        in_specs=[vmem] * len(args),
        out_specs=[vmem] * len(shapes),
        compiler_params=pltpu.CompilerParams(vmem_limit_bytes=VMEM_LIMIT),
        cost_estimate=pl.CostEstimate(flops=flops, bytes_accessed=2000000, transcendentals=0),
    )(*args)


def pack_halos(*args):
    hbm, vmem = [pl.BlockSpec(memory_space=m) for m in (pltpu.HBM, pltpu.VMEM)]
    return pl.pallas_call(
        pack_kernel,
        out_shape=[jax.ShapeDtypeStruct((2, NODES, LANES), F32)] * 2,
        in_specs=[hbm] * len(args),
        out_specs=[vmem] * 2,
        scratch_shapes=[pltpu.VMEM(x.shape, F32) for x in args]
        + [pltpu.SemaphoreType.DMA((len(args),))],
        compiler_params=pltpu.CompilerParams(vmem_limit_bytes=LOAD_LIMIT),
    )(*args)


def body(
    field, geometry, mass, cycle_id, cycle_radial, cycle_axial, cycle_weights, az_elem, az_weights
):
    axial_count, girth_count = lax.axis_size("axial"), lax.axis_size("girth")
    up = [(i, i + 1) for i in range(axial_count - 1)]
    down = [(j, i) for i, j in up]
    around = [(i, (i + 1) % girth_count) for i in range(girth_count)]
    back = [(j, i) for i, j in around]
    field = field.reshape(C, NODES, LANES)
    geom = geometry.reshape(3, NODES, LANES)
    mass = mass.reshape(NODES, LANES)
    table = jnp.asarray(stiffness_table())
    to_right, to_left = pack_halos(field, geom, mass)
    tile_flops = 18 * 2 * 256**3

    left = lax.ppermute(to_right, "girth", around)
    right = lax.ppermute(to_left, "girth", back)
    (own_total,) = call(own_kernel, [(NODES, C * LANES)], 2 * tile_flops, field, geom, table)

    def exchange(low, high):
        return lax.ppermute(high, "axial", up), lax.ppermute(low, "axial", down)

    whole, narrow = (NODES, WIDE), (NODES, NARROW)
    face_static, sent = (16, STATIC + 4 * NARROW), (16, FIRST_SENT + 6 * LANES)
    halo_geom, state, lumped, ends, low, high, send_low, send_high = call(
        halo_kernel,
        [(3, NODES, 2 * LANES), whole, narrow, narrow, face_static, face_static, sent, sent],
        2 * tile_flops,
        left,
        right,
        own_total,
        field,
        mass,
        geom,
        table,
    )
    got_low, got_high = exchange(send_low, send_high)
    (second,) = call(second_kernel, [whole], 3 * tile_flops, state, geom, halo_geom, table)
    state, inverse, own_low, own_high, send_low, send_high = call(
        middle_kernel,
        [whole, narrow, (16, STATIC), (16, STATIC), (16, SECOND_SENT), (16, SECOND_SENT)],
        4 * tile_flops,
        state,
        second,
        lumped,
        ends,
        low,
        high,
        got_low,
        got_high,
        geom,
        halo_geom,
        table,
    )
    new_low, new_high = exchange(send_low, send_high)
    (second,) = call(second_kernel, [whole], 3 * tile_flops, state, geom, halo_geom, table)

    slot_count = cycle_id.shape[0]
    slab, girth_weight, select, header = call(
        weights_kernel,
        [
            (slot_count, NODES),
            (LANES, LANES),
            (SLOTS * axial_count, slot_count),
            (axial_count, LANES),
        ],
        1000000,
        cycle_id,
        cycle_radial,
        cycle_axial,
        cycle_weights,
        az_elem,
        az_weights,
    )

    final, packed, probes = call(
        last_kernel,
        [(C, NODES, LANES), (axial_count, C * SLOTS, LANES), (slot_count, C * LANES)],
        tile_flops,
        state,
        second,
        inverse,
        ends,
        low,
        high,
        got_low,
        got_high,
        own_low,
        own_high,
        new_low,
        new_high,
        slab,
        girth_weight,
        select,
        header,
        table,
    )
    pieces = lax.all_to_all(packed, "axial", 0, 0)

    vmem = pl.BlockSpec(memory_space=pltpu.VMEM)
    rows, crowded = pl.pallas_call(
        unpack_kernel,
        out_shape=[
            jax.ShapeDtypeStruct((C * ROWS_DEV, LANES), F32),
            jax.ShapeDtypeStruct((1, 1), jnp.int32),
        ],
        in_specs=[vmem],
        out_specs=[vmem, pl.BlockSpec(memory_space=pltpu.SMEM)],
        compiler_params=pltpu.CompilerParams(vmem_limit_bytes=VMEM_LIMIT),
    )(pieces)

    def dense(rows, probes, cycle_id):
        wanted = jnp.arange(ROWS_DEV * axial_count, dtype=jnp.int32)
        chosen = (wanted[:, None] == cycle_id[None, :]).astype(F32)
        rows = jnp.dot(chosen, probes, precision=lax.Precision.HIGHEST)
        rows = rows.reshape(axial_count, ROWS_DEV, C * LANES)
        rows = jnp.sum(lax.all_to_all(rows, "axial", 0, 0), axis=0)
        return rows.reshape(ROWS_DEV, C, LANES).swapaxes(0, 1).reshape(C * ROWS_DEV, LANES)

    rows = lax.cond(
        crowded[0, 0] > 0, dense, lambda rows, *_: rows, rows, probes, cycle_id
    )
    rows = lax.all_gather(rows, "girth")
    table_high, table_low, phases = dft_tables()
    phase = lax.dynamic_index_in_dim(
        jnp.asarray(phases), lax.axis_index("girth"), 0, keepdims=False
    )
    (spectrum,) = call(
        dft_kernel,
        [(2, ROWS_DEV, C, LANES)],
        tile_flops,
        rows,
        phase,
        jnp.asarray(table_high),
        jnp.asarray(table_low),
    )
    return final.reshape(C, 16, 16, LANES), spectrum


def solution(mesh):
    return jax.shard_map(
        body,
        mesh=mesh,
        in_specs=(
            P(None, None, "axial", "girth"),
            P(None, None, "axial", "girth"),
            P(None, "axial", "girth"),
            P("axial"),
            P("axial"),
            P("axial"),
            P(None, None, "axial"),
            P("girth"),
            P(None, "girth"),
        ),
        out_specs=(P(None, None, "axial", "girth"), P(None, "axial", None, "girth")),
        check_vma=False,
    )
```
